32 devices in a mesh: seq: 8 (over z, y), grp: 4 (over x, core).
Axes of the slice: x: 2, y: 2, z: 4, core: 2. Of those that a mesh axis runs over, the one named last changes fastest.
Arguments:
- x_in: bfloat16 [1024, 8192], P('seq', 'grp'), may hold values from -6 to 6
- multiplier_channels: bfloat16 [1024, 8192], P('seq', 'grp'), may hold values from -6 to 6
- b_proj: bfloat16 [1024, 1024], P('seq', 'grp'), may hold values from -6 to 6
- c_proj: bfloat16 [1024, 1024], P('seq', 'grp'), may hold values from -0.5 to 0.5
- dt_raw: float32 [1024, 64], P('seq', 'grp'), as said below
- dt_bias: float32 [64], P('grp'), may hold values from -3.5 to -1.5
- a_log: float32 [64], P('grp'), as said below
- skip_d: float32 [64], P('grp'), may hold values from 0.2 to 1
- norm_gain: float32 [8192], P('grp'), may hold values from 0.5 to 1.5
- w_out: bfloat16 [8192, 8192], P('grp', 'seq'), may hold values from -0.03125 to 0.03125
Outputs:
- mixed: bfloat16 [1024, 8192], P('seq', 'grp')
The draws below stay inside these ranges and needn't reach their ends.
Inputs may be any that keep to these rules, and one draw needn't show every extreme that they name: `dt_raw`: step size offsets, with bursts at a few positions of the sequence shared by all heads. `a_log`: log decay rates per head, between log(0.1 / (0.08 * 1024)) and log(0.6).
All inputs are finite; a program needn't handle non-finite values.
Results may differ from the reference program's by a relative error of at most 0.0049.
Values may be sent and summed in bfloat16 or wider, within the bound.
No kernel may reach another device: no remote copies, remote signals or barrier semaphores. Data moves between devices by JAX's collectives and lax.ppermute only.
A program may use at most 128 MiB of HBM per device.

```python
import math
import jax
import jax.numpy as jnp
from jax import lax

D_MODEL = 8192
HEADS = 64
CHANNEL_WIDTH = 128
STATE = 128
HEAD_GROUPS = 8
TOK_DEV = 128
LENGTH_OF_TEXT = 1024


def draw_a_log(key, part):
    first, latter_portion, third = jax.random.split(jax.random.fold_in(key, 11), 3)
    share = 0.5
    slow = jax.random.uniform(first, (HEADS,), jnp.float32) < share
    slow_rate = jnp.exp(jax.random.uniform(latter_portion, (HEADS,), jnp.float32, math.log(0.1), math.log(1.0))) / (0.08 * LENGTH_OF_TEXT)
    fast_rate = jnp.exp(jax.random.uniform(third, (HEADS,), jnp.float32, math.log(0.06), math.log(0.6)))
    return jnp.log(jnp.where(slow, slow_rate, fast_rate)).astype(jnp.float32)


def draw_dt_raw(key, part):
    first, latter_portion, third = jax.random.split(jax.random.fold_in(key, 23), 3)
    shift_start_index = 0.5 * jax.random.normal(first, (LENGTH_OF_TEXT, HEADS), jnp.float32)
    block_count = LENGTH_OF_TEXT // TOK_DEV
    block_shift = jax.random.uniform(third, (block_count, HEADS), jnp.float32, -1.5, 1.5)
    block_shift = jnp.repeat(block_shift, TOK_DEV, axis=0)
    position_spans = jax.random.uniform(latter_portion, (LENGTH_OF_TEXT, 1), jnp.float32) < 6.0 / LENGTH_OF_TEXT
    base_values = shift_start_index + block_shift
    return jnp.where(position_spans, 3.0 + base_values, base_values).astype(jnp.float32)


def levels(rng, dims, pieces, low, largest):
    def one(position, shards_of):
        heights = jax.random.uniform(jax.random.fold_in(jax.random.fold_in(rng, 6), position), (shards_of,), jnp.float32, low / len(pieces), largest / len(pieces))
        return jnp.repeat(jnp.exp(heights), dims[position] // shards_of).reshape((-1,) + (1,) * (len(dims) - position - 1))

    loudness = one(*pieces[0])
    for cut in pieces[1:]:
        loudness = loudness * one(*cut)
    return loudness


def centred(key, dims, scale, bound, cuts=(), held_as=jnp.bfloat16):
    gain = levels(key, dims, cuts, -0.22, 0.18) if cuts else 1.0
    array = jax.random.normal(key, dims, jnp.float32) * scale * gain
    return jnp.minimum(jnp.maximum(array, -bound), bound).astype(held_as)


def setup_inputs(seed: int = 0) -> dict:
    arg_keys = jax.random.split(jax.random.key(seed), 11)
    return {
        "x_in": centred(arg_keys[0], (LENGTH_OF_TEXT, HEADS * CHANNEL_WIDTH), 1.0, 6.0, ((0, 8), (1, 4))),
        "multiplier_channels": centred(arg_keys[1], (LENGTH_OF_TEXT, HEADS * CHANNEL_WIDTH), 1.0, 6.0, ((0, 8), (1, 4))),
        "b_proj": centred(arg_keys[2], (LENGTH_OF_TEXT, HEAD_GROUPS * STATE), 1.0, 6.0, ((0, 8), (1, 4))),
        "c_proj": centred(arg_keys[3], (LENGTH_OF_TEXT, HEAD_GROUPS * STATE), STATE ** -0.5, 0.5, ((0, 8), (1, 4))),
        "dt_raw": draw_dt_raw(jax.random.fold_in(arg_keys[10], 71), 0),
        "dt_bias": jnp.clip(-3.5 + 2.0 * jax.random.uniform(arg_keys[5], (HEADS,), jnp.float32) ** levels(arg_keys[5], (HEADS,), ((0, 4),), -0.2, 0.2), -3.5, -1.5),
        "a_log": draw_a_log(jax.random.fold_in(arg_keys[10], 71), 0),
        "skip_d": jnp.clip(0.2 + 0.8 * jax.random.uniform(arg_keys[7], (HEADS,), jnp.float32) ** levels(arg_keys[7], (HEADS,), ((0, 4),), -0.2, 0.2), 0.2, 1.0),
        "norm_gain": jnp.clip(1.0 + 0.1 * jax.random.normal(arg_keys[8], (HEADS * CHANNEL_WIDTH,), jnp.float32), 0.5, 1.5),
        "w_out": centred(arg_keys[9], (HEADS * CHANNEL_WIDTH, D_MODEL), (4 * HEADS * CHANNEL_WIDTH) ** -0.5, 0.03125, ((0, 4), (1, 8))),
    }


HIGH = lax.Precision.HIGHEST

def ssd_blocks(xf, dt, la, bm, cm, init):
    length, heads, width = xf.shape
    groups = bm.shape[1]
    ratio = heads // groups
    block = math.gcd(length, 256)
    count = length // block

    def step(state, blk):
        xb, dtb, lab, bb, cb = blk
        cum = jnp.cumsum(lab, axis=0)
        attention_logits = jnp.einsum('tgn,sgn->gts', cb, bb, precision=HIGH)
        attention_logits = jnp.repeat(attention_logits, ratio, axis=0)
        diff = cum.T[:, :, None] - cum.T[:, None, :]
        rows = lax.broadcasted_iota(jnp.int32, (block, block), 0)
        cols = lax.broadcasted_iota(jnp.int32, (block, block), 1)
        mask = (rows >= cols)[None, :, :]
        decay = jnp.exp(jnp.where(mask, diff, -1e+30))
        mixing = decay * attention_logits * dtb.T[:, None, :]
        outs = jnp.einsum('hts,shp->thp', mixing, xb, precision=HIGH)
        cheads = jnp.repeat(cb, ratio, axis=1)
        incoming_channel_bundles = jnp.repeat(bb, ratio, axis=1)
        outs = outs + jnp.exp(cum)[:, :, None] * jnp.einsum('thn,hpn->thp', cheads, state, precision=HIGH)
        weights = jnp.exp(cum[-1][None, :] - cum) * dtb
        fresh = jnp.einsum('sh,shp,shn->hpn', weights, xb, incoming_channel_bundles, precision=HIGH)
        state = jnp.exp(cum[-1])[:, None, None] * state + fresh
        return (state, outs)
    blocks = (xf.reshape(count, block, heads, width), dt.reshape(count, block, heads), la.reshape(count, block, heads), bm.reshape(count, block, groups, -1), cm.reshape(count, block, groups, -1))
    final, outs = lax.scan(step, init, blocks)
    return (outs.reshape(length, heads, width), final, lax.optimization_barrier(jnp.sum(la, axis=0)))

def gated_norm_output(y, multiplier_channels, norm_gain, groups):
    length = y.shape[0]
    gated = y.reshape(length, -1) * jax.nn.silu(multiplier_channels.astype(jnp.float32))
    split = gated.reshape(length, groups, -1)
    split = split * lax.rsqrt(lax.optimization_barrier(jnp.mean(split * split, axis=-1, keepdims=True)) + 1e-05)
    return (split.reshape(length, -1) * norm_gain).astype(jnp.bfloat16)

def reference(x_in, multiplier_channels, b_proj, c_proj, dt_raw, dt_bias, a_log, skip_d, norm_gain, w_out):
    length = x_in.shape[0]
    xf = x_in.astype(jnp.float32).reshape(length, HEADS, CHANNEL_WIDTH)
    dt = jax.nn.softplus(dt_raw + dt_bias)
    la = -jnp.exp(a_log) * dt
    bm = b_proj.astype(jnp.float32).reshape(length, HEAD_GROUPS, STATE)
    cm = c_proj.astype(jnp.float32).reshape(length, HEAD_GROUPS, STATE)
    init = jnp.zeros((HEADS, CHANNEL_WIDTH, STATE), jnp.float32)
    y, final, total = ssd_blocks(xf, dt, la, bm, cm, init)
    y = y + skip_d[None, :, None] * xf
    normed = gated_norm_output(y, multiplier_channels, norm_gain, HEAD_GROUPS)
    return jnp.dot(normed, w_out, preferred_element_type=jnp.float32).astype(jnp.bfloat16)
```

```python
import math

import jax
import jax.numpy as jnp
from jax import lax
from jax.experimental import pallas as pl
from jax.experimental.pallas import tpu as pltpu
from jax.sharding import PartitionSpec as P

CHANNEL_WIDTH = 128
STATE = 128
EPS = 1e-05

HIGH = lax.Precision.HIGHEST
F32 = jnp.float32
BF16 = jnp.bfloat16
NT = (((1,), (1,)), ((), ()))
TN = (((0,), (0,)), ((), ()))
VMEM_LIMIT = 48 * 2**20


def params(grid_dims=0):
    return pltpu.CompilerParams(
        vmem_limit_bytes=VMEM_LIMIT,
        dimension_semantics=("arbitrary",) * grid_dims if grid_dims else None,
    )


def cost(flops, moved):
    return pl.CostEstimate(flops=int(flops), bytes_accessed=int(moved), transcendentals=0)


def iota(shape, axis):
    return lax.broadcasted_iota(jnp.int32, shape, axis)


def spread(values, width):
    heads = values.shape[1]
    return jnp.concatenate(
        [jnp.broadcast_to(values[:, h : h + 1], (values.shape[0], width)) for h in range(heads)], axis=1
    )


def split3(value):
    hi = value.astype(BF16)
    rest = value - hi.astype(F32)
    mid = rest.astype(BF16)
    return hi, mid, (rest - mid.astype(F32)).astype(BF16)


def pack_kernel(y_ref, x_ref, b_ref, c_ref, dt_ref, out_ref, *, heads):
    width, state = x_ref.shape[1], b_ref.shape[1]
    out_ref[:, :width] = x_ref[...]
    out_ref[:, width : width + state] = b_ref[...]
    out_ref[:, width + state : width + 2 * state] = c_ref[...]
    other = 1 - y_ref[0]
    rows, cols = iota((2 * heads, 128), 0), iota((2 * heads, 128), 1)
    total = jnp.zeros((x_ref.shape[0], 128), F32)
    for part, value in enumerate(split3(dt_ref[...])):
        place = (cols == rows - other * heads + part * heads) & (rows // heads == other)
        total = total + jnp.dot(value, place.astype(BF16), preferred_element_type=F32)
    out_ref[:, width + 2 * state :] = total.astype(BF16)


def pack(y, x, b, c, dt, heads):
    tokens, width, state = x.shape[0], heads * CHANNEL_WIDTH, STATE
    full = width + 2 * state + 128
    return pl.pallas_call(
        lambda *refs: pack_kernel(*refs, heads=heads),
        grid_spec=pltpu.PrefetchScalarGridSpec(
            num_scalar_prefetch=1,
            grid=(1,),
            in_specs=[
                pl.BlockSpec((tokens, width), lambda i, y: (0, 1 - y[0])),
                pl.BlockSpec((tokens, state), lambda i, y: (0, 1 - y[0])),
                pl.BlockSpec((tokens, state), lambda i, y: (0, 1 - y[0])),
                pl.BlockSpec(dt.shape, lambda i, y: (0, 0)),
            ],
            out_specs=pl.BlockSpec((tokens, full), lambda i, y: (0, 0)),
        ),
        out_shape=jax.ShapeDtypeStruct((tokens, full), BF16),
        compiler_params=params(1),
        cost_estimate=cost(1e6, 4 * tokens * full),
        name="pack",
    )(y, x, b, c, dt)


def local_state_kernel(
    y_ref, x_ref, b_ref, c_ref, dt_ref, pk_ref, bias_ref, alog_ref,
    xs_ref, bs_ref, cs_ref, scal_ref, send_ref, s_ref, *, heads,
):
    tokens, width = x_ref.shape
    state = b_ref.shape[1]
    y = y_ref[0]
    mine, theirs = pl.multiple_of(y * tokens, tokens), pl.multiple_of((1 - y) * tokens, tokens)
    xs_ref[pl.ds(mine, tokens), :] = x_ref[...]
    xs_ref[pl.ds(theirs, tokens), :] = pk_ref[:, :width]
    bs_ref[pl.ds(mine, tokens), :] = b_ref[...]
    bs_ref[pl.ds(theirs, tokens), :] = pk_ref[:, width : width + state]
    cs_ref[pl.ds(mine, tokens), :] = c_ref[...]
    cs_ref[pl.ds(theirs, tokens), :] = pk_ref[:, width + state : width + 2 * state]
    rows, cols = iota((2 * heads, heads), 0), iota((2 * heads, heads), 1)
    own = jnp.dot(dt_ref[...], (rows == cols + y * heads).astype(F32), precision=HIGH)
    rows, cols = iota((128, heads), 0), iota((128, heads), 1)
    take = ((rows % heads == cols) & (rows < 3 * heads)).astype(BF16)
    other = jnp.dot(pk_ref[:, width + 2 * state :], take, preferred_element_type=F32)
    raw = jnp.concatenate([jnp.where(y == 0, own, other), jnp.where(y == 0, other, own)], axis=0)
    raw = raw + bias_ref[...]
    dt = jnp.maximum(raw, 0.0) + jnp.log1p(jnp.exp(-jnp.abs(raw)))
    la = -jnp.exp(alog_ref[...]) * dt
    length = 2 * tokens
    lower = (iota((length, length), 0) >= iota((length, length), 1)).astype(F32)
    cum = jnp.dot(lower, la, precision=HIGH)
    last = cum[length - 1 : length, :]
    scal_ref[:, :heads] = cum
    scal_ref[:, heads : 2 * heads] = dt
    weights = jnp.exp(last - cum) * dt
    scaled = (xs_ref[...].astype(F32) * spread(weights, CHANNEL_WIDTH)).astype(BF16)
    s = lax.dot_general(bs_ref[...], scaled, TN, preferred_element_type=F32)
    s_ref[:state, :] = s
    send_ref[:state, :] = s.astype(BF16)
    decay = spread(jnp.exp(last), CHANNEL_WIDTH)
    s_ref[state:, :] = jnp.broadcast_to(decay, (8, width))
    hi, mid, lo = split3(decay)
    which = iota((16, width), 0)
    parts = jnp.where(which == 0, hi.astype(F32), jnp.where(which == 1, mid.astype(F32), lo.astype(F32)))
    send_ref[state:, :] = jnp.where(which < 3, parts, 0.0).astype(BF16)


def local_state(y, x, b, c, dt, pk, bias, alog, heads):
    tokens, width, state = x.shape[0], heads * CHANNEL_WIDTH, STATE
    whole = lambda a: pl.BlockSpec(a.shape, lambda i, y: (0,) * a.ndim)
    outs = [
        jax.ShapeDtypeStruct((2 * tokens, width), BF16),
        jax.ShapeDtypeStruct((2 * tokens, state), BF16),
        jax.ShapeDtypeStruct((2 * tokens, state), BF16),
        jax.ShapeDtypeStruct((2 * tokens, 2 * heads), F32),
        jax.ShapeDtypeStruct((state + 16, width), BF16),
        jax.ShapeDtypeStruct((state + 8, width), F32),
    ]
    return pl.pallas_call(
        lambda *refs: local_state_kernel(*refs, heads=heads),
        grid_spec=pltpu.PrefetchScalarGridSpec(
            num_scalar_prefetch=1,
            grid=(1,),
            in_specs=[
                pl.BlockSpec((tokens, width), lambda i, y: (0, y[0])),
                pl.BlockSpec((tokens, state), lambda i, y: (0, y[0])),
                pl.BlockSpec((tokens, state), lambda i, y: (0, y[0])),
                whole(dt),
                whole(pk),
                whole(bias),
                whole(alog),
            ],
            out_specs=[whole(o) for o in outs],
        ),
        out_shape=outs,
        compiler_params=params(1),
        cost_estimate=cost(2e8, 3e6),
        name="local_state",
    )(y, x, b, c, dt, pk, bias, alog)


def local_y_kernel(xs_ref, bs_ref, cs_ref, scal_ref, skip_ref, out_ref, *, heads, tokens):
    cum, dt = scal_ref[:, :heads], scal_ref[:, heads : 2 * heads]
    length = 2 * tokens
    eye = (iota((length, length), 0) == iota((length, length), 1)).astype(F32)
    flat = lax.dot_general(scal_ref[...], eye, TN, precision=HIGH)
    cum_row, dt_row = flat[:heads, :], flat[heads : 2 * heads, :]
    mask = iota((tokens, tokens), 0) >= iota((tokens, tokens), 1)
    logits = []
    for k in range(2):
        at = pl.ds(k * tokens, tokens)
        logits.append(lax.dot_general(cs_ref[at, :], bs_ref[at, :], NT, preferred_element_type=F32))
    middle = cum[tokens - 1 : tokens, :]
    weights = jnp.exp(middle - cum[:tokens, :]) * dt[:tokens, :]
    scaled = (xs_ref[:tokens, :].astype(F32) * spread(weights, CHANNEL_WIDTH)).astype(BF16)
    s = lax.dot_general(bs_ref[:tokens, :], scaled, TN, preferred_element_type=F32).astype(BF16)
    carried = jnp.dot(cs_ref[tokens:, :], s, preferred_element_type=F32)
    carried = carried * spread(jnp.exp(cum[tokens:, :] - middle), CHANNEL_WIDTH)
    for k in range(2):
        lo = k * tokens
        for h in range(heads):
            at = h * CHANNEL_WIDTH
            xh = xs_ref[lo : lo + tokens, at : at + CHANNEL_WIDTH]
            diff = cum[lo : lo + tokens, h : h + 1] - cum_row[h : h + 1, lo : lo + tokens]
            mix = jnp.exp(jnp.where(mask, diff, -1e30)) * logits[k] * dt_row[h : h + 1, lo : lo + tokens]
            yh = jnp.dot(mix.astype(BF16), xh, preferred_element_type=F32)
            yh = yh + skip_ref[:, at : at + CHANNEL_WIDTH] * xh.astype(F32)
            if k == 1:
                yh = yh + carried[:, at : at + CHANNEL_WIDTH]
            out_ref[lo : lo + tokens, at : at + CHANNEL_WIDTH] = yh


def local_y(xs, bs, cs, scal, skip, heads):
    length, width = xs.shape
    return pl.pallas_call(
        lambda *refs: local_y_kernel(*refs, heads=heads, tokens=length // 2),
        out_shape=jax.ShapeDtypeStruct((length, width), F32),
        compiler_params=params(),
        cost_estimate=cost(4e8, 4e6),
        name="local_y",
    )(xs, bs, cs, scal, skip)


def join_kernel(send_ref, s_ref, got_ref, out_ref):
    state = out_ref.shape[0]
    out_ref[...] = (s_ref[:state, :] + s_ref[state : state + 1, :] * got_ref[:state, :].astype(F32)).astype(BF16)


def join(send, s, got):
    return pl.pallas_call(
        join_kernel,
        out_shape=jax.ShapeDtypeStruct((STATE, s.shape[1]), BF16),
        compiler_params=params(),
        cost_estimate=cost(1e6, 1.5e6),
        name="join",
    )(send, s, got)


def finish_kernel(y_ref, local_ref, cs_ref, scal_ref, one_ref, two_ref, gate_ref, got_ref, gain_ref, out_ref, *, heads):
    length, width = local_ref.shape
    state, tokens = two_ref.shape[0], length // 2
    y = y_ref[0]
    decay = jnp.sum(one_ref[state:, :].astype(F32), axis=0, keepdims=True)
    start = one_ref[:state, :].astype(F32) + decay * two_ref[...].astype(F32)
    hi = start.astype(BF16)
    grow = jnp.exp(scal_ref[:, :heads])
    for k in range(2):
        at = pl.ds(k * tokens, tokens)
        carried = jnp.dot(cs_ref[at, :], hi, preferred_element_type=F32)
        value = local_ref[at, :] + carried * spread(grow[k * tokens : (k + 1) * tokens, :], CHANNEL_WIDTH)
        gate = jnp.where(y == k, gate_ref[...], got_ref[...]).astype(F32)
        value = value * (gate / (1.0 + jnp.exp(-gate)))
        mean = jnp.sum(value * value, axis=1, keepdims=True) / width
        out_ref[at, :] = (value * lax.rsqrt(mean + EPS) * gain_ref[...]).astype(BF16)


def finish(y, local, cs, scal, one, two, gate, got, gain, heads):
    length, width = local.shape
    whole = lambda a: pl.BlockSpec(a.shape, lambda i, y: (0,) * a.ndim)
    return pl.pallas_call(
        lambda *refs: finish_kernel(*refs, heads=heads),
        grid_spec=pltpu.PrefetchScalarGridSpec(
            num_scalar_prefetch=1,
            grid=(1,),
            in_specs=[
                whole(local),
                whole(cs),
                whole(scal),
                whole(one),
                whole(two),
                pl.BlockSpec((length // 2, width), lambda i, y: (0, y[0])),
                whole(got),
                whole(gain),
            ],
            out_specs=pl.BlockSpec((length, width), lambda i, y: (0, 0)),
        ),
        out_shape=jax.ShapeDtypeStruct((length, width), BF16),
        compiler_params=params(1),
        cost_estimate=cost(1e8, 4e6),
        name="finish",
    )(y, local, cs, scal, one, two, gate, got, gain)


def project_kernel(y_ref, a_ref, own_ref, got_ref, out_ref, half_ref):
    block = a_ref[...]
    for k, ref in enumerate((own_ref, got_ref)):
        part = jnp.dot(block, ref[...], preferred_element_type=F32)
        out_ref[0, k] = part
        half_ref[0, k] = part.astype(BF16)


def project(y, block, weights, got):
    tokens, depth = block.shape[0] // 2, block.shape[1]
    cols = weights.shape[1]
    shape = (2, 2, tokens, cols)
    return pl.pallas_call(
        project_kernel,
        grid_spec=pltpu.PrefetchScalarGridSpec(
            num_scalar_prefetch=1,
            grid=(2,),
            in_specs=[
                pl.BlockSpec((tokens, depth), lambda i, y: (i + y[0] - 2 * i * y[0], 0)),
                pl.BlockSpec((depth, cols), lambda i, y: (y[0], 0)),
                pl.BlockSpec((depth, cols), lambda i, y: (0, 0)),
            ],
            out_specs=[
                pl.BlockSpec((1,) + shape[1:], lambda i, y: (i, 0, 0, 0)),
                pl.BlockSpec((1,) + shape[1:], lambda i, y: (i, 0, 0, 0)),
            ],
        ),
        out_shape=[jax.ShapeDtypeStruct(shape, F32), jax.ShapeDtypeStruct(shape, BF16)],
        compiler_params=params(1),
        cost_estimate=cost(8.0 * tokens * depth * cols, 9e6),
        name="project",
    )(y, block, weights, got)


def pair_shards(nz, x_in, gate, b_proj, c_proj, dt_raw, dt_bias, a_log, skip_d, norm_gain, w_out):
    tokens = x_in.shape[0]
    heads = dt_raw.shape[1] // 2
    width = heads * CHANNEL_WIDTH
    seq, grp = lax.axis_index("seq"), lax.axis_index("grp")
    z, y = seq // 2, seq % 2
    yv = y.astype(jnp.int32).reshape(1)
    both = ("seq", "grp")
    spots = [(a, b, g) for a in range(nz) for b in range(2) for g in range(nz)]
    flat = lambda a, b, g: (a * 2 + b) * nz + g

    def half(v, axis, which):
        n = v.shape[axis] // 2
        return lax.dynamic_slice_in_dim(v, which * n, n, axis)

    flip = [(s, s ^ 1) for s in range(2 * nz)]
    got = lax.ppermute(pack(yv, x_in, b_proj, c_proj, dt_raw, heads), "seq", flip)
    got_gate = lax.ppermute(half(gate, 1, 1 - y), "seq", flip)
    got_w = lax.ppermute(half(w_out, 0, 1 - y), "seq", flip)
    bias, alog = half(dt_bias, 0, y)[None, :], half(a_log, 0, y)[None, :]
    skip = jnp.repeat(half(skip_d, 0, y), CHANNEL_WIDTH)[None, :]
    gain = half(norm_gain, 0, y)[None, :]

    def along(v, step, senders):
        pairs = [(a * 2 + b, (a + step) * 2 + b) for a in senders for b in range(2)]
        return lax.ppermute(v, "seq", pairs)

    xs, bs, cs, scal, send, s = local_state(yv, x_in, b_proj, c_proj, dt_raw, got, bias, alog, heads)
    one = along(send, 1, range(nz - 1))
    base = local_y(xs, bs, cs, scal, skip, heads)
    two = along(join(send, s, one), 2, range(nz - 2))
    block = finish(yv, base, cs, scal, one, two, gate, got_gate, gain, heads)

    up1, down1 = along(block, 1, range(nz - 1)), along(block, -1, range(1, nz))
    up2, down2 = along(up1, 1, range(1, nz - 1)), along(down1, -1, range(1, nz - 1))
    far = jnp.where(z == 1, down2, up2)
    far = lax.ppermute(far, "seq", [(2 + b, b) for b in range(2)] + [(4 + b, 6 + b) for b in range(2)])
    table = [(0, 1, 2, 3), (1, 2, 0, 3), (2, 1, 3, 0), (3, 2, 1, 0)]
    slots = [
        block,
        jnp.where(z < 2, down1, up1),
        jnp.where(z == 0, down2, jnp.where(z == 1, up1, jnp.where(z == 2, down1, up2))),
        jnp.where(z == 1, down2, jnp.where(z == 2, up2, far)),
    ]
    total = None
    for slot, value in enumerate(slots):
        full, rounded = project(yv, value, w_out, got_w)
        owner = lambda a: table[a][slot]
        pairs = [(flat(a, b, g ^ 1), flat(a, b, g)) for a, b, g in spots if g % 2 == owner(a) % 2]
        summed = full + lax.ppermute(rounded, both, pairs).astype(F32)
        pairs = [(flat(a, 1 - b, g), flat(a, b, g)) for a, b, g in spots if g % 2 == owner(a) % 2]
        r = lax.ppermute(summed[1].astype(BF16), both, pairs).astype(F32)
        summed = summed[0] + r[::-1]
        pairs = [(flat(a, b, g ^ 2), flat(a, b, g)) for a, b, g in spots if g == owner(a)]
        summed = summed + lax.ppermute(summed.astype(BF16), both, pairs).astype(F32)
        result = summed.astype(BF16)
        if slot:
            pairs = [(flat(a, b, g), flat(g, b, a)) for a, b, g in spots if g == owner(a)]
            result = lax.ppermute(result, both, pairs)
            total = total + result
        else:
            total = jnp.where(z == grp, result, jnp.zeros_like(result))
    left = jnp.where(y == 0, total[0], total[1])
    right = jnp.where(y == 0, total[1], total[0])
    return jnp.concatenate([left, right], axis=1)


def prefix(array, axis, combine, identity):
    length, mine = (lax.axis_size(axis), lax.axis_index(axis))
    everything = jax.tree.map(lambda part: lax.all_gather(part, axis), array)
    start = jax.tree.map(
        lambda part, zero: jnp.broadcast_to(jnp.asarray(zero, part.dtype), part.shape),
        array,
        identity,
    )

    def turn(k, before):
        reached = k < mine
        new = combine(before, jax.tree.map(lambda part: part[k], everything))
        return jax.tree.map(lambda a, b: jnp.where(reached, a, b), new, before)

    return lax.fori_loop(0, length, turn, start)


def ssd_blocks(xf, dt, la, bm, cm, braw, craw, init):
    length, heads, width = xf.shape
    groups = bm.shape[1]
    ratio = heads // groups
    block = math.gcd(length, 256)
    count = length // block

    def step(state, blk):
        xb, dtb, lab, bb, cb, bnar, cnar = blk
        cum = jnp.cumsum(lab, axis=0)
        attention_logits = jnp.einsum("tgn,sgn->gts", cnar, bnar, preferred_element_type=F32)
        attention_logits = jnp.repeat(attention_logits, ratio, axis=0)
        diff = cum.T[:, :, None] - cum.T[:, None, :]
        rows = lax.broadcasted_iota(jnp.int32, (block, block), 0)
        cols = lax.broadcasted_iota(jnp.int32, (block, block), 1)
        mask = (rows >= cols)[None, :, :]
        decay = jnp.exp(jnp.where(mask, diff, -1e30))
        mixing = decay * attention_logits * dtb.T[:, None, :]
        outs = jnp.einsum("hts,shp->thp", mixing, xb, precision=HIGH)
        cheads = jnp.repeat(cb, ratio, axis=1)
        bheads = jnp.repeat(bb, ratio, axis=1)
        outs = outs + jnp.exp(cum)[:, :, None] * jnp.einsum("thn,hpn->thp", cheads, state, precision=HIGH)
        weights = jnp.exp(cum[-1][None, :] - cum) * dtb
        fresh = jnp.einsum("sh,shp,shn->hpn", weights, xb, bheads, precision=HIGH)
        state = jnp.exp(cum[-1])[:, None, None] * state + fresh
        return (state, outs)

    cut = lambda v: v.reshape((count, block) + v.shape[1:])
    final, outs = lax.scan(step, init, jax.tree.map(cut, (xf, dt, la, bm, cm, braw, craw)))
    return (outs.reshape(length, heads, width), final, jnp.sum(la, axis=0))


def gated_norm_output(y, multiplier_channels, norm_gain, groups):
    length = y.shape[0]
    gated = y.reshape(length, -1) * jax.nn.silu(multiplier_channels.astype(F32))
    split = gated.reshape(length, groups, -1)
    split = split * lax.rsqrt(jnp.mean(split * split, axis=-1, keepdims=True) + EPS)
    return (split.reshape(length, -1) * norm_gain).astype(BF16)


def combine_states(earlier_state, later):
    return (earlier_state[0] * later[0], later[0][:, None, None] * earlier_state[1] + later[1])


def general_shards(x_in, gate, b_proj, c_proj, dt_raw, dt_bias, a_log, skip_d, norm_gain, w_out):
    length = x_in.shape[0]
    heads = dt_raw.shape[1]
    groups = b_proj.shape[1] // STATE
    xf = x_in.astype(F32).reshape(length, heads, CHANNEL_WIDTH)
    dt = jax.nn.softplus(dt_raw + dt_bias)
    la = -jnp.exp(a_log) * dt
    braw = b_proj.reshape(length, groups, STATE)
    craw = c_proj.reshape(length, groups, STATE)
    bm = braw.astype(F32)
    cm = craw.astype(F32)
    empty = jnp.zeros((heads, CHANNEL_WIDTH, STATE), F32)
    y, local_end, total = ssd_blocks(xf, dt, la, bm, cm, braw, craw, empty)
    identity = (jnp.ones((heads,), F32), empty)
    carried = prefix((jnp.exp(total), local_end), "seq", combine_states, identity)
    cum = jnp.cumsum(la, axis=0)
    cheads = jnp.repeat(cm, heads // groups, axis=1)
    y = y + jnp.exp(cum)[:, :, None] * jnp.einsum("thn,hpn->thp", cheads, carried[1], precision=HIGH)
    y = y + skip_d[None, :, None] * xf
    normed = gated_norm_output(y, gate, norm_gain, groups)
    partial_out = jnp.dot(
        normed, lax.all_gather(w_out, "seq", axis=1, tiled=True), preferred_element_type=F32
    )
    return lax.psum_scatter(partial_out, "grp", scatter_dimension=1, tiled=True).astype(BF16)


def solution(mesh):
    seq, grp = mesh.shape["seq"], mesh.shape["grp"]

    def shards(*args):
        groups = args[2].shape[1] // STATE
        if grp == 4 and seq == 2 * grp and groups == 2:
            return pair_shards(grp, *args)
        return general_shards(*args)

    return jax.shard_map(
        shards,
        mesh=mesh,
        in_specs=(
            P("seq", "grp"),
            P("seq", "grp"),
            P("seq", "grp"),
            P("seq", "grp"),
            P("seq", "grp"),
            P("grp"),
            P("grp"),
            P("grp"),
            P("grp"),
            P("grp", "seq"),
        ),
        out_specs=P("seq", "grp"),
        check_vma=False,
    )
```

```python
import math

import jax
import jax.numpy as jnp
from jax import lax
from jax.experimental import pallas as pl
from jax.experimental.pallas import tpu as pltpu
from jax.sharding import PartitionSpec as P

CHANNEL_WIDTH = 128
STATE = 128
EPS = 1e-05

HIGH = lax.Precision.HIGHEST
F32 = jnp.float32
BF16 = jnp.bfloat16
NT = (((1,), (1,)), ((), ()))
TN = (((0,), (0,)), ((), ()))
VMEM_LIMIT = 24 * 2**20


def params(grid_dims=0):
    return pltpu.CompilerParams(
        vmem_limit_bytes=VMEM_LIMIT,
        dimension_semantics=("arbitrary",) * grid_dims if grid_dims else None,
    )


def cost(flops, moved):
    return pl.CostEstimate(flops=1, bytes_accessed=1, transcendentals=0)


def iota(shape, axis):
    return lax.broadcasted_iota(jnp.int32, shape, axis)


def spread(values, width):
    heads = values.shape[1]
    return jnp.concatenate(
        [jnp.broadcast_to(values[:, h : h + 1], (values.shape[0], width)) for h in range(heads)], axis=1
    )


def split3(value):
    hi = value.astype(BF16)
    rest = value - hi.astype(F32)
    mid = rest.astype(BF16)
    return hi, mid, (rest - mid.astype(F32)).astype(BF16)


def pack_kernel(y_ref, x_ref, b_ref, c_ref, dt_ref, out_ref, *, heads):
    width, state = x_ref.shape[1], b_ref.shape[1]
    out_ref[:, :width] = x_ref[...]
    out_ref[:, width : width + state] = b_ref[...]
    out_ref[:, width + state : width + 2 * state] = c_ref[...]
    other = 1 - y_ref[0]
    rows, cols = iota((2 * heads, 128), 0), iota((2 * heads, 128), 1)
    total = jnp.zeros((x_ref.shape[0], 128), F32)
    for part, value in enumerate(split3(dt_ref[...])):
        place = (cols == rows - other * heads + part * heads) & (rows // heads == other)
        total = total + lax.dot_general(value, place.astype(BF16), TN, preferred_element_type=F32)
    out_ref[:, width + 2 * state :] = total.astype(BF16)


def pack(y, x, b, c, dt, heads):
    tokens, width, state = x.shape[0], heads * CHANNEL_WIDTH, STATE
    full = width + 2 * state + 128
    return pl.pallas_call(
        lambda *refs: pack_kernel(*refs, heads=heads),
        grid_spec=pltpu.PrefetchScalarGridSpec(
            num_scalar_prefetch=1,
            grid=(1,),
            in_specs=[
                pl.BlockSpec((tokens, width), lambda i, y: (0, 1 - y[0])),
                pl.BlockSpec((tokens, state), lambda i, y: (0, 1 - y[0])),
                pl.BlockSpec((tokens, state), lambda i, y: (0, 1 - y[0])),
                pl.BlockSpec(dt.shape, lambda i, y: (0, 0)),
            ],
            out_specs=pl.BlockSpec((tokens, full), lambda i, y: (0, 0)),
        ),
        out_shape=jax.ShapeDtypeStruct((tokens, full), BF16),
        compiler_params=params(1),
        cost_estimate=cost(1e6, 4 * tokens * full),
        name="pack",
    )(y, x, b, c, dt)


def local_state_kernel(
    y_ref, x_ref, b_ref, c_ref, dt_ref, pk_ref, bias_ref, alog_ref,
    xs_ref, bs_ref, cs_ref, scal_ref, send_ref, s_ref, *, heads,
):
    tokens, width = x_ref.shape
    state = b_ref.shape[1]
    y = y_ref[0]
    mine, theirs = pl.multiple_of(y * tokens, tokens), pl.multiple_of((1 - y) * tokens, tokens)
    xs_ref[pl.ds(mine, tokens), :] = x_ref[...]
    xs_ref[pl.ds(theirs, tokens), :] = pk_ref[:, :width]
    bs_ref[pl.ds(mine, tokens), :] = b_ref[...]
    bs_ref[pl.ds(theirs, tokens), :] = pk_ref[:, width : width + state]
    cs_ref[pl.ds(mine, tokens), :] = c_ref[...]
    cs_ref[pl.ds(theirs, tokens), :] = pk_ref[:, width + state : width + 2 * state]
    rows, cols = iota((2 * heads, heads), 0), iota((2 * heads, heads), 1)
    own = lax.dot_general(dt_ref[...], (rows == cols + y * heads).astype(F32), TN, precision=HIGH)
    rows, cols = iota((128, heads), 0), iota((128, heads), 1)
    take = ((rows % heads == cols) & (rows < 3 * heads)).astype(BF16)
    other = jnp.dot(pk_ref[:, width + 2 * state :], take, preferred_element_type=F32)
    raw = jnp.concatenate([jnp.where(y == 0, own, other), jnp.where(y == 0, other, own)], axis=0)
    raw = raw + bias_ref[...]
    dt = jnp.maximum(raw, 0.0) + jnp.log1p(jnp.exp(-jnp.abs(raw)))
    la = -jnp.exp(alog_ref[...]) * dt
    length = 2 * tokens
    lower = (iota((length, length), 0) >= iota((length, length), 1)).astype(F32)
    cum = jnp.dot(lower, la, precision=HIGH)
    last = cum[length - 1 : length, :]
    scal_ref[:, :heads] = cum
    scal_ref[:, heads : 2 * heads] = dt
    weights = jnp.exp(last - cum) * dt
    scaled = (xs_ref[...].astype(F32) * spread(weights, CHANNEL_WIDTH)).astype(BF16)
    s = lax.dot_general(bs_ref[...], scaled, TN, preferred_element_type=F32)
    s_ref[:state, :] = s
    send_ref[:state, :] = s.astype(BF16)
    decay = spread(jnp.exp(last), CHANNEL_WIDTH)
    s_ref[state:, :] = jnp.broadcast_to(decay, (8, width))
    hi, mid, lo = split3(decay)
    which = iota((16, width), 0)
    parts = jnp.where(which == 0, hi.astype(F32), jnp.where(which == 1, mid.astype(F32), lo.astype(F32)))
    send_ref[state:, :] = jnp.where(which < 3, parts, 0.0).astype(BF16)


def local_state(y, x, b, c, dt, pk, bias, alog, heads):
    tokens, width, state = x.shape[0], heads * CHANNEL_WIDTH, STATE
    whole = lambda a: pl.BlockSpec(a.shape, lambda i, y: (0,) * a.ndim)
    outs = [
        jax.ShapeDtypeStruct((2 * tokens, width), BF16),
        jax.ShapeDtypeStruct((2 * tokens, state), BF16),
        jax.ShapeDtypeStruct((2 * tokens, state), BF16),
        jax.ShapeDtypeStruct((2 * tokens, 2 * heads), F32),
        jax.ShapeDtypeStruct((state + 16, width), BF16),
        jax.ShapeDtypeStruct((state + 8, width), F32),
    ]
    return pl.pallas_call(
        lambda *refs: local_state_kernel(*refs, heads=heads),
        grid_spec=pltpu.PrefetchScalarGridSpec(
            num_scalar_prefetch=1,
            grid=(1,),
            in_specs=[
                pl.BlockSpec((tokens, width), lambda i, y: (0, y[0])),
                pl.BlockSpec((tokens, state), lambda i, y: (0, y[0])),
                pl.BlockSpec((tokens, state), lambda i, y: (0, y[0])),
                whole(dt),
                whole(pk),
                whole(bias),
                whole(alog),
            ],
            out_specs=[whole(o) for o in outs],
        ),
        out_shape=outs,
        compiler_params=params(1),
        cost_estimate=cost(2e8, 3e6),
        name="local_state",
    )(y, x, b, c, dt, pk, bias, alog)


def local_y_kernel(xs_ref, bs_ref, cs_ref, scal_ref, skip_ref, out_ref, *, heads, tokens):
    cum, dt = scal_ref[:, :heads], scal_ref[:, heads : 2 * heads]
    length = 2 * tokens
    eye = (iota((length, length), 0) == iota((length, length), 1)).astype(F32)
    flat = lax.dot_general(scal_ref[...], eye, TN, precision=HIGH)
    cum_row, dt_row = flat[:heads, :], flat[heads : 2 * heads, :]
    mask = iota((tokens, tokens), 0) >= iota((tokens, tokens), 1)
    logits = []
    for k in range(2):
        at = pl.ds(k * tokens, tokens)
        logits.append(lax.dot_general(cs_ref[at, :], bs_ref[at, :], NT, preferred_element_type=F32))
    middle = cum[tokens - 1 : tokens, :]
    weights = jnp.exp(middle - cum[:tokens, :]) * dt[:tokens, :]
    scaled = (xs_ref[:tokens, :].astype(F32) * spread(weights, CHANNEL_WIDTH)).astype(BF16)
    s = lax.dot_general(bs_ref[:tokens, :], scaled, TN, preferred_element_type=F32).astype(BF16)
    carried = jnp.dot(cs_ref[tokens:, :], s, preferred_element_type=F32)
    carried = carried * spread(jnp.exp(cum[tokens:, :] - middle), CHANNEL_WIDTH)
    for k in range(2):
        lo = k * tokens
        for h in range(heads):
            at = h * CHANNEL_WIDTH
            xh = xs_ref[lo : lo + tokens, at : at + CHANNEL_WIDTH]
            diff = cum[lo : lo + tokens, h : h + 1] - cum_row[h : h + 1, lo : lo + tokens]
            mix = jnp.exp(jnp.where(mask, diff, -1e30)) * logits[k] * dt_row[h : h + 1, lo : lo + tokens]
            top = mix.astype(BF16)
            yh = jnp.dot(top, xh, preferred_element_type=F32)
            yh = yh + jnp.dot((mix - top.astype(F32)).astype(BF16), xh, preferred_element_type=F32)
            yh = yh + skip_ref[:, at : at + CHANNEL_WIDTH] * xh.astype(F32)
            if k == 1:
                yh = yh + carried[:, at : at + CHANNEL_WIDTH]
            out_ref[lo : lo + tokens, at : at + CHANNEL_WIDTH] = yh


def local_y(xs, bs, cs, scal, skip, heads):
    length, width = xs.shape
    return pl.pallas_call(
        lambda *refs: local_y_kernel(*refs, heads=heads, tokens=length // 2),
        out_shape=jax.ShapeDtypeStruct((length, width), F32),
        compiler_params=params(),
        cost_estimate=cost(4e8, 4e6),
        name="local_y",
    )(xs, bs, cs, scal, skip)


def join_kernel(send_ref, s_ref, got_ref, out_ref):
    state = out_ref.shape[0]
    out_ref[...] = (s_ref[:state, :] + s_ref[state : state + 1, :] * got_ref[:state, :].astype(F32)).astype(BF16)


def join(send, s, got):
    return pl.pallas_call(
        join_kernel,
        out_shape=jax.ShapeDtypeStruct((STATE, s.shape[1]), BF16),
        compiler_params=params(),
        cost_estimate=cost(1e6, 1.5e6),
        name="join",
    )(send, s, got)


def finish_kernel(y_ref, local_ref, cs_ref, scal_ref, one_ref, two_ref, gate_ref, got_ref, gain_ref, out_ref, *, heads):
    length, width = local_ref.shape
    state, tokens = two_ref.shape[0], length // 2
    y = y_ref[0]
    decay = jnp.sum(one_ref[state:, :].astype(F32), axis=0, keepdims=True)
    start = one_ref[:state, :].astype(F32) + decay * two_ref[...].astype(F32)
    hi = start.astype(BF16)
    grow = jnp.exp(scal_ref[:, :heads])
    for k in range(2):
        at = pl.ds(k * tokens, tokens)
        carried = jnp.dot(cs_ref[at, :], hi, preferred_element_type=F32)
        value = local_ref[at, :] + carried * spread(grow[k * tokens : (k + 1) * tokens, :], CHANNEL_WIDTH)
        gate = jnp.where(y == k, gate_ref[...], got_ref[...]).astype(F32)
        value = value * (gate / (1.0 + jnp.exp(-gate)))
        mean = jnp.sum(value * value, axis=1, keepdims=True) / width
        out_ref[at, :] = (value * lax.rsqrt(mean + EPS) * gain_ref[...]).astype(BF16)


def finish(y, local, cs, scal, one, two, gate, got, gain, heads):
    length, width = local.shape
    whole = lambda a: pl.BlockSpec(a.shape, lambda i, y: (0,) * a.ndim)
    return pl.pallas_call(
        lambda *refs: finish_kernel(*refs, heads=heads),
        grid_spec=pltpu.PrefetchScalarGridSpec(
            num_scalar_prefetch=1,
            grid=(1,),
            in_specs=[
                whole(local),
                whole(cs),
                whole(scal),
                whole(one),
                whole(two),
                pl.BlockSpec((length // 2, width), lambda i, y: (0, y[0])),
                whole(got),
                whole(gain),
            ],
            out_specs=pl.BlockSpec((length, width), lambda i, y: (0, 0)),
        ),
        out_shape=jax.ShapeDtypeStruct((length, width), BF16),
        compiler_params=params(1),
        cost_estimate=cost(1e8, 4e6),
        name="finish",
    )(y, local, cs, scal, one, two, gate, got, gain)


def project_kernel(yc_ref, own_ref, got_ref, w_ref, w0_ref, w1_ref, keep_ref, send_ref, both_ref):
    tokens, depth = keep_ref.shape[0], own_ref.shape[1]
    y, core = yc_ref[0], yc_ref[1]

    @pl.when(pl.program_id(0) == 0)
    def _():
        for k in range(2):
            at = pl.multiple_of(jnp.where(y == 0, k, 1 - k) * tokens, tokens)
            rows = pl.ds(k * tokens, tokens)
            own, got = own_ref[pl.ds(at, tokens), :], got_ref[pl.ds(at, tokens), :]
            both_ref[rows, :depth] = jnp.where(core == 0, own, got)
            both_ref[rows, depth:] = jnp.where(core == 0, got, own)

    def multiply(first, second):
        part = jnp.dot(both_ref[:, :depth], first[...], preferred_element_type=F32)
        part = part + jnp.dot(both_ref[:, depth:], second[...], preferred_element_type=F32)
        keep_ref[...] = part[:tokens, :]
        send_ref[...] = part[tokens:, :].astype(BF16)

    @pl.when(core == 0)
    def _():
        multiply(w_ref, w0_ref)

    @pl.when(core == 1)
    def _():
        multiply(w0_ref, w1_ref)


def project(yc, own, got, w, w0, w1):
    tokens, depth = own.shape[0] // 2, own.shape[1]
    cols = w.shape[1]
    tile = min(cols, 256)
    return pl.pallas_call(
        project_kernel,
        grid_spec=pltpu.PrefetchScalarGridSpec(
            num_scalar_prefetch=1,
            grid=(cols // tile,),
            in_specs=[
                pl.BlockSpec(own.shape, lambda i, yc: (0, 0)),
                pl.BlockSpec(own.shape, lambda i, yc: (0, 0)),
                pl.BlockSpec((depth, tile), lambda i, yc: (yc[0], jnp.where(yc[1] == 0, i, 0))),
                pl.BlockSpec((depth, tile), lambda i, yc: (0, i)),
                pl.BlockSpec((depth, tile), lambda i, yc: (0, jnp.where(yc[1] == 1, i, 0))),
            ],
            out_specs=[
                pl.BlockSpec((tokens, tile), lambda i, yc: (0, i)),
                pl.BlockSpec((tokens, tile), lambda i, yc: (0, i)),
            ],
            scratch_shapes=[pltpu.VMEM((2 * tokens, 2 * depth), BF16)],
        ),
        out_shape=[jax.ShapeDtypeStruct((tokens, cols), F32), jax.ShapeDtypeStruct((tokens, cols), BF16)],
        compiler_params=params(1),
        cost_estimate=cost(8.0 * tokens * depth * cols, 6e6),
        name="project",
    )(yc, own, got, w, w0, w1)


def place_kernel(at_ref, mine_ref, got_ref, out_ref):
    cols = got_ref.shape[1]
    part = at_ref[0]
    out_ref[:, pl.ds(pl.multiple_of(part * cols, cols), cols)] = mine_ref[...]
    out_ref[:, pl.ds(pl.multiple_of((1 - part) * cols, cols), cols)] = got_ref[...]


def place(at, mine, got):
    tokens, cols = got.shape
    whole = pl.BlockSpec((tokens, cols), lambda i, at: (0, 0))
    return pl.pallas_call(
        place_kernel,
        grid_spec=pltpu.PrefetchScalarGridSpec(
            num_scalar_prefetch=1,
            grid=(1,),
            in_specs=[whole, whole],
            out_specs=pl.BlockSpec((tokens, 2 * cols), lambda i, at: (0, 0)),
        ),
        out_shape=jax.ShapeDtypeStruct((tokens, 2 * cols), BF16),
        compiler_params=params(1),
        cost_estimate=cost(1e6, 2e6),
        name="place",
    )(at, mine, got)


def pair_shards(nz, x_in, gate, b_proj, c_proj, dt_raw, dt_bias, a_log, skip_d, norm_gain, w_out):
    tokens = x_in.shape[0]
    heads = dt_raw.shape[1] // 2
    width = heads * CHANNEL_WIDTH
    seq, grp = lax.axis_index("seq"), lax.axis_index("grp")
    z, y = seq // 2, seq % 2
    yv = y.astype(jnp.int32).reshape(1)
    yc = jnp.stack([y, grp % 2]).astype(jnp.int32)
    dt_raw = dt_raw.T
    both = ("seq", "grp")
    core = grp % 2
    spots = [(a, b, c, d) for a in range(nz) for b in range(2) for c in range(nz // 2) for d in range(2)]
    flat = lambda a, b, c, d: ((a * 2 + b) * (nz // 2) + c) * 2 + d
    tie = lax.optimization_barrier

    def half(v, axis, which):
        n = v.shape[axis] // 2
        return lax.dynamic_slice_in_dim(v, which * n, n, axis)

    flip = [(s, s ^ 1) for s in range(2 * nz)]
    sibling = [(g, g ^ 1) for g in range(nz)]
    across = [(flat(a, b, c, d), flat(a, 1 - b, c, 1 - d)) for a, b, c, d in spots]

    def along(v, step, senders):
        pairs = [(a * 2 + b, (a + step) * 2 + b) for a in senders for b in range(2)]
        return lax.ppermute(v, "seq", pairs)

    got = lax.ppermute(pack(yv, x_in, b_proj, c_proj, dt_raw, heads), "seq", flip)
    swap, go = half(w_out, 0, y ^ 1 ^ core), half(w_out, 0, 1 - y)
    gate_half = half(gate, 1, 1 - y)
    bias, alog = half(dt_bias, 0, y)[None, :], half(a_log, 0, y)[None, :]
    skip = jnp.repeat(half(skip_d, 0, y), CHANNEL_WIDTH)[None, :]
    gain = half(norm_gain, 0, y)[None, :]
    got, swap, go, gate_half, bias, alog, skip, gain = tie((got, swap, go, gate_half, bias, alog, skip, gain))

    xs, bs, cs, scal, send, s = local_state(yv, x_in, b_proj, c_proj, dt_raw, got, bias, alog, heads)
    one = along(send, 1, range(nz - 1))
    gate_half, _ = tie((gate_half, send))
    got_gate = lax.ppermute(gate_half, "seq", flip)
    base = local_y(xs, bs, cs, scal, skip, heads)
    one, got_gate, base, swap, go = tie((one, got_gate, base, swap, go))

    joined = join(send, s, one)
    two = along(joined, 2, range(nz - 2))
    swap, go, _ = tie((swap, go, joined))
    pairs = [(flat(a, b, c, 0), flat(a, 1 - b, c, 1)) for a, b, c, d in spots if d == 0]
    pairs += [(flat(a, b, c, 1), flat(a, b, c, 0)) for a, b, c, d in spots if d == 0]
    w0 = lax.ppermute(swap, both, pairs)
    w1 = lax.ppermute(go, both, [(flat(a, b, c, 1), flat(a, 1 - b, c, 1)) for a, b, c, d in spots if d == 0])
    block = finish(yv, base, cs, scal, one, two, gate, got_gate, gain, heads)

    table = [(0, 1, 2, 3), (1, 2, 3, 0), (2, 1, 0, 3), (3, 2, 1, 0)]
    cross = lambda value: lax.ppermute(value, "grp", sibling)

    def reduce_y(full, rounded):
        return (full + lax.ppermute(rounded, both, across).astype(F32)).astype(BF16)

    def deliver(slot, value):
        parts = []
        for turn in range(2):
            pairs = [
                (flat(a, b, c, d), flat(table[a][slot], b, a // 2, d)) for a, b, c, d in spots if c ^ turn == a // 2
            ]
            parts.append(lax.ppermute(value, both, pairs) if slot or turn else value)
        return parts

    up1, down1 = along(block, 1, range(nz - 1)), along(block, -1, range(1, nz))
    flip0 = cross(block)
    up1, down1, flip0, block = tie((up1, down1, flip0, block))
    up2, down2 = along(up1, 1, range(1, nz - 1)), along(down1, -1, range(1, nz - 1))
    slot1 = jnp.where(z < 2, down1, up1)
    flip1 = cross(slot1)
    up2, down2, flip1, slot1 = tie((up2, down2, flip1, slot1))
    far = jnp.where(z == 1, down2, up2)
    far = lax.ppermute(far, "seq", [(2 + b, b) for b in range(2)] + [(4 + b, 6 + b) for b in range(2)])
    slot2 = jnp.where(z < 2, down2, up2)
    flip2 = cross(slot2)
    a0 = project(yc, block, flip0, w_out, w0, w1)
    a1 = project(yc, slot1, flip1, w_out, w0, w1)
    b0 = reduce_y(*a0)
    far, flip2, a1, b0 = tie((far, flip2, a1, b0))
    slot3 = jnp.where(z == 1, up1, jnp.where(z == 2, down1, far))
    flip3 = cross(slot3)
    b1 = reduce_y(*a1)
    a2 = project(yc, slot2, flip2, w_out, w0, w1)
    flip3, slot3, b1, a2 = tie((flip3, slot3, b1, a2))
    b2 = reduce_y(*a2)
    a3 = project(yc, slot3, flip3, w_out, w0, w1)
    r0 = deliver(0, b0)
    r0, b2, a3 = tie((r0, b2, a3))
    b3 = reduce_y(*a3)
    r1 = deliver(1, b1)
    r1, b3 = tie((r1, b3))
    results = [r0, r1, deliver(2, b2), deliver(3, b3)]
    results = [p.astype(F32) + q.astype(F32) for p, q in results]
    marks = []
    for slot in range(nz):
        mark = jnp.int32(-1)
        for a in range(nz):
            mark = jnp.where((z == table[a][slot]) & (grp // 2 == a // 2), a % 2, mark)
        marks.append(mark)
    pick = lambda which: sum(jnp.where(mark == which, r, 0.0) for mark, r in zip(marks, results)).astype(BF16)
    at = (y ^ core).astype(jnp.int32).reshape(1)
    return place(at, pick(core), cross(pick(1 - core)))


def prefix(array, axis, combine, identity):
    length, mine = (lax.axis_size(axis), lax.axis_index(axis))
    everything = jax.tree.map(lambda part: lax.all_gather(part, axis), array)
    start = jax.tree.map(
        lambda part, zero: jnp.broadcast_to(jnp.asarray(zero, part.dtype), part.shape),
        array,
        identity,
    )

    def turn(k, before):
        reached = k < mine
        new = combine(before, jax.tree.map(lambda part: part[k], everything))
        return jax.tree.map(lambda a, b: jnp.where(reached, a, b), new, before)

    return lax.fori_loop(0, length, turn, start)


def ssd_blocks(xf, dt, la, bm, cm, braw, craw, init):
    length, heads, width = xf.shape
    groups = bm.shape[1]
    ratio = heads // groups
    block = math.gcd(length, 256)
    count = length // block

    def step(state, blk):
        xb, dtb, lab, bb, cb, bnar, cnar = blk
        cum = jnp.cumsum(lab, axis=0)
        attention_logits = jnp.einsum("tgn,sgn->gts", cnar, bnar, preferred_element_type=F32)
        attention_logits = jnp.repeat(attention_logits, ratio, axis=0)
        diff = cum.T[:, :, None] - cum.T[:, None, :]
        rows = lax.broadcasted_iota(jnp.int32, (block, block), 0)
        cols = lax.broadcasted_iota(jnp.int32, (block, block), 1)
        mask = (rows >= cols)[None, :, :]
        decay = jnp.exp(jnp.where(mask, diff, -1e30))
        mixing = decay * attention_logits * dtb.T[:, None, :]
        outs = jnp.einsum("hts,shp->thp", mixing, xb, precision=HIGH)
        cheads = jnp.repeat(cb, ratio, axis=1)
        bheads = jnp.repeat(bb, ratio, axis=1)
        outs = outs + jnp.exp(cum)[:, :, None] * jnp.einsum("thn,hpn->thp", cheads, state, precision=HIGH)
        weights = jnp.exp(cum[-1][None, :] - cum) * dtb
        fresh = jnp.einsum("sh,shp,shn->hpn", weights, xb, bheads, precision=HIGH)
        state = jnp.exp(cum[-1])[:, None, None] * state + fresh
        return (state, outs)

    cut = lambda v: v.reshape((count, block) + v.shape[1:])
    final, outs = lax.scan(step, init, jax.tree.map(cut, (xf, dt, la, bm, cm, braw, craw)))
    return (outs.reshape(length, heads, width), final, jnp.sum(la, axis=0))


def gated_norm_output(y, multiplier_channels, norm_gain, groups):
    length = y.shape[0]
    gated = y.reshape(length, -1) * jax.nn.silu(multiplier_channels.astype(F32))
    split = gated.reshape(length, groups, -1)
    split = split * lax.rsqrt(jnp.mean(split * split, axis=-1, keepdims=True) + EPS)
    return (split.reshape(length, -1) * norm_gain).astype(BF16)


def combine_states(earlier_state, later):
    return (earlier_state[0] * later[0], later[0][:, None, None] * earlier_state[1] + later[1])


def general_shards(x_in, gate, b_proj, c_proj, dt_raw, dt_bias, a_log, skip_d, norm_gain, w_out):
    length = x_in.shape[0]
    heads = dt_raw.shape[1]
    groups = b_proj.shape[1] // STATE
    xf = x_in.astype(F32).reshape(length, heads, CHANNEL_WIDTH)
    dt = jax.nn.softplus(dt_raw + dt_bias)
    la = -jnp.exp(a_log) * dt
    braw = b_proj.reshape(length, groups, STATE)
    craw = c_proj.reshape(length, groups, STATE)
    bm = braw.astype(F32)
    cm = craw.astype(F32)
    empty = jnp.zeros((heads, CHANNEL_WIDTH, STATE), F32)
    y, local_end, total = ssd_blocks(xf, dt, la, bm, cm, braw, craw, empty)
    identity = (jnp.ones((heads,), F32), empty)
    carried = prefix((jnp.exp(total), local_end), "seq", combine_states, identity)
    cum = jnp.cumsum(la, axis=0)
    cheads = jnp.repeat(cm, heads // groups, axis=1)
    y = y + jnp.exp(cum)[:, :, None] * jnp.einsum("thn,hpn->thp", cheads, carried[1], precision=HIGH)
    y = y + skip_d[None, :, None] * xf
    normed = gated_norm_output(y, gate, norm_gain, groups)
    partial_out = jnp.dot(
        normed, lax.all_gather(w_out, "seq", axis=1, tiled=True), preferred_element_type=F32
    )
    return lax.psum_scatter(partial_out, "grp", scatter_dimension=1, tiled=True).astype(BF16)


def solution(mesh):
    seq, grp = mesh.shape["seq"], mesh.shape["grp"]

    def shards(*args):
        groups = args[2].shape[1] // STATE
        if grp == 4 and seq == 2 * grp and groups == 2:
            return pair_shards(grp, *args)
        return general_shards(*args)

    return jax.shard_map(
        shards,
        mesh=mesh,
        in_specs=(
            P("seq", "grp"),
            P("seq", "grp"),
            P("seq", "grp"),
            P("seq", "grp"),
            P("seq", "grp"),
            P("grp"),
            P("grp"),
            P("grp"),
            P("grp"),
            P("grp", "seq"),
        ),
        out_specs=P("seq", "grp"),
        check_vma=False,
    )
```

```python
import math

import jax
import jax.numpy as jnp
from jax import lax
from jax.experimental import pallas as pl
from jax.experimental.pallas import tpu as pltpu
from jax.sharding import PartitionSpec as P

CHANNEL_WIDTH = 128
STATE = 128
EPS = 1e-05

HIGH = lax.Precision.HIGHEST
F32 = jnp.float32
BF16 = jnp.bfloat16
NT = (((1,), (1,)), ((), ()))
TN = (((0,), (0,)), ((), ()))
VMEM_LIMIT = 24 * 2**20


def params(grid_dims=0, limit=VMEM_LIMIT):
    return pltpu.CompilerParams(
        vmem_limit_bytes=limit,
        dimension_semantics=("arbitrary",) * grid_dims if grid_dims else None,
    )


def cost(flops, moved):
    return pl.CostEstimate(flops=1, bytes_accessed=1, transcendentals=0)


def iota(shape, axis):
    return lax.broadcasted_iota(jnp.int32, shape, axis)


def spread(values, width):
    heads = values.shape[1]
    return jnp.concatenate(
        [jnp.broadcast_to(values[:, h : h + 1], (values.shape[0], width)) for h in range(heads)], axis=1
    )


def split3(value):
    hi = value.astype(BF16)
    rest = value - hi.astype(F32)
    mid = rest.astype(BF16)
    return hi, mid, (rest - mid.astype(F32)).astype(BF16)


def pack_kernel(y_ref, x_ref, b_ref, c_ref, dt_ref, out_ref, *, heads):
    width, state = x_ref.shape[1], b_ref.shape[1]
    out_ref[:, :width] = x_ref[...]
    out_ref[:, width : width + state] = b_ref[...]
    out_ref[:, width + state : width + 2 * state] = c_ref[...]
    other = 1 - y_ref[0]
    rows, cols = iota((2 * heads, 128), 0), iota((2 * heads, 128), 1)
    total = jnp.zeros((x_ref.shape[0], 128), F32)
    for part, value in enumerate(split3(dt_ref[...])):
        place = (cols == rows - other * heads + part * heads) & (rows // heads == other)
        total = total + lax.dot_general(value, place.astype(BF16), TN, preferred_element_type=F32)
    out_ref[:, width + 2 * state :] = total.astype(BF16)


def pack(y, x, b, c, dt, heads):
    tokens, width, state = x.shape[0], heads * CHANNEL_WIDTH, STATE
    full = width + 2 * state + 128
    return pl.pallas_call(
        lambda *refs: pack_kernel(*refs, heads=heads),
        grid_spec=pltpu.PrefetchScalarGridSpec(
            num_scalar_prefetch=1,
            grid=(1,),
            in_specs=[
                pl.BlockSpec((tokens, width), lambda i, y: (0, 1 - y[0])),
                pl.BlockSpec((tokens, state), lambda i, y: (0, 1 - y[0])),
                pl.BlockSpec((tokens, state), lambda i, y: (0, 1 - y[0])),
                pl.BlockSpec(dt.shape, lambda i, y: (0, 0)),
            ],
            out_specs=pl.BlockSpec((tokens, full), lambda i, y: (0, 0)),
        ),
        out_shape=jax.ShapeDtypeStruct((tokens, full), BF16),
        compiler_params=params(1, 60 * 2**20),
        cost_estimate=cost(1e6, 4 * tokens * full),
        name="pack",
    )(y, x, b, c, dt)


def local_state_kernel(
    y_ref, x_ref, b_ref, c_ref, dt_ref, pk_ref, bias_ref, alog_ref,
    xs_ref, bs_ref, cs_ref, scal_ref, send_ref, s_ref, *, heads,
):
    tokens, width = x_ref.shape
    state = b_ref.shape[1]
    y = y_ref[0]
    mine, theirs = pl.multiple_of(y * tokens, tokens), pl.multiple_of((1 - y) * tokens, tokens)
    xs_ref[pl.ds(mine, tokens), :] = x_ref[...]
    xs_ref[pl.ds(theirs, tokens), :] = pk_ref[:, :width]
    bs_ref[pl.ds(mine, tokens), :] = b_ref[...]
    bs_ref[pl.ds(theirs, tokens), :] = pk_ref[:, width : width + state]
    cs_ref[pl.ds(mine, tokens), :] = c_ref[...]
    cs_ref[pl.ds(theirs, tokens), :] = pk_ref[:, width + state : width + 2 * state]
    rows, cols = iota((2 * heads, heads), 0), iota((2 * heads, heads), 1)
    own = lax.dot_general(dt_ref[...], (rows == cols + y * heads).astype(F32), TN, precision=HIGH)
    rows, cols = iota((128, heads), 0), iota((128, heads), 1)
    take = ((rows % heads == cols) & (rows < 3 * heads)).astype(BF16)
    other = jnp.dot(pk_ref[:, width + 2 * state :], take, preferred_element_type=F32)
    raw = jnp.concatenate([jnp.where(y == 0, own, other), jnp.where(y == 0, other, own)], axis=0)
    raw = raw + bias_ref[...]
    dt = jnp.maximum(raw, 0.0) + jnp.log1p(jnp.exp(-jnp.abs(raw)))
    la = -jnp.exp(alog_ref[...]) * dt
    length = 2 * tokens
    lower = (iota((length, length), 0) >= iota((length, length), 1)).astype(F32)
    cum = jnp.dot(lower, la, precision=HIGH)
    last = cum[length - 1 : length, :]
    scal_ref[:, :heads] = cum
    scal_ref[:, heads : 2 * heads] = dt
    weights = jnp.exp(last - cum) * dt
    scaled = (xs_ref[...].astype(F32) * spread(weights, CHANNEL_WIDTH)).astype(BF16)
    s = lax.dot_general(bs_ref[...], scaled, TN, preferred_element_type=F32)
    s_ref[:state, :] = s
    send_ref[:state, :] = s.astype(BF16)
    decay = spread(jnp.exp(last), CHANNEL_WIDTH)
    s_ref[state:, :] = jnp.broadcast_to(decay, (8, width))
    hi, mid, lo = split3(decay)
    which = iota((16, width), 0)
    parts = jnp.where(which == 0, hi.astype(F32), jnp.where(which == 1, mid.astype(F32), lo.astype(F32)))
    send_ref[state:, :] = jnp.where(which < 3, parts, 0.0).astype(BF16)


def local_state(y, x, b, c, dt, pk, bias, alog, heads):
    tokens, width, state = x.shape[0], heads * CHANNEL_WIDTH, STATE
    whole = lambda a: pl.BlockSpec(a.shape, lambda i, y: (0,) * a.ndim)
    outs = [
        jax.ShapeDtypeStruct((2 * tokens, width), BF16),
        jax.ShapeDtypeStruct((2 * tokens, state), BF16),
        jax.ShapeDtypeStruct((2 * tokens, state), BF16),
        jax.ShapeDtypeStruct((2 * tokens, 2 * heads), F32),
        jax.ShapeDtypeStruct((state + 16, width), BF16),
        jax.ShapeDtypeStruct((state + 8, width), F32),
    ]
    return pl.pallas_call(
        lambda *refs: local_state_kernel(*refs, heads=heads),
        grid_spec=pltpu.PrefetchScalarGridSpec(
            num_scalar_prefetch=1,
            grid=(1,),
            in_specs=[
                pl.BlockSpec((tokens, width), lambda i, y: (0, y[0])),
                pl.BlockSpec((tokens, state), lambda i, y: (0, y[0])),
                pl.BlockSpec((tokens, state), lambda i, y: (0, y[0])),
                whole(dt),
                whole(pk),
                whole(bias),
                whole(alog),
            ],
            out_specs=[whole(o) for o in outs],
        ),
        out_shape=outs,
        compiler_params=params(1),
        cost_estimate=cost(2e8, 3e6),
        name="local_state",
    )(y, x, b, c, dt, pk, bias, alog)


def local_y_kernel(xs_ref, bs_ref, cs_ref, scal_ref, skip_ref, out_ref, *, heads, tokens):
    cum, dt = scal_ref[:, :heads], scal_ref[:, heads : 2 * heads]
    length = 2 * tokens
    eye = (iota((length, length), 0) == iota((length, length), 1)).astype(F32)
    flat = lax.dot_general(scal_ref[...], eye, TN, precision=HIGH)
    cum_row, dt_row = flat[:heads, :], flat[heads : 2 * heads, :]
    mask = iota((tokens, tokens), 0) >= iota((tokens, tokens), 1)
    logits = []
    for k in range(2):
        at = pl.ds(k * tokens, tokens)
        logits.append(lax.dot_general(cs_ref[at, :], bs_ref[at, :], NT, preferred_element_type=F32))
    middle = cum[tokens - 1 : tokens, :]
    weights = jnp.exp(middle - cum[:tokens, :]) * dt[:tokens, :]
    scaled = (xs_ref[:tokens, :].astype(F32) * spread(weights, CHANNEL_WIDTH)).astype(BF16)
    s = lax.dot_general(bs_ref[:tokens, :], scaled, TN, preferred_element_type=F32).astype(BF16)
    carried = jnp.dot(cs_ref[tokens:, :], s, preferred_element_type=F32)
    carried = carried * spread(jnp.exp(cum[tokens:, :] - middle), CHANNEL_WIDTH)
    for k in range(2):
        lo = k * tokens
        for h in range(heads):
            at = h * CHANNEL_WIDTH
            xh = xs_ref[lo : lo + tokens, at : at + CHANNEL_WIDTH]
            diff = cum[lo : lo + tokens, h : h + 1] - cum_row[h : h + 1, lo : lo + tokens]
            mix = jnp.exp(jnp.where(mask, diff, -1e30)) * logits[k] * dt_row[h : h + 1, lo : lo + tokens]
            top = mix.astype(BF16)
            yh = jnp.dot(top, xh, preferred_element_type=F32)
            yh = yh + jnp.dot((mix - top.astype(F32)).astype(BF16), xh, preferred_element_type=F32)
            yh = yh + skip_ref[:, at : at + CHANNEL_WIDTH] * xh.astype(F32)
            if k == 1:
                yh = yh + carried[:, at : at + CHANNEL_WIDTH]
            out_ref[lo : lo + tokens, at : at + CHANNEL_WIDTH] = yh


def local_y(xs, bs, cs, scal, skip, heads):
    length, width = xs.shape
    return pl.pallas_call(
        lambda *refs: local_y_kernel(*refs, heads=heads, tokens=length // 2),
        out_shape=jax.ShapeDtypeStruct((length, width), F32),
        compiler_params=params(),
        cost_estimate=cost(4e8, 4e6),
        name="local_y",
    )(xs, bs, cs, scal, skip)


def join_kernel(send_ref, s_ref, got_ref, out_ref):
    state = out_ref.shape[0]
    out_ref[...] = (s_ref[:state, :] + s_ref[state : state + 1, :] * got_ref[:state, :].astype(F32)).astype(BF16)


def join(send, s, got):
    return pl.pallas_call(
        join_kernel,
        out_shape=jax.ShapeDtypeStruct((STATE, s.shape[1]), BF16),
        compiler_params=params(),
        cost_estimate=cost(1e6, 1.5e6),
        name="join",
    )(send, s, got)


def finish_kernel(y_ref, local_ref, cs_ref, scal_ref, one_ref, two_ref, gate_ref, got_ref, gain_ref, out_ref, *, heads):
    length, width = local_ref.shape
    state, tokens = two_ref.shape[0], length // 2
    y = y_ref[0]
    decay = jnp.sum(one_ref[state:, :].astype(F32), axis=0, keepdims=True)
    start = one_ref[:state, :].astype(F32) + decay * two_ref[...].astype(F32)
    top = start.astype(BF16)
    low = (start - top.astype(F32)).astype(BF16)
    grow = jnp.exp(scal_ref[:, :heads])
    for k in range(2):
        at = pl.ds(k * tokens, tokens)
        carried = jnp.dot(cs_ref[at, :], top, preferred_element_type=F32)
        carried = carried + jnp.dot(cs_ref[at, :], low, preferred_element_type=F32)
        value = local_ref[at, :] + carried * spread(grow[k * tokens : (k + 1) * tokens, :], CHANNEL_WIDTH)
        gate = jnp.where(y == k, gate_ref[...], got_ref[...]).astype(F32)
        value = value * (gate / (1.0 + jnp.exp(-gate)))
        mean = jnp.sum(value * value, axis=1, keepdims=True) / width
        out_ref[at, :] = (value * lax.rsqrt(mean + EPS) * gain_ref[...]).astype(BF16)


def finish(y, local, cs, scal, one, two, gate, got, gain, heads):
    length, width = local.shape
    whole = lambda a: pl.BlockSpec(a.shape, lambda i, y: (0,) * a.ndim)
    return pl.pallas_call(
        lambda *refs: finish_kernel(*refs, heads=heads),
        grid_spec=pltpu.PrefetchScalarGridSpec(
            num_scalar_prefetch=1,
            grid=(1,),
            in_specs=[
                whole(local),
                whole(cs),
                whole(scal),
                whole(one),
                whole(two),
                pl.BlockSpec((length // 2, width), lambda i, y: (0, y[0])),
                whole(got),
                whole(gain),
            ],
            out_specs=pl.BlockSpec((length, width), lambda i, y: (0, 0)),
        ),
        out_shape=jax.ShapeDtypeStruct((length, width), BF16),
        compiler_params=params(1),
        cost_estimate=cost(1e8, 4e6),
        name="finish",
    )(y, local, cs, scal, one, two, gate, got, gain)


def project_kernel(yc_ref, *refs):
    *pair_refs, w_ref, w0_ref, w1_ref, keep_ref, send_ref, both_ref = refs
    slots, depth = len(pair_refs) // 2, pair_refs[0].shape[1]
    kept = keep_ref.shape[0]
    tokens = kept // slots
    y, core = yc_ref[0], yc_ref[1]

    @pl.when(pl.program_id(0) == 0)
    def _():
        for slot in range(slots):
            own_ref, got_ref = pair_refs[2 * slot], pair_refs[2 * slot + 1]
            for k in range(2):
                at = pl.ds(pl.multiple_of(jnp.where(y == 0, k, 1 - k) * tokens, tokens), tokens)
                rows = pl.ds(k * kept + slot * tokens, tokens)
                both_ref[rows, :depth] = jnp.where(core == 0, own_ref[at, :], got_ref[at, :])
                both_ref[rows, depth:] = jnp.where(core == 0, got_ref[at, :], own_ref[at, :])

    def multiply(first, second):
        part = jnp.dot(both_ref[:, :depth], first[...], preferred_element_type=F32)
        part = part + jnp.dot(both_ref[:, depth:], second[...], preferred_element_type=F32)
        keep_ref[...] = part[:kept, :]
        send_ref[...] = part[kept:, :].astype(BF16)

    @pl.when(core == 0)
    def _():
        multiply(w_ref, w0_ref)

    @pl.when(core == 1)
    def _():
        multiply(w0_ref, w1_ref)


def project(yc, pairs, w, w0, w1):
    length, depth = pairs[0][0].shape
    kept = len(pairs) * length // 2
    cols = w.shape[1]
    tile = min(cols, 256)
    return pl.pallas_call(
        project_kernel,
        grid_spec=pltpu.PrefetchScalarGridSpec(
            num_scalar_prefetch=1,
            grid=(cols // tile,),
            in_specs=[pl.BlockSpec((length, depth), lambda i, yc: (0, 0))] * (2 * len(pairs))
            + [
                pl.BlockSpec((depth, tile), lambda i, yc: (yc[0], jnp.where(yc[1] == 0, i, 0))),
                pl.BlockSpec((depth, tile), lambda i, yc: (0, i)),
                pl.BlockSpec((depth, tile), lambda i, yc: (0, jnp.where(yc[1] == 1, i, 0))),
            ],
            out_specs=[
                pl.BlockSpec((kept, tile), lambda i, yc: (0, i)),
                pl.BlockSpec((kept, tile), lambda i, yc: (0, i)),
            ],
            scratch_shapes=[pltpu.VMEM((2 * kept, 2 * depth), BF16)],
        ),
        out_shape=[jax.ShapeDtypeStruct((kept, cols), F32), jax.ShapeDtypeStruct((kept, cols), BF16)],
        compiler_params=params(1),
        cost_estimate=cost(8.0 * kept * depth * cols, 6e6),
        name="project",
    )(yc, *[v for pair in pairs for v in pair], w, w0, w1)


def place_kernel(at_ref, mine_ref, got_ref, out_ref):
    cols = got_ref.shape[1]
    part = at_ref[0]
    out_ref[:, pl.ds(pl.multiple_of(part * cols, cols), cols)] = mine_ref[...]
    out_ref[:, pl.ds(pl.multiple_of((1 - part) * cols, cols), cols)] = got_ref[...]


def place(at, mine, got):
    tokens, cols = got.shape
    whole = pl.BlockSpec((tokens, cols), lambda i, at: (0, 0))
    return pl.pallas_call(
        place_kernel,
        grid_spec=pltpu.PrefetchScalarGridSpec(
            num_scalar_prefetch=1,
            grid=(1,),
            in_specs=[whole, whole],
            out_specs=pl.BlockSpec((tokens, 2 * cols), lambda i, at: (0, 0)),
        ),
        out_shape=jax.ShapeDtypeStruct((tokens, 2 * cols), BF16),
        compiler_params=params(1),
        cost_estimate=cost(1e6, 2e6),
        name="place",
    )(at, mine, got)


def pair_shards(nz, x_in, gate, b_proj, c_proj, dt_raw, dt_bias, a_log, skip_d, norm_gain, w_out):
    tokens = x_in.shape[0]
    heads = dt_raw.shape[1] // 2
    width = heads * CHANNEL_WIDTH
    seq, grp = lax.axis_index("seq"), lax.axis_index("grp")
    z, y = seq // 2, seq % 2
    yv = y.astype(jnp.int32).reshape(1)
    yc = jnp.stack([y, grp % 2]).astype(jnp.int32)
    dt_raw = dt_raw.T
    both = ("seq", "grp")
    core = grp % 2
    spots = [(a, b, c, d) for a in range(nz) for b in range(2) for c in range(nz // 2) for d in range(2)]
    flat = lambda a, b, c, d: ((a * 2 + b) * (nz // 2) + c) * 2 + d
    tie = lax.optimization_barrier

    def half(v, axis, which):
        n = v.shape[axis] // 2
        return lax.dynamic_slice_in_dim(v, which * n, n, axis)

    flip = [(s, s ^ 1) for s in range(2 * nz)]
    sibling = [(g, g ^ 1) for g in range(nz)]
    across = [(flat(a, b, c, d), flat(a, 1 - b, c, 1 - d)) for a, b, c, d in spots]

    def along(v, step, senders):
        pairs = [(a * 2 + b, (a + step) * 2 + b) for a in senders for b in range(2)]
        return lax.ppermute(v, "seq", pairs)

    got = lax.ppermute(pack(yv, x_in, b_proj, c_proj, dt_raw, heads), "seq", flip)
    swap, go = half(w_out, 0, y ^ 1 ^ core), half(w_out, 0, 1 - y)
    gate_half = half(gate, 1, 1 - y)
    bias, alog = half(dt_bias, 0, y)[None, :], half(a_log, 0, y)[None, :]
    skip = jnp.repeat(half(skip_d, 0, y), CHANNEL_WIDTH)[None, :]
    gain = half(norm_gain, 0, y)[None, :]
    got_gate = lax.ppermute(gate_half, "seq", flip)
    got, swap, go, bias, alog, skip, gain = tie((got, swap, go, bias, alog, skip, gain))

    xs, bs, cs, scal, send, s = local_state(yv, x_in, b_proj, c_proj, dt_raw, got, bias, alog, heads)
    one = along(send, 1, range(nz - 1))
    got_gate, after = tie((got_gate, xs))
    base = local_y(after, bs, cs, scal, skip, heads)
    one, got_gate, base, swap, go = tie((one, got_gate, base, swap, go))

    two = along(join(send, s, one), 2, range(nz - 2))
    pairs = [(flat(a, b, c, 0), flat(a, 1 - b, c, 1)) for a, b, c, d in spots if d == 0]
    pairs += [(flat(a, b, c, 1), flat(a, b, c, 0)) for a, b, c, d in spots if d == 0]
    w0 = lax.ppermute(swap, both, pairs)
    w1 = lax.ppermute(go, both, [(flat(a, b, c, 1), flat(a, 1 - b, c, 1)) for a, b, c, d in spots if d == 0])
    block = finish(yv, base, cs, scal, one, two, gate, got_gate, gain, heads)

    table = [(0, 1, 2, 3), (1, 2, 3, 0), (2, 1, 0, 3), (3, 2, 1, 0)]
    cross = lambda value: lax.ppermute(value, "grp", sibling)

    def reduce_y(full, rounded):
        return (full + lax.ppermute(rounded, both, across).astype(F32)).astype(BF16)

    def deliver(slot, value, turn):
        pairs = [(flat(a, b, c, d), flat(table[a][slot], b, a // 2, d)) for a, b, c, d in spots if c ^ turn == a // 2]
        return lax.ppermute(value, both, pairs).astype(F32)

    up1, down1 = along(block, 1, range(nz - 1)), along(block, -1, range(1, nz))
    up1, down1, block = tie((up1, down1, block))
    up2, down2 = along(up1, 1, range(1, nz - 1)), along(down1, -1, range(1, nz - 1))
    slot1 = jnp.where(z < 2, down1, up1)
    flip0, flip1 = cross(block), cross(slot1)
    up2, down2, w0, w1 = tie((up2, down2, w0, w1))
    moves = [(2, 3), (1, 0), (0, 1), (3, 2)]
    slot3 = jnp.where(z == 1, down2, jnp.where(z == 2, up2, block))
    slot3 = lax.ppermute(slot3, "seq", [(i * 2 + b, j * 2 + b) for i, j in moves for b in range(2)])
    slot2 = jnp.where(z < 2, down2, up2)
    flip2 = cross(slot2)
    a0 = project(yc, [(block, flip0), (slot1, flip1)], w_out, w0, w1)
    flip2, slot2, a0 = tie((flip2, slot2, a0))
    a2 = project(yc, [(slot2, flip2)], w_out, w0, w1)
    slot3, a2 = tie((slot3, a2))
    flip3 = cross(slot3)
    b0 = reduce_y(*a0)
    flip3, slot3, b0 = tie((flip3, slot3, b0))
    a3 = project(yc, [(slot3, flip3)], w_out, w0, w1)
    b2 = reduce_y(*a2)
    chips = [(flat(a, b, 1 - c, d), flat(a, b, c, d)) for a, b, c, d in spots if c == a // 2]
    c0 = b0.astype(F32) + lax.ppermute(b0, both, chips).astype(F32)
    a3, b2 = tie((a3, b2))
    b3 = reduce_y(*a3)
    b3, c0 = tie((b3, c0))
    r1 = deliver(1, c0[tokens:].astype(BF16), 0)
    r2 = [deliver(2, b2, turn) for turn in range(2)]
    r3 = [deliver(3, b3, turn) for turn in range(2)]
    results = [c0[:tokens], r1, r2[0] + r2[1], r3[0] + r3[1]]
    marks = []
    for slot in range(nz):
        mark = jnp.int32(-1)
        for a in range(nz):
            mark = jnp.where((z == table[a][slot]) & (grp // 2 == a // 2), a % 2, mark)
        marks.append(mark)
    pick = lambda which: sum(jnp.where(mark == which, r, 0.0) for mark, r in zip(marks, results)).astype(BF16)
    at = (y ^ core).astype(jnp.int32).reshape(1)
    return place(at, pick(core), cross(pick(1 - core)))


def prefix(array, axis, combine, identity):
    length, mine = (lax.axis_size(axis), lax.axis_index(axis))
    everything = jax.tree.map(lambda part: lax.all_gather(part, axis), array)
    start = jax.tree.map(
        lambda part, zero: jnp.broadcast_to(jnp.asarray(zero, part.dtype), part.shape),
        array,
        identity,
    )

    def turn(k, before):
        reached = k < mine
        new = combine(before, jax.tree.map(lambda part: part[k], everything))
        return jax.tree.map(lambda a, b: jnp.where(reached, a, b), new, before)

    return lax.fori_loop(0, length, turn, start)


def ssd_blocks(xf, dt, la, bm, cm, braw, craw, init):
    length, heads, width = xf.shape
    groups = bm.shape[1]
    ratio = heads // groups
    block = math.gcd(length, 256)
    count = length // block

    def step(state, blk):
        xb, dtb, lab, bb, cb, bnar, cnar = blk
        cum = jnp.cumsum(lab, axis=0)
        attention_logits = jnp.einsum("tgn,sgn->gts", cnar, bnar, preferred_element_type=F32)
        attention_logits = jnp.repeat(attention_logits, ratio, axis=0)
        diff = cum.T[:, :, None] - cum.T[:, None, :]
        rows = lax.broadcasted_iota(jnp.int32, (block, block), 0)
        cols = lax.broadcasted_iota(jnp.int32, (block, block), 1)
        mask = (rows >= cols)[None, :, :]
        decay = jnp.exp(jnp.where(mask, diff, -1e30))
        mixing = decay * attention_logits * dtb.T[:, None, :]
        outs = jnp.einsum("hts,shp->thp", mixing, xb, precision=HIGH)
        cheads = jnp.repeat(cb, ratio, axis=1)
        bheads = jnp.repeat(bb, ratio, axis=1)
        outs = outs + jnp.exp(cum)[:, :, None] * jnp.einsum("thn,hpn->thp", cheads, state, precision=HIGH)
        weights = jnp.exp(cum[-1][None, :] - cum) * dtb
        fresh = jnp.einsum("sh,shp,shn->hpn", weights, xb, bheads, precision=HIGH)
        state = jnp.exp(cum[-1])[:, None, None] * state + fresh
        return (state, outs)

    cut = lambda v: v.reshape((count, block) + v.shape[1:])
    final, outs = lax.scan(step, init, jax.tree.map(cut, (xf, dt, la, bm, cm, braw, craw)))
    return (outs.reshape(length, heads, width), final, jnp.sum(la, axis=0))


def gated_norm_output(y, multiplier_channels, norm_gain, groups):
    length = y.shape[0]
    gated = y.reshape(length, -1) * jax.nn.silu(multiplier_channels.astype(F32))
    split = gated.reshape(length, groups, -1)
    split = split * lax.rsqrt(jnp.mean(split * split, axis=-1, keepdims=True) + EPS)
    return (split.reshape(length, -1) * norm_gain).astype(BF16)


def combine_states(earlier_state, later):
    return (earlier_state[0] * later[0], later[0][:, None, None] * earlier_state[1] + later[1])


def general_shards(x_in, gate, b_proj, c_proj, dt_raw, dt_bias, a_log, skip_d, norm_gain, w_out):
    length = x_in.shape[0]
    heads = dt_raw.shape[1]
    groups = b_proj.shape[1] // STATE
    xf = x_in.astype(F32).reshape(length, heads, CHANNEL_WIDTH)
    dt = jax.nn.softplus(dt_raw + dt_bias)
    la = -jnp.exp(a_log) * dt
    braw = b_proj.reshape(length, groups, STATE)
    craw = c_proj.reshape(length, groups, STATE)
    bm = braw.astype(F32)
    cm = craw.astype(F32)
    empty = jnp.zeros((heads, CHANNEL_WIDTH, STATE), F32)
    y, local_end, total = ssd_blocks(xf, dt, la, bm, cm, braw, craw, empty)
    identity = (jnp.ones((heads,), F32), empty)
    carried = prefix((jnp.exp(total), local_end), "seq", combine_states, identity)
    cum = jnp.cumsum(la, axis=0)
    cheads = jnp.repeat(cm, heads // groups, axis=1)
    y = y + jnp.exp(cum)[:, :, None] * jnp.einsum("thn,hpn->thp", cheads, carried[1], precision=HIGH)
    y = y + skip_d[None, :, None] * xf
    normed = gated_norm_output(y, gate, norm_gain, groups)
    partial_out = jnp.dot(
        normed, lax.all_gather(w_out, "seq", axis=1, tiled=True), preferred_element_type=F32
    )
    return lax.psum_scatter(partial_out, "grp", scatter_dimension=1, tiled=True).astype(BF16)


def solution(mesh):
    seq, grp = mesh.shape["seq"], mesh.shape["grp"]

    def shards(*args):
        groups = args[2].shape[1] // STATE
        if grp == 4 and seq == 2 * grp and groups == 2:
            return pair_shards(grp, *args)
        return general_shards(*args)

    return jax.shard_map(
        shards,
        mesh=mesh,
        in_specs=(
            P("seq", "grp"),
            P("seq", "grp"),
            P("seq", "grp"),
            P("seq", "grp"),
            P("seq", "grp"),
            P("grp"),
            P("grp"),
            P("grp"),
            P("grp"),
            P("grp", "seq"),
        ),
        out_specs=P("seq", "grp"),
        check_vma=False,
    )
```

```python
import math

import jax
import jax.numpy as jnp
from jax import lax
from jax.experimental import pallas as pl
from jax.experimental.pallas import tpu as pltpu
from jax.sharding import PartitionSpec as P

CHANNEL_WIDTH = 128
STATE = 128
EPS = 1e-05

HIGH = lax.Precision.HIGHEST
F32 = jnp.float32
BF16 = jnp.bfloat16
NT = (((1,), (1,)), ((), ()))
TN = (((0,), (0,)), ((), ()))
VMEM_LIMIT = 24 * 2**20


def params(grid_dims=0, limit=VMEM_LIMIT):
    return pltpu.CompilerParams(
        vmem_limit_bytes=limit,
        dimension_semantics=("arbitrary",) * grid_dims if grid_dims else None,
    )


def cost(flops, moved):
    return pl.CostEstimate(flops=1, bytes_accessed=1, transcendentals=0)


def iota(shape, axis):
    return lax.broadcasted_iota(jnp.int32, shape, axis)


def spread(values, width):
    heads = values.shape[1]
    return jnp.concatenate(
        [jnp.broadcast_to(values[:, h : h + 1], (values.shape[0], width)) for h in range(heads)], axis=1
    )


def split3(value):
    hi = value.astype(BF16)
    rest = value - hi.astype(F32)
    mid = rest.astype(BF16)
    return hi, mid, (rest - mid.astype(F32)).astype(BF16)


def pack_kernel(y_ref, x_ref, b_ref, c_ref, dt_ref, own_ref, out_ref, *, heads):
    width, state = x_ref.shape[1] // 2, b_ref.shape[1] // 2
    rows, cols = iota((2 * heads, 128), 0), iota((2 * heads, 128), 1)
    parts = split3(dt_ref[...])
    for group in range(2):
        total = jnp.zeros((x_ref.shape[0], 128), F32)
        for part, value in enumerate(parts):
            where = (cols == rows - group * heads + part * heads) & (rows // heads == group)
            total = total + lax.dot_general(value, where.astype(BF16), TN, preferred_element_type=F32)
        steps = total.astype(BF16)

        def fill(ref):
            ref[:, :width] = x_ref[:, group * width : (group + 1) * width]
            ref[:, width : width + state] = b_ref[:, group * state : (group + 1) * state]
            ref[:, width + state : width + 2 * state] = c_ref[:, group * state : (group + 1) * state]
            ref[:, width + 2 * state :] = steps

        @pl.when(y_ref[0] == group)
        def _():
            fill(own_ref)

        @pl.when(y_ref[0] != group)
        def _():
            fill(out_ref)


def pack(y, x, b, c, dt, heads):
    tokens = x.shape[0]
    full = heads * CHANNEL_WIDTH + 2 * STATE + 128
    whole = lambda a: pl.BlockSpec(a.shape, lambda i, y: (0,) * a.ndim)
    out = jax.ShapeDtypeStruct((tokens, full), BF16)
    return pl.pallas_call(
        lambda *refs: pack_kernel(*refs, heads=heads),
        grid_spec=pltpu.PrefetchScalarGridSpec(
            num_scalar_prefetch=1,
            grid=(1,),
            in_specs=[whole(x), whole(b), whole(c), whole(dt)],
            out_specs=[whole(out), whole(out)],
        ),
        out_shape=[out, out],
        compiler_params=params(1, 60 * 2**20),
        cost_estimate=cost(1e6, 4 * tokens * full),
        name="pack",
    )(y, x, b, c, dt)


def local_state_kernel(
    y_ref, own_ref, pk_ref, bias_ref, alog_ref, xs_ref, bs_ref, cs_ref, scal_ref, send_ref, s_ref, *, heads,
):
    tokens = own_ref.shape[0]
    width, state = xs_ref.shape[1], bs_ref.shape[1]
    y = y_ref[0]
    rows, cols = iota((128, heads), 0), iota((128, heads), 1)
    take = ((rows % heads == cols) & (rows < 3 * heads)).astype(BF16)
    steps = []
    for ref, place in ((own_ref, y), (pk_ref, 1 - y)):
        at = pl.ds(pl.multiple_of(place * tokens, tokens), tokens)
        xs_ref[at, :] = ref[:, :width]
        bs_ref[at, :] = ref[:, width : width + state]
        cs_ref[at, :] = ref[:, width + state : width + 2 * state]
        steps.append(jnp.dot(ref[:, width + 2 * state :], take, preferred_element_type=F32))
    own, other = steps
    raw = jnp.concatenate([jnp.where(y == 0, own, other), jnp.where(y == 0, other, own)], axis=0)
    raw = raw + bias_ref[...]
    dt = jnp.maximum(raw, 0.0) + jnp.log1p(jnp.exp(-jnp.abs(raw)))
    la = -jnp.exp(alog_ref[...]) * dt
    length = 2 * tokens
    lower = (iota((length, length), 0) >= iota((length, length), 1)).astype(F32)
    cum = jnp.dot(lower, la, precision=HIGH)
    last = cum[length - 1 : length, :]
    scal_ref[:, :heads] = cum
    scal_ref[:, heads : 2 * heads] = dt
    weights = jnp.exp(last - cum) * dt
    scaled = (xs_ref[...].astype(F32) * spread(weights, CHANNEL_WIDTH)).astype(BF16)
    s = lax.dot_general(bs_ref[...], scaled, TN, preferred_element_type=F32)
    s_ref[:state, :] = s
    send_ref[:state, :] = s.astype(BF16)
    decay = spread(jnp.exp(last), CHANNEL_WIDTH)
    s_ref[state:, :] = jnp.broadcast_to(decay, (8, width))
    hi, mid, lo = split3(decay)
    which = iota((16, width), 0)
    parts = jnp.where(which == 0, hi.astype(F32), jnp.where(which == 1, mid.astype(F32), lo.astype(F32)))
    send_ref[state:, :] = jnp.where(which < 3, parts, 0.0).astype(BF16)


def local_state(y, own, pk, bias, alog, heads):
    tokens, width, state = own.shape[0], heads * CHANNEL_WIDTH, STATE
    whole = lambda a: pl.BlockSpec(a.shape, lambda i, y: (0,) * a.ndim)
    outs = [
        jax.ShapeDtypeStruct((2 * tokens, width), BF16),
        jax.ShapeDtypeStruct((2 * tokens, state), BF16),
        jax.ShapeDtypeStruct((2 * tokens, state), BF16),
        jax.ShapeDtypeStruct((2 * tokens, 2 * heads), F32),
        jax.ShapeDtypeStruct((state + 16, width), BF16),
        jax.ShapeDtypeStruct((state + 8, width), F32),
    ]
    return pl.pallas_call(
        lambda *refs: local_state_kernel(*refs, heads=heads),
        grid_spec=pltpu.PrefetchScalarGridSpec(
            num_scalar_prefetch=1,
            grid=(1,),
            in_specs=[whole(own), whole(pk), whole(bias), whole(alog)],
            out_specs=[whole(o) for o in outs],
        ),
        out_shape=outs,
        compiler_params=params(1),
        cost_estimate=cost(2e8, 3e6),
        name="local_state",
    )(y, own, pk, bias, alog)


def local_y_kernel(xs_ref, bs_ref, cs_ref, scal_ref, skip_ref, out_ref, *, heads, tokens):
    cum, dt = scal_ref[:, :heads], scal_ref[:, heads : 2 * heads]
    length = 2 * tokens
    eye = (iota((length, length), 0) == iota((length, length), 1)).astype(F32)
    flat = lax.dot_general(scal_ref[...], eye, TN, precision=HIGH)
    cum_row, dt_row = flat[:heads, :], flat[heads : 2 * heads, :]
    mask = iota((tokens, tokens), 0) >= iota((tokens, tokens), 1)
    logits = []
    for k in range(2):
        at = pl.ds(k * tokens, tokens)
        logits.append(lax.dot_general(cs_ref[at, :], bs_ref[at, :], NT, preferred_element_type=F32))
    middle = cum[tokens - 1 : tokens, :]
    weights = jnp.exp(middle - cum[:tokens, :]) * dt[:tokens, :]
    scaled = (xs_ref[:tokens, :].astype(F32) * spread(weights, CHANNEL_WIDTH)).astype(BF16)
    s = lax.dot_general(bs_ref[:tokens, :], scaled, TN, preferred_element_type=F32).astype(BF16)
    carried = jnp.dot(cs_ref[tokens:, :], s, preferred_element_type=F32)
    carried = carried * spread(jnp.exp(cum[tokens:, :] - middle), CHANNEL_WIDTH)
    for k in range(2):
        lo = k * tokens
        for h in range(heads):
            at = h * CHANNEL_WIDTH
            xh = xs_ref[lo : lo + tokens, at : at + CHANNEL_WIDTH]
            diff = cum[lo : lo + tokens, h : h + 1] - cum_row[h : h + 1, lo : lo + tokens]
            mix = jnp.exp(jnp.where(mask, diff, -1e30)) * logits[k] * dt_row[h : h + 1, lo : lo + tokens]
            top = mix.astype(BF16)
            yh = jnp.dot(top, xh, preferred_element_type=F32)
            yh = yh + jnp.dot((mix - top.astype(F32)).astype(BF16), xh, preferred_element_type=F32)
            yh = yh + skip_ref[:, at : at + CHANNEL_WIDTH] * xh.astype(F32)
            if k == 1:
                yh = yh + carried[:, at : at + CHANNEL_WIDTH]
            out_ref[lo : lo + tokens, at : at + CHANNEL_WIDTH] = yh


def local_y(xs, bs, cs, scal, skip, heads):
    length, width = xs.shape
    return pl.pallas_call(
        lambda *refs: local_y_kernel(*refs, heads=heads, tokens=length // 2),
        out_shape=jax.ShapeDtypeStruct((length, width), F32),
        compiler_params=params(),
        cost_estimate=cost(4e8, 4e6),
        name="local_y",
    )(xs, bs, cs, scal, skip)


def join_kernel(send_ref, s_ref, got_ref, out_ref):
    state = out_ref.shape[0]
    out_ref[...] = (s_ref[:state, :] + s_ref[state : state + 1, :] * got_ref[:state, :].astype(F32)).astype(BF16)


def join(send, s, got):
    return pl.pallas_call(
        join_kernel,
        out_shape=jax.ShapeDtypeStruct((STATE, s.shape[1]), BF16),
        compiler_params=params(),
        cost_estimate=cost(1e6, 1.5e6),
        name="join",
    )(send, s, got)


def finish_kernel(y_ref, local_ref, cs_ref, scal_ref, one_ref, two_ref, gate_ref, got_ref, gain_ref, out_ref, *, heads):
    length, width = local_ref.shape
    state, tokens = two_ref.shape[0], length // 2
    y = y_ref[0]
    decay = jnp.sum(one_ref[state:, :].astype(F32), axis=0, keepdims=True)
    start = one_ref[:state, :].astype(F32) + decay * two_ref[...].astype(F32)
    top = start.astype(BF16)
    low = (start - top.astype(F32)).astype(BF16)
    grow = jnp.exp(scal_ref[:, :heads])
    for k in range(2):
        at = pl.ds(k * tokens, tokens)
        carried = jnp.dot(cs_ref[at, :], top, preferred_element_type=F32)
        carried = carried + jnp.dot(cs_ref[at, :], low, preferred_element_type=F32)
        value = local_ref[at, :] + carried * spread(grow[k * tokens : (k + 1) * tokens, :], CHANNEL_WIDTH)
        gate = jnp.where(y == k, gate_ref[...], got_ref[...]).astype(F32)
        value = value * (gate / (1.0 + jnp.exp(-gate)))
        mean = jnp.sum(value * value, axis=1, keepdims=True) / width
        out_ref[at, :] = (value * lax.rsqrt(mean + EPS) * gain_ref[...]).astype(BF16)


def finish(y, local, cs, scal, one, two, gate, got, gain, heads):
    length, width = local.shape
    whole = lambda a: pl.BlockSpec(a.shape, lambda i, y: (0,) * a.ndim)
    return pl.pallas_call(
        lambda *refs: finish_kernel(*refs, heads=heads),
        grid_spec=pltpu.PrefetchScalarGridSpec(
            num_scalar_prefetch=1,
            grid=(1,),
            in_specs=[
                whole(local),
                whole(cs),
                whole(scal),
                whole(one),
                whole(two),
                pl.BlockSpec((length // 2, width), lambda i, y: (0, y[0])),
                whole(got),
                whole(gain),
            ],
            out_specs=pl.BlockSpec((length, width), lambda i, y: (0, 0)),
        ),
        out_shape=jax.ShapeDtypeStruct((length, width), BF16),
        compiler_params=params(1),
        cost_estimate=cost(1e8, 4e6),
        name="finish",
    )(y, local, cs, scal, one, two, gate, got, gain)


def project_kernel(yc_ref, *refs):
    *pair_refs, first_ref, second_ref, keep_ref, send_ref, both_ref = refs
    slots, depth = len(pair_refs) // 2, pair_refs[0].shape[1]
    kept = keep_ref.shape[0]
    tokens = kept // slots
    core = yc_ref[1]

    @pl.when(pl.program_id(0) == 0)
    def _():
        for slot in range(slots):
            own_ref, got_ref = pair_refs[2 * slot], pair_refs[2 * slot + 1]
            for k in range(2):
                at = pl.ds(pl.multiple_of(jnp.where(core == 0, k, 1 - k) * tokens, tokens), tokens)
                rows = pl.ds(k * kept + slot * tokens, tokens)
                both_ref[rows, :depth] = own_ref[at, :]
                both_ref[rows, depth:] = got_ref[at, :]

    part = jnp.dot(both_ref[:, :depth], first_ref[...], preferred_element_type=F32)
    part = part + jnp.dot(both_ref[:, depth:], second_ref[...], preferred_element_type=F32)
    keep_ref[...] = part[:kept, :]
    send_ref[...] = part[kept:, :].astype(BF16)


def project(yc, pairs, w):
    length, depth = pairs[0][0].shape
    kept = len(pairs) * length // 2
    cols = w.shape[1]
    tile = min(cols, 256)
    return pl.pallas_call(
        project_kernel,
        grid_spec=pltpu.PrefetchScalarGridSpec(
            num_scalar_prefetch=1,
            grid=(cols // tile,),
            in_specs=[pl.BlockSpec((length, depth), lambda i, yc: (0, 0))] * (2 * len(pairs))
            + [
                pl.BlockSpec((depth, tile), lambda i, yc: (yc[0], i)),
                pl.BlockSpec((depth, tile), lambda i, yc: (1 - yc[0], i)),
            ],
            out_specs=[
                pl.BlockSpec((kept, tile), lambda i, yc: (0, i)),
                pl.BlockSpec((kept, tile), lambda i, yc: (0, i)),
            ],
            scratch_shapes=[pltpu.VMEM((2 * kept, 2 * depth), BF16)],
        ),
        out_shape=[jax.ShapeDtypeStruct((kept, cols), F32), jax.ShapeDtypeStruct((kept, cols), BF16)],
        compiler_params=params(1),
        cost_estimate=cost(8.0 * kept * depth * cols, 6e6),
        name="project",
    )(yc, *[v for pair in pairs for v in pair], w, w)


def place_kernel(at_ref, mine_ref, got_ref, out_ref):
    cols = got_ref.shape[1]
    part = at_ref[0]
    out_ref[:, pl.ds(pl.multiple_of(part * cols, cols), cols)] = mine_ref[...]
    out_ref[:, pl.ds(pl.multiple_of((1 - part) * cols, cols), cols)] = got_ref[...]


def place(at, mine, got):
    tokens, cols = got.shape
    whole = pl.BlockSpec((tokens, cols), lambda i, at: (0, 0))
    return pl.pallas_call(
        place_kernel,
        grid_spec=pltpu.PrefetchScalarGridSpec(
            num_scalar_prefetch=1,
            grid=(1,),
            in_specs=[whole, whole],
            out_specs=pl.BlockSpec((tokens, 2 * cols), lambda i, at: (0, 0)),
        ),
        out_shape=jax.ShapeDtypeStruct((tokens, 2 * cols), BF16),
        compiler_params=params(1),
        cost_estimate=cost(1e6, 2e6),
        name="place",
    )(at, mine, got)


def pair_shards(nz, x_in, gate, b_proj, c_proj, dt_raw, dt_bias, a_log, skip_d, norm_gain, w_out):
    tokens = x_in.shape[0]
    heads = dt_raw.shape[1] // 2
    width = heads * CHANNEL_WIDTH
    seq, grp = lax.axis_index("seq"), lax.axis_index("grp")
    z, y = seq // 2, seq % 2
    yv = y.astype(jnp.int32).reshape(1)
    yc = jnp.stack([y, grp % 2]).astype(jnp.int32)
    dt_raw = dt_raw.T
    both = ("seq", "grp")
    core = grp % 2
    spots = [(a, b, c, d) for a in range(nz) for b in range(2) for c in range(nz // 2) for d in range(2)]
    flat = lambda a, b, c, d: ((a * 2 + b) * (nz // 2) + c) * 2 + d
    tie = lax.optimization_barrier

    def half(v, axis, which):
        n = v.shape[axis] // 2
        return lax.dynamic_slice_in_dim(v, which * n, n, axis)

    flip = [(s, s ^ 1) for s in range(2 * nz)]
    sibling = [(g, g ^ 1) for g in range(nz)]
    def along(v, step, senders):
        pairs = [(a * 2 + b, (a + step) * 2 + b) for a in senders for b in range(2)]
        return lax.ppermute(v, "seq", pairs)

    own, packed = pack(yv, x_in, b_proj, c_proj, dt_raw, heads)
    got = lax.ppermute(packed, "seq", flip)
    gate_half = half(gate, 1, 1 - y)
    bias, alog = half(dt_bias, 0, y)[None, :], half(a_log, 0, y)[None, :]
    skip = jnp.repeat(half(skip_d, 0, y), CHANNEL_WIDTH)[None, :]
    gain = half(norm_gain, 0, y)[None, :]
    got_gate = lax.ppermute(gate_half, "seq", flip)
    got, bias, alog, skip, gain = tie((got, bias, alog, skip, gain))

    xs, bs, cs, scal, send, s = local_state(yv, own, got, bias, alog, heads)
    one = along(send, 1, range(nz - 1))
    base = local_y(xs, bs, cs, scal, skip, heads)
    one, base = tie((one, base))

    two = along(join(send, s, one), 2, range(nz - 2))
    block = finish(yv, base, cs, scal, one, two, gate, got_gate, gain, heads)

    hop = lambda value, *moves: lax.ppermute(value, "seq", [(i * 2 + b, j * 2 + b) for i, j in moves for b in range(2)])
    inner = (z == 1) | (z == 2)
    across = lambda value: lax.ppermute(value, "seq", flip)
    cross = lambda value: lax.ppermute(value, "grp", sibling)

    def reduce_core(full, rounded):
        return (full + cross(rounded).astype(F32)).astype(BF16)

    def deliver(slot, near, distant):
        near_x, total = grp // 2 == z // 2, 0.0
        for turn in range(2):
            pairs = []
            for a, b, c, d in spots:
                at = slot if c ^ turn == a // 2 else slot + 2
                pairs.append((flat(a, b, c, d), flat(a ^ at, d, a // 2, b)))
            value = jnp.where(near_x, near, distant) if turn == 0 else jnp.where(near_x, distant, near)
            moved = lax.ppermute(value, both, [(i, j) for i, j in pairs if i != j])
            if any(i == j for i, j in pairs):
                moved = jnp.where(near_x & (y == core), near, moved)
            total = total + moved.astype(F32)
        return total

    slot1 = hop(block, (0, 1), (1, 0), (2, 3), (3, 2))
    middle = hop(block, (1, 2), (2, 1))
    other0 = across(block)
    inward, outward = hop(slot1, (1, 2), (2, 1)), hop(middle, (1, 0), (2, 3))
    other1 = across(slot1)
    a0 = project(yc, [(block, other0)], w_out)
    inward, outward, other1, a0 = tie((inward, outward, other1, a0))
    last = hop(inward, (1, 0), (2, 3))
    slot2 = jnp.where(inner, inward, outward)
    other2 = across(slot2)
    a1 = project(yc, [(slot1, other1)], w_out)
    b0 = reduce_core(*a0)
    last, other2, a1, b0 = tie((last, other2, a1, b0))
    slot3 = jnp.where(inner, middle, last)
    other3 = across(slot3)
    b1 = reduce_core(*a1)
    b2 = reduce_core(*project(yc, [(slot2, other2)], w_out))
    other3, b2, b1 = tie((other3, b2, b1))
    b3 = reduce_core(*project(yc, [(slot3, other3)], w_out))
    even = deliver(0, b0, b2)
    b3, = tie((b3,))
    odd = deliver(1, b1, b3)
    here = core == z % 2
    mine, theirs = jnp.where(here, even, odd), jnp.where(here, odd, even)
    return place(core.astype(jnp.int32).reshape(1), mine.astype(BF16), cross(theirs.astype(BF16)))


def prefix(array, axis, combine, identity):
    length, mine = (lax.axis_size(axis), lax.axis_index(axis))
    everything = jax.tree.map(lambda part: lax.all_gather(part, axis), array)
    start = jax.tree.map(
        lambda part, zero: jnp.broadcast_to(jnp.asarray(zero, part.dtype), part.shape),
        array,
        identity,
    )

    def turn(k, before):
        reached = k < mine
        new = combine(before, jax.tree.map(lambda part: part[k], everything))
        return jax.tree.map(lambda a, b: jnp.where(reached, a, b), new, before)

    return lax.fori_loop(0, length, turn, start)


def ssd_blocks(xf, dt, la, bm, cm, braw, craw, init):
    length, heads, width = xf.shape
    groups = bm.shape[1]
    ratio = heads // groups
    block = math.gcd(length, 256)
    count = length // block

    def step(state, blk):
        xb, dtb, lab, bb, cb, bnar, cnar = blk
        cum = jnp.cumsum(lab, axis=0)
        attention_logits = jnp.einsum("tgn,sgn->gts", cnar, bnar, preferred_element_type=F32)
        attention_logits = jnp.repeat(attention_logits, ratio, axis=0)
        diff = cum.T[:, :, None] - cum.T[:, None, :]
        rows = lax.broadcasted_iota(jnp.int32, (block, block), 0)
        cols = lax.broadcasted_iota(jnp.int32, (block, block), 1)
        mask = (rows >= cols)[None, :, :]
        decay = jnp.exp(jnp.where(mask, diff, -1e30))
        mixing = decay * attention_logits * dtb.T[:, None, :]
        outs = jnp.einsum("hts,shp->thp", mixing, xb, precision=HIGH)
        cheads = jnp.repeat(cb, ratio, axis=1)
        bheads = jnp.repeat(bb, ratio, axis=1)
        outs = outs + jnp.exp(cum)[:, :, None] * jnp.einsum("thn,hpn->thp", cheads, state, precision=HIGH)
        weights = jnp.exp(cum[-1][None, :] - cum) * dtb
        fresh = jnp.einsum("sh,shp,shn->hpn", weights, xb, bheads, precision=HIGH)
        state = jnp.exp(cum[-1])[:, None, None] * state + fresh
        return (state, outs)

    cut = lambda v: v.reshape((count, block) + v.shape[1:])
    final, outs = lax.scan(step, init, jax.tree.map(cut, (xf, dt, la, bm, cm, braw, craw)))
    return (outs.reshape(length, heads, width), final, jnp.sum(la, axis=0))


def gated_norm_output(y, multiplier_channels, norm_gain, groups):
    length = y.shape[0]
    gated = y.reshape(length, -1) * jax.nn.silu(multiplier_channels.astype(F32))
    split = gated.reshape(length, groups, -1)
    split = split * lax.rsqrt(jnp.mean(split * split, axis=-1, keepdims=True) + EPS)
    return (split.reshape(length, -1) * norm_gain).astype(BF16)


def combine_states(earlier_state, later):
    return (earlier_state[0] * later[0], later[0][:, None, None] * earlier_state[1] + later[1])


def general_shards(x_in, gate, b_proj, c_proj, dt_raw, dt_bias, a_log, skip_d, norm_gain, w_out):
    length = x_in.shape[0]
    heads = dt_raw.shape[1]
    groups = b_proj.shape[1] // STATE
    xf = x_in.astype(F32).reshape(length, heads, CHANNEL_WIDTH)
    dt = jax.nn.softplus(dt_raw + dt_bias)
    la = -jnp.exp(a_log) * dt
    braw = b_proj.reshape(length, groups, STATE)
    craw = c_proj.reshape(length, groups, STATE)
    bm = braw.astype(F32)
    cm = craw.astype(F32)
    empty = jnp.zeros((heads, CHANNEL_WIDTH, STATE), F32)
    y, local_end, total = ssd_blocks(xf, dt, la, bm, cm, braw, craw, empty)
    identity = (jnp.ones((heads,), F32), empty)
    carried = prefix((jnp.exp(total), local_end), "seq", combine_states, identity)
    cum = jnp.cumsum(la, axis=0)
    cheads = jnp.repeat(cm, heads // groups, axis=1)
    y = y + jnp.exp(cum)[:, :, None] * jnp.einsum("thn,hpn->thp", cheads, carried[1], precision=HIGH)
    y = y + skip_d[None, :, None] * xf
    normed = gated_norm_output(y, gate, norm_gain, groups)
    partial_out = jnp.dot(
        normed, lax.all_gather(w_out, "seq", axis=1, tiled=True), preferred_element_type=F32
    )
    return lax.psum_scatter(partial_out, "grp", scatter_dimension=1, tiled=True).astype(BF16)


def solution(mesh):
    seq, grp = mesh.shape["seq"], mesh.shape["grp"]

    def shards(*args):
        groups = args[2].shape[1] // STATE
        if grp == 4 and seq == 2 * grp and groups == 2:
            return pair_shards(grp, *args)
        return general_shards(*args)

    return jax.shard_map(
        shards,
        mesh=mesh,
        in_specs=(
            P("seq", "grp"),
            P("seq", "grp"),
            P("seq", "grp"),
            P("seq", "grp"),
            P("seq", "grp"),
            P("grp"),
            P("grp"),
            P("grp"),
            P("grp"),
            P("grp", "seq"),
        ),
        out_specs=P("seq", "grp"),
        check_vma=False,
    )
```

```python
import math

import jax
import jax.numpy as jnp
from jax import lax
from jax.experimental import pallas as pl
from jax.experimental.pallas import tpu as pltpu
from jax.sharding import PartitionSpec as P

CHANNEL_WIDTH = 128
STATE = 128
EPS = 1e-05

HIGH = lax.Precision.HIGHEST
F32 = jnp.float32
BF16 = jnp.bfloat16
NT = (((1,), (1,)), ((), ()))
TN = (((0,), (0,)), ((), ()))
VMEM_LIMIT = 24 * 2**20


def params(grid_dims=0, limit=VMEM_LIMIT):
    return pltpu.CompilerParams(
        vmem_limit_bytes=limit,
        dimension_semantics=("arbitrary",) * grid_dims if grid_dims else None,
    )


def cost(flops, moved):
    return pl.CostEstimate(flops=1, bytes_accessed=1, transcendentals=0)


def iota(shape, axis):
    return lax.broadcasted_iota(jnp.int32, shape, axis)


def spread(values, width):
    heads = values.shape[1]
    return jnp.concatenate(
        [jnp.broadcast_to(values[:, h : h + 1], (values.shape[0], width)) for h in range(heads)], axis=1
    )


def split3(value):
    hi = value.astype(BF16)
    rest = value - hi.astype(F32)
    mid = rest.astype(BF16)
    return hi, mid, (rest - mid.astype(F32)).astype(BF16)


def pack_kernel(y_ref, x_ref, b_ref, c_ref, dt_ref, own_ref, out_ref, *, heads):
    width, state = x_ref.shape[1] // 2, b_ref.shape[1] // 2
    rows, cols = iota((2 * heads, 128), 0), iota((2 * heads, 128), 1)
    parts = split3(dt_ref[...])
    for group in range(2):
        total = jnp.zeros((x_ref.shape[0], 128), F32)
        for part, value in enumerate(parts):
            where = (cols == rows - group * heads + part * heads) & (rows // heads == group)
            total = total + lax.dot_general(value, where.astype(BF16), TN, preferred_element_type=F32)
        steps = total.astype(BF16)

        def fill(ref):
            ref[:, :width] = x_ref[:, group * width : (group + 1) * width]
            ref[:, width : width + state] = b_ref[:, group * state : (group + 1) * state]
            ref[:, width + state : width + 2 * state] = c_ref[:, group * state : (group + 1) * state]
            ref[:, width + 2 * state :] = steps

        @pl.when(y_ref[0] == group)
        def _():
            fill(own_ref)

        @pl.when(y_ref[0] != group)
        def _():
            fill(out_ref)


def pack(y, x, b, c, dt, heads):
    tokens = x.shape[0]
    full = heads * CHANNEL_WIDTH + 2 * STATE + 128
    whole = lambda a: pl.BlockSpec(a.shape, lambda i, y: (0,) * a.ndim)
    out = jax.ShapeDtypeStruct((tokens, full), BF16)
    return pl.pallas_call(
        lambda *refs: pack_kernel(*refs, heads=heads),
        grid_spec=pltpu.PrefetchScalarGridSpec(
            num_scalar_prefetch=1,
            grid=(1,),
            in_specs=[whole(x), whole(b), whole(c), whole(dt)],
            out_specs=[whole(out), whole(out)],
        ),
        out_shape=[out, out],
        compiler_params=params(1, 60 * 2**20),
        cost_estimate=cost(1e6, 4 * tokens * full),
        name="pack",
    )(y, x, b, c, dt)


def local_state_kernel(
    y_ref, own_ref, pk_ref, bias_ref, alog_ref, xs_ref, bs_ref, cs_ref, scal_ref, send_ref, s_ref, *, heads,
):
    tokens = own_ref.shape[0]
    width, state = xs_ref.shape[1], bs_ref.shape[1]
    y = y_ref[0]
    rows, cols = iota((128, heads), 0), iota((128, heads), 1)
    take = ((rows % heads == cols) & (rows < 3 * heads)).astype(BF16)
    steps = []
    for ref, place in ((own_ref, y), (pk_ref, 1 - y)):
        at = pl.ds(pl.multiple_of(place * tokens, tokens), tokens)
        xs_ref[at, :] = ref[:, :width]
        bs_ref[at, :] = ref[:, width : width + state]
        cs_ref[at, :] = ref[:, width + state : width + 2 * state]
        steps.append(jnp.dot(ref[:, width + 2 * state :], take, preferred_element_type=F32))
    own, other = steps
    raw = jnp.concatenate([jnp.where(y == 0, own, other), jnp.where(y == 0, other, own)], axis=0)
    raw = raw + bias_ref[...]
    dt = jnp.maximum(raw, 0.0) + jnp.log1p(jnp.exp(-jnp.abs(raw)))
    la = -jnp.exp(alog_ref[...]) * dt
    length = 2 * tokens
    lower = (iota((length, length), 0) >= iota((length, length), 1)).astype(F32)
    cum = jnp.dot(lower, la, precision=HIGH)
    last = cum[length - 1 : length, :]
    scal_ref[:, :heads] = cum
    scal_ref[:, heads : 2 * heads] = dt
    weights = jnp.exp(last - cum) * dt
    scaled = (xs_ref[...].astype(F32) * spread(weights, CHANNEL_WIDTH)).astype(BF16)
    s = lax.dot_general(bs_ref[...], scaled, TN, preferred_element_type=F32)
    s_ref[:state, :] = s
    send_ref[:state, :] = s.astype(BF16)
    decay = spread(jnp.exp(last), CHANNEL_WIDTH)
    s_ref[state:, :] = jnp.broadcast_to(decay, (8, width))
    hi, mid, lo = split3(decay)
    which = iota((16, width), 0)
    parts = jnp.where(which == 0, hi.astype(F32), jnp.where(which == 1, mid.astype(F32), lo.astype(F32)))
    send_ref[state:, :] = jnp.where(which < 3, parts, 0.0).astype(BF16)


def local_state(y, own, pk, bias, alog, heads):
    tokens, width, state = own.shape[0], heads * CHANNEL_WIDTH, STATE
    whole = lambda a: pl.BlockSpec(a.shape, lambda i, y: (0,) * a.ndim)
    outs = [
        jax.ShapeDtypeStruct((2 * tokens, width), BF16),
        jax.ShapeDtypeStruct((2 * tokens, state), BF16),
        jax.ShapeDtypeStruct((2 * tokens, state), BF16),
        jax.ShapeDtypeStruct((2 * tokens, 2 * heads), F32),
        jax.ShapeDtypeStruct((state + 16, width), BF16),
        jax.ShapeDtypeStruct((state + 8, width), F32),
    ]
    return pl.pallas_call(
        lambda *refs: local_state_kernel(*refs, heads=heads),
        grid_spec=pltpu.PrefetchScalarGridSpec(
            num_scalar_prefetch=1,
            grid=(1,),
            in_specs=[whole(own), whole(pk), whole(bias), whole(alog)],
            out_specs=[whole(o) for o in outs],
        ),
        out_shape=outs,
        compiler_params=params(1),
        cost_estimate=cost(2e8, 3e6),
        name="local_state",
    )(y, own, pk, bias, alog)


def local_y_kernel(xs_ref, bs_ref, cs_ref, scal_ref, skip_ref, out_ref, *, heads, tokens):
    cum, dt = scal_ref[:, :heads], scal_ref[:, heads : 2 * heads]
    length = 2 * tokens
    eye = (iota((length, length), 0) == iota((length, length), 1)).astype(F32)
    flat = lax.dot_general(scal_ref[...], eye, TN, precision=HIGH)
    cum_row, dt_row = flat[:heads, :], flat[heads : 2 * heads, :]
    mask = iota((tokens, tokens), 0) >= iota((tokens, tokens), 1)
    logits = []
    for k in range(2):
        at = pl.ds(k * tokens, tokens)
        logits.append(lax.dot_general(cs_ref[at, :], bs_ref[at, :], NT, preferred_element_type=F32))
    middle = cum[tokens - 1 : tokens, :]
    weights = jnp.exp(middle - cum[:tokens, :]) * dt[:tokens, :]
    scaled = (xs_ref[:tokens, :].astype(F32) * spread(weights, CHANNEL_WIDTH)).astype(BF16)
    s = lax.dot_general(bs_ref[:tokens, :], scaled, TN, preferred_element_type=F32).astype(BF16)
    carried = jnp.dot(cs_ref[tokens:, :], s, preferred_element_type=F32)
    carried = carried * spread(jnp.exp(cum[tokens:, :] - middle), CHANNEL_WIDTH)
    for k in range(2):
        lo = k * tokens
        for h in range(heads):
            at = h * CHANNEL_WIDTH
            xh = xs_ref[lo : lo + tokens, at : at + CHANNEL_WIDTH]
            diff = cum[lo : lo + tokens, h : h + 1] - cum_row[h : h + 1, lo : lo + tokens]
            mix = jnp.exp(jnp.where(mask, diff, -1e30)) * logits[k] * dt_row[h : h + 1, lo : lo + tokens]
            top = mix.astype(BF16)
            yh = jnp.dot(top, xh, preferred_element_type=F32)
            yh = yh + jnp.dot((mix - top.astype(F32)).astype(BF16), xh, preferred_element_type=F32)
            yh = yh + skip_ref[:, at : at + CHANNEL_WIDTH] * xh.astype(F32)
            if k == 1:
                yh = yh + carried[:, at : at + CHANNEL_WIDTH]
            out_ref[lo : lo + tokens, at : at + CHANNEL_WIDTH] = yh


def local_y(xs, bs, cs, scal, skip, heads):
    length, width = xs.shape
    return pl.pallas_call(
        lambda *refs: local_y_kernel(*refs, heads=heads, tokens=length // 2),
        out_shape=jax.ShapeDtypeStruct((length, width), F32),
        compiler_params=params(),
        cost_estimate=cost(4e8, 4e6),
        name="local_y",
    )(xs, bs, cs, scal, skip)


def join_kernel(send_ref, s_ref, got_ref, out_ref):
    state = out_ref.shape[0]
    out_ref[...] = (s_ref[:state, :] + s_ref[state : state + 1, :] * got_ref[:state, :].astype(F32)).astype(BF16)


def join(send, s, got):
    return pl.pallas_call(
        join_kernel,
        out_shape=jax.ShapeDtypeStruct((STATE, s.shape[1]), BF16),
        compiler_params=params(),
        cost_estimate=cost(1e6, 1.5e6),
        name="join",
    )(send, s, got)


def finish_kernel(y_ref, local_ref, cs_ref, scal_ref, one_ref, two_ref, gate_ref, got_ref, gain_ref, out_ref, *, heads):
    length, width = local_ref.shape
    state, tokens = two_ref.shape[0], length // 2
    y = y_ref[0]
    decay = jnp.sum(one_ref[state:, :].astype(F32), axis=0, keepdims=True)
    start = one_ref[:state, :].astype(F32) + decay * two_ref[...].astype(F32)
    top = start.astype(BF16)
    low = (start - top.astype(F32)).astype(BF16)
    grow = jnp.exp(scal_ref[:, :heads])
    for k in range(2):
        at = pl.ds(k * tokens, tokens)
        carried = jnp.dot(cs_ref[at, :], top, preferred_element_type=F32)
        carried = carried + jnp.dot(cs_ref[at, :], low, preferred_element_type=F32)
        value = local_ref[at, :] + carried * spread(grow[k * tokens : (k + 1) * tokens, :], CHANNEL_WIDTH)
        gate = jnp.where(y == k, gate_ref[...], got_ref[...]).astype(F32)
        value = value * (gate / (1.0 + jnp.exp(-gate)))
        mean = jnp.sum(value * value, axis=1, keepdims=True) / width
        out_ref[at, :] = (value * lax.rsqrt(mean + EPS) * gain_ref[...]).astype(BF16)


def finish(y, local, cs, scal, one, two, gate, got, gain, heads):
    length, width = local.shape
    whole = lambda a: pl.BlockSpec(a.shape, lambda i, y: (0,) * a.ndim)
    return pl.pallas_call(
        lambda *refs: finish_kernel(*refs, heads=heads),
        grid_spec=pltpu.PrefetchScalarGridSpec(
            num_scalar_prefetch=1,
            grid=(1,),
            in_specs=[
                whole(local),
                whole(cs),
                whole(scal),
                whole(one),
                whole(two),
                pl.BlockSpec((length // 2, width), lambda i, y: (0, y[0])),
                whole(got),
                whole(gain),
            ],
            out_specs=pl.BlockSpec((length, width), lambda i, y: (0, 0)),
        ),
        out_shape=jax.ShapeDtypeStruct((length, width), BF16),
        compiler_params=params(1),
        cost_estimate=cost(1e8, 4e6),
        name="finish",
    )(y, local, cs, scal, one, two, gate, got, gain)


def project_kernel(yc_ref, own_ref, *refs):
    *got_refs, first_ref, second_ref, keep_ref, send_ref, both_ref = refs
    tokens, depth = keep_ref.shape[0], own_ref.shape[1]
    core = yc_ref[1]

    @pl.when(pl.program_id(0) == 0)
    def _():
        def fill(lower, upper):
            for k in range(2):
                rows = pl.ds(pl.multiple_of(jnp.where(core == 0, k, 1 - k) * tokens, tokens), tokens)
                both_ref[rows, :depth] = own_ref[k * tokens : (k + 1) * tokens, :]
                both_ref[rows, depth:] = (lower, upper)[k]()

        whole = got_refs[0]
        halves = lambda: fill(lambda: whole[:tokens, :], lambda: whole[tokens:, :])
        if len(got_refs) == 1:
            halves()
        else:
            pl.when(yc_ref[2] == 1)(halves)
            pl.when(yc_ref[2] == 0)(lambda: fill(lambda: got_refs[1][...], lambda: got_refs[2][...]))

    part = jnp.dot(both_ref[:, :depth], first_ref[...], preferred_element_type=F32)
    part = part + jnp.dot(both_ref[:, depth:], second_ref[...], preferred_element_type=F32)
    keep_ref[...] = part[:tokens, :]
    send_ref[...] = part[tokens:, :].astype(BF16)


def project(yc, own, got, w):
    length, depth = own.shape
    tokens, cols = length // 2, w.shape[1]
    tile = min(cols, 256)
    whole = lambda a: pl.BlockSpec(a.shape, lambda i, yc: (0, 0))
    return pl.pallas_call(
        project_kernel,
        grid_spec=pltpu.PrefetchScalarGridSpec(
            num_scalar_prefetch=1,
            grid=(cols // tile,),
            in_specs=[whole(own)]
            + [whole(v) for v in got]
            + [
                pl.BlockSpec((depth, tile), lambda i, yc: (yc[0], i)),
                pl.BlockSpec((depth, tile), lambda i, yc: (1 - yc[0], i)),
            ],
            out_specs=[
                pl.BlockSpec((tokens, tile), lambda i, yc: (0, i)),
                pl.BlockSpec((tokens, tile), lambda i, yc: (0, i)),
            ],
            scratch_shapes=[pltpu.VMEM((length, 2 * depth), BF16)],
        ),
        out_shape=[jax.ShapeDtypeStruct((tokens, cols), F32), jax.ShapeDtypeStruct((tokens, cols), BF16)],
        compiler_params=params(1),
        cost_estimate=cost(4.0 * length * depth * cols, 6e6),
        name="project",
    )(yc, own, *got, w, w)


def place_kernel(at_ref, mine_ref, got_ref, out_ref):
    cols = got_ref.shape[1]
    part = at_ref[0]
    out_ref[:, pl.ds(pl.multiple_of(part * cols, cols), cols)] = mine_ref[...]
    out_ref[:, pl.ds(pl.multiple_of((1 - part) * cols, cols), cols)] = got_ref[...]


def place(at, mine, got):
    tokens, cols = got.shape
    whole = pl.BlockSpec((tokens, cols), lambda i, at: (0, 0))
    return pl.pallas_call(
        place_kernel,
        grid_spec=pltpu.PrefetchScalarGridSpec(
            num_scalar_prefetch=1,
            grid=(1,),
            in_specs=[whole, whole],
            out_specs=pl.BlockSpec((tokens, 2 * cols), lambda i, at: (0, 0)),
        ),
        out_shape=jax.ShapeDtypeStruct((tokens, 2 * cols), BF16),
        compiler_params=params(1),
        cost_estimate=cost(1e6, 2e6),
        name="place",
    )(at, mine, got)


def pair_shards(nz, x_in, gate, b_proj, c_proj, dt_raw, dt_bias, a_log, skip_d, norm_gain, w_out):
    tokens = x_in.shape[0]
    heads = dt_raw.shape[1] // 2
    width = heads * CHANNEL_WIDTH
    seq, grp = lax.axis_index("seq"), lax.axis_index("grp")
    z, y = seq // 2, seq % 2
    yv = y.astype(jnp.int32).reshape(1)
    dt_raw = dt_raw.T
    both = ("seq", "grp")
    core = grp % 2
    spots = [(a, b, c, d) for a in range(nz) for b in range(2) for c in range(nz // 2) for d in range(2)]
    flat = lambda a, b, c, d: ((a * 2 + b) * (nz // 2) + c) * 2 + d
    tie = lax.optimization_barrier

    def half(v, axis, which):
        n = v.shape[axis] // 2
        return lax.dynamic_slice_in_dim(v, which * n, n, axis)

    flip = [(s, s ^ 1) for s in range(2 * nz)]
    sibling = [(g, g ^ 1) for g in range(nz)]
    def along(v, step, senders):
        pairs = [(a * 2 + b, (a + step) * 2 + b) for a in senders for b in range(2)]
        return lax.ppermute(v, "seq", pairs)

    own, packed = pack(yv, x_in, b_proj, c_proj, dt_raw, heads)
    got = lax.ppermute(packed, "seq", flip)
    gate_half = half(gate, 1, 1 - y)
    bias, alog = half(dt_bias, 0, y)[None, :], half(a_log, 0, y)[None, :]
    skip = jnp.repeat(half(skip_d, 0, y), CHANNEL_WIDTH)[None, :]
    gain = half(norm_gain, 0, y)[None, :]
    got_gate = lax.ppermute(gate_half, "seq", flip)
    got, bias, alog, skip, gain = tie((got, bias, alog, skip, gain))

    xs, bs, cs, scal, send, s = local_state(yv, own, got, bias, alog, heads)
    one = along(send, 1, range(nz - 1))
    base = local_y(xs, bs, cs, scal, skip, heads)
    one, base = tie((one, base))

    two = along(join(send, s, one), 2, range(nz - 2))
    block = finish(yv, base, cs, scal, one, two, gate, got_gate, gain, heads)

    hop = lambda value, *moves: lax.ppermute(value, "seq", [(i * 2 + b, j * 2 + b) for i, j in moves for b in range(2)])
    inner = (z == 1) | (z == 2)
    yc = jnp.stack([y, core, inner]).astype(jnp.int32)
    across = lambda value: lax.ppermute(value, "seq", flip)
    cross = lambda value: lax.ppermute(value, "grp", sibling)

    def reduce_core(full, rounded):
        return (full + cross(rounded).astype(F32)).astype(BF16)

    def deliver(slot, near, distant):
        near_x, total = grp // 2 == z // 2, 0.0
        for turn in range(2):
            pairs = []
            for a, b, c, d in spots:
                at = slot if c ^ turn == a // 2 else slot + 2
                pairs.append((flat(a, b, c, d), flat(a ^ at, d, a // 2, b)))
            value = jnp.where(near_x, near, distant) if turn == 0 else jnp.where(near_x, distant, near)
            moved = lax.ppermute(value, both, [(i, j) for i, j in pairs if i != j])
            if any(i == j for i, j in pairs):
                moved = jnp.where(near_x & (y == core), near, moved)
            total = total + moved.astype(F32)
        return total

    slot1 = hop(block, (0, 1), (1, 0), (2, 3), (3, 2))
    middle = hop(block, (1, 2), (2, 1))
    other0 = across(block)
    inward, outward = hop(slot1, (1, 2), (2, 1)), hop(middle, (1, 0), (2, 3))
    other1 = across(slot1)
    a0 = project(yc, block, [other0], w_out)
    inward, outward, other1, a0 = tie((inward, outward, other1, a0))
    last = hop(inward, (1, 0), (2, 3))
    slot2 = jnp.where(inner, inward, outward)
    other2 = across(slot2)
    a1 = project(yc, slot1, [other1], w_out)
    b0 = reduce_core(*a0)
    inner3 = hop(other0, (1, 2), (2, 1))
    last, other2, inner3, a1, b0 = tie((last, other2, inner3, a1, b0))
    slot3 = jnp.where(inner, middle, last)
    lower3 = lax.ppermute(last[:tokens], "seq", [(i * 2 + b, i * 2 + 1 - b) for i in (0, 3) for b in range(2)])
    upper3 = hop(other2[tokens:], (1, 0), (2, 3))
    b1 = reduce_core(*a1)
    a2 = project(yc, slot2, [other2], w_out)
    lower3, upper3, a2, b1 = tie((lower3, upper3, a2, b1))
    b2 = reduce_core(*a2)
    b3 = reduce_core(*project(yc, slot3, [inner3, lower3, upper3], w_out))
    even = deliver(0, b0, b2)
    b3, = tie((b3,))
    odd = deliver(1, b1, b3)
    here = core == z % 2
    mine, theirs = jnp.where(here, even, odd), jnp.where(here, odd, even)
    return place(core.astype(jnp.int32).reshape(1), mine.astype(BF16), cross(theirs.astype(BF16)))


def prefix(array, axis, combine, identity):
    length, mine = (lax.axis_size(axis), lax.axis_index(axis))
    everything = jax.tree.map(lambda part: lax.all_gather(part, axis), array)
    start = jax.tree.map(
        lambda part, zero: jnp.broadcast_to(jnp.asarray(zero, part.dtype), part.shape),
        array,
        identity,
    )

    def turn(k, before):
        reached = k < mine
        new = combine(before, jax.tree.map(lambda part: part[k], everything))
        return jax.tree.map(lambda a, b: jnp.where(reached, a, b), new, before)

    return lax.fori_loop(0, length, turn, start)


def ssd_blocks(xf, dt, la, bm, cm, braw, craw, init):
    length, heads, width = xf.shape
    groups = bm.shape[1]
    ratio = heads // groups
    block = math.gcd(length, 256)
    count = length // block

    def step(state, blk):
        xb, dtb, lab, bb, cb, bnar, cnar = blk
        cum = jnp.cumsum(lab, axis=0)
        attention_logits = jnp.einsum("tgn,sgn->gts", cnar, bnar, preferred_element_type=F32)
        attention_logits = jnp.repeat(attention_logits, ratio, axis=0)
        diff = cum.T[:, :, None] - cum.T[:, None, :]
        rows = lax.broadcasted_iota(jnp.int32, (block, block), 0)
        cols = lax.broadcasted_iota(jnp.int32, (block, block), 1)
        mask = (rows >= cols)[None, :, :]
        decay = jnp.exp(jnp.where(mask, diff, -1e30))
        mixing = decay * attention_logits * dtb.T[:, None, :]
        outs = jnp.einsum("hts,shp->thp", mixing, xb, precision=HIGH)
        cheads = jnp.repeat(cb, ratio, axis=1)
        bheads = jnp.repeat(bb, ratio, axis=1)
        outs = outs + jnp.exp(cum)[:, :, None] * jnp.einsum("thn,hpn->thp", cheads, state, precision=HIGH)
        weights = jnp.exp(cum[-1][None, :] - cum) * dtb
        fresh = jnp.einsum("sh,shp,shn->hpn", weights, xb, bheads, precision=HIGH)
        state = jnp.exp(cum[-1])[:, None, None] * state + fresh
        return (state, outs)

    cut = lambda v: v.reshape((count, block) + v.shape[1:])
    final, outs = lax.scan(step, init, jax.tree.map(cut, (xf, dt, la, bm, cm, braw, craw)))
    return (outs.reshape(length, heads, width), final, jnp.sum(la, axis=0))


def gated_norm_output(y, multiplier_channels, norm_gain, groups):
    length = y.shape[0]
    gated = y.reshape(length, -1) * jax.nn.silu(multiplier_channels.astype(F32))
    split = gated.reshape(length, groups, -1)
    split = split * lax.rsqrt(jnp.mean(split * split, axis=-1, keepdims=True) + EPS)
    return (split.reshape(length, -1) * norm_gain).astype(BF16)


def combine_states(earlier_state, later):
    return (earlier_state[0] * later[0], later[0][:, None, None] * earlier_state[1] + later[1])


def general_shards(x_in, gate, b_proj, c_proj, dt_raw, dt_bias, a_log, skip_d, norm_gain, w_out):
    length = x_in.shape[0]
    heads = dt_raw.shape[1]
    groups = b_proj.shape[1] // STATE
    xf = x_in.astype(F32).reshape(length, heads, CHANNEL_WIDTH)
    dt = jax.nn.softplus(dt_raw + dt_bias)
    la = -jnp.exp(a_log) * dt
    braw = b_proj.reshape(length, groups, STATE)
    craw = c_proj.reshape(length, groups, STATE)
    bm = braw.astype(F32)
    cm = craw.astype(F32)
    empty = jnp.zeros((heads, CHANNEL_WIDTH, STATE), F32)
    y, local_end, total = ssd_blocks(xf, dt, la, bm, cm, braw, craw, empty)
    identity = (jnp.ones((heads,), F32), empty)
    carried = prefix((jnp.exp(total), local_end), "seq", combine_states, identity)
    cum = jnp.cumsum(la, axis=0)
    cheads = jnp.repeat(cm, heads // groups, axis=1)
    y = y + jnp.exp(cum)[:, :, None] * jnp.einsum("thn,hpn->thp", cheads, carried[1], precision=HIGH)
    y = y + skip_d[None, :, None] * xf
    normed = gated_norm_output(y, gate, norm_gain, groups)
    partial_out = jnp.dot(
        normed, lax.all_gather(w_out, "seq", axis=1, tiled=True), preferred_element_type=F32
    )
    return lax.psum_scatter(partial_out, "grp", scatter_dimension=1, tiled=True).astype(BF16)


def solution(mesh):
    seq, grp = mesh.shape["seq"], mesh.shape["grp"]

    def shards(*args):
        groups = args[2].shape[1] // STATE
        if grp == 4 and seq == 2 * grp and groups == 2:
            return pair_shards(grp, *args)
        return general_shards(*args)

    return jax.shard_map(
        shards,
        mesh=mesh,
        in_specs=(
            P("seq", "grp"),
            P("seq", "grp"),
            P("seq", "grp"),
            P("seq", "grp"),
            P("seq", "grp"),
            P("grp"),
            P("grp"),
            P("grp"),
            P("grp"),
            P("grp", "seq"),
        ),
        out_specs=P("seq", "grp"),
        check_vma=False,
    )
```

```python
import math

import jax
import jax.numpy as jnp
from jax import lax
from jax.experimental import pallas as pl
from jax.experimental.pallas import tpu as pltpu
from jax.sharding import PartitionSpec as P

CHANNEL_WIDTH = 128
STATE = 128
EPS = 1e-05

HIGH = lax.Precision.HIGHEST
F32 = jnp.float32
BF16 = jnp.bfloat16
NT = (((1,), (1,)), ((), ()))
TN = (((0,), (0,)), ((), ()))
VMEM_LIMIT = 24 * 2**20


def params(grid_dims=0, limit=VMEM_LIMIT):
    return pltpu.CompilerParams(
        vmem_limit_bytes=limit,
        dimension_semantics=("arbitrary",) * grid_dims if grid_dims else None,
    )


def cost(flops, moved):
    return pl.CostEstimate(flops=1, bytes_accessed=1, transcendentals=0)


def iota(shape, axis):
    return lax.broadcasted_iota(jnp.int32, shape, axis)


def spread(values, width):
    heads = values.shape[1]
    return jnp.concatenate(
        [jnp.broadcast_to(values[:, h : h + 1], (values.shape[0], width)) for h in range(heads)], axis=1
    )


def split3(value):
    hi = value.astype(BF16)
    rest = value - hi.astype(F32)
    mid = rest.astype(BF16)
    return hi, mid, (rest - mid.astype(F32)).astype(BF16)


def pack_kernel(group_ref, x_ref, b_ref, c_ref, dt_ref, out_ref, *, heads):
    width, state = x_ref.shape[1], b_ref.shape[1]
    out_ref[:, :width] = x_ref[...]
    out_ref[:, width : width + state] = b_ref[...]
    out_ref[:, width + state : width + 2 * state] = c_ref[...]
    group = group_ref[0]
    rows, cols = iota((2 * heads, 128), 0), iota((2 * heads, 128), 1)
    total = jnp.zeros((x_ref.shape[0], 128), F32)
    for part, value in enumerate(split3(dt_ref[...])):
        where = (cols == rows - group * heads + part * heads) & (rows // heads == group)
        total = total + lax.dot_general(value, where.astype(BF16), TN, preferred_element_type=F32)
    out_ref[:, width + 2 * state :] = total.astype(BF16)


def pack(group, x, b, c, dt, heads, limit):
    tokens, width, state = x.shape[0], heads * CHANNEL_WIDTH, STATE
    out = jax.ShapeDtypeStruct((tokens, width + 2 * state + 128), BF16)
    return pl.pallas_call(
        lambda *refs: pack_kernel(*refs, heads=heads),
        grid_spec=pltpu.PrefetchScalarGridSpec(
            num_scalar_prefetch=1,
            grid=(1,),
            in_specs=[
                pl.BlockSpec((tokens, width), lambda i, g: (0, g[0])),
                pl.BlockSpec((tokens, state), lambda i, g: (0, g[0])),
                pl.BlockSpec((tokens, state), lambda i, g: (0, g[0])),
                pl.BlockSpec(dt.shape, lambda i, g: (0, 0)),
            ],
            out_specs=pl.BlockSpec(out.shape, lambda i, g: (0, 0)),
        ),
        out_shape=out,
        compiler_params=params(1, limit),
        cost_estimate=cost(1e6, 1e6),
        name="pack",
    )(group, x, b, c, dt)


def local_state_kernel(
    y_ref, own_ref, pk_ref, bias_ref, alog_ref, xs_ref, bs_ref, cs_ref, scal_ref, send_ref, s_ref, *, heads,
):
    tokens = own_ref.shape[0]
    width, state = xs_ref.shape[1], bs_ref.shape[1]
    y = y_ref[0]
    rows, cols = iota((128, heads), 0), iota((128, heads), 1)
    take = ((rows % heads == cols) & (rows < 3 * heads)).astype(BF16)
    steps = []
    for ref, place in ((own_ref, y), (pk_ref, 1 - y)):
        at = pl.ds(pl.multiple_of(place * tokens, tokens), tokens)
        xs_ref[at, :] = ref[:, :width]
        bs_ref[at, :] = ref[:, width : width + state]
        cs_ref[at, :] = ref[:, width + state : width + 2 * state]
        steps.append(jnp.dot(ref[:, width + 2 * state :], take, preferred_element_type=F32))
    own, other = steps
    raw = jnp.concatenate([jnp.where(y == 0, own, other), jnp.where(y == 0, other, own)], axis=0)
    raw = raw + bias_ref[...]
    dt = jnp.maximum(raw, 0.0) + jnp.log1p(jnp.exp(-jnp.abs(raw)))
    la = -jnp.exp(alog_ref[...]) * dt
    length = 2 * tokens
    lower = (iota((length, length), 0) >= iota((length, length), 1)).astype(F32)
    cum = jnp.dot(lower, la, precision=HIGH)
    last = cum[length - 1 : length, :]
    scal_ref[:, :heads] = cum
    scal_ref[:, heads : 2 * heads] = dt
    weights = jnp.exp(last - cum) * dt
    scaled = (xs_ref[...].astype(F32) * spread(weights, CHANNEL_WIDTH)).astype(BF16)
    s = lax.dot_general(bs_ref[...], scaled, TN, preferred_element_type=F32)
    s_ref[:state, :] = s
    send_ref[:state, :] = s.astype(BF16)
    decay = spread(jnp.exp(last), CHANNEL_WIDTH)
    s_ref[state:, :] = jnp.broadcast_to(decay, (8, width))
    hi, mid, lo = split3(decay)
    which = iota((16, width), 0)
    parts = jnp.where(which == 0, hi.astype(F32), jnp.where(which == 1, mid.astype(F32), lo.astype(F32)))
    send_ref[state:, :] = jnp.where(which < 3, parts, 0.0).astype(BF16)


def local_state(y, own, pk, bias, alog, heads):
    tokens, width, state = own.shape[0], heads * CHANNEL_WIDTH, STATE
    whole = lambda a: pl.BlockSpec(a.shape, lambda i, y: (0,) * a.ndim)
    outs = [
        jax.ShapeDtypeStruct((2 * tokens, width), BF16),
        jax.ShapeDtypeStruct((2 * tokens, state), BF16),
        jax.ShapeDtypeStruct((2 * tokens, state), BF16),
        jax.ShapeDtypeStruct((2 * tokens, 2 * heads), F32),
        jax.ShapeDtypeStruct((state + 16, width), BF16),
        jax.ShapeDtypeStruct((state + 8, width), F32),
    ]
    return pl.pallas_call(
        lambda *refs: local_state_kernel(*refs, heads=heads),
        grid_spec=pltpu.PrefetchScalarGridSpec(
            num_scalar_prefetch=1,
            grid=(1,),
            in_specs=[whole(own), whole(pk), whole(bias), whole(alog)],
            out_specs=[whole(o) for o in outs],
        ),
        out_shape=outs,
        compiler_params=params(1),
        cost_estimate=cost(2e8, 3e6),
        name="local_state",
    )(y, own, pk, bias, alog)


def local_y_kernel(xs_ref, bs_ref, cs_ref, scal_ref, skip_ref, out_ref, *, heads, tokens):
    cum, dt = scal_ref[:, :heads], scal_ref[:, heads : 2 * heads]
    length = 2 * tokens
    eye = (iota((length, length), 0) == iota((length, length), 1)).astype(F32)
    flat = lax.dot_general(scal_ref[...], eye, TN, precision=HIGH)
    cum_row, dt_row = flat[:heads, :], flat[heads : 2 * heads, :]
    mask = iota((tokens, tokens), 0) >= iota((tokens, tokens), 1)
    logits = []
    for k in range(2):
        at = pl.ds(k * tokens, tokens)
        logits.append(lax.dot_general(cs_ref[at, :], bs_ref[at, :], NT, preferred_element_type=F32))
    middle = cum[tokens - 1 : tokens, :]
    weights = jnp.exp(middle - cum[:tokens, :]) * dt[:tokens, :]
    scaled = (xs_ref[:tokens, :].astype(F32) * spread(weights, CHANNEL_WIDTH)).astype(BF16)
    s = lax.dot_general(bs_ref[:tokens, :], scaled, TN, preferred_element_type=F32).astype(BF16)
    carried = jnp.dot(cs_ref[tokens:, :], s, preferred_element_type=F32)
    carried = carried * spread(jnp.exp(cum[tokens:, :] - middle), CHANNEL_WIDTH)
    for k in range(2):
        lo = k * tokens
        for h in range(heads):
            at = h * CHANNEL_WIDTH
            xh = xs_ref[lo : lo + tokens, at : at + CHANNEL_WIDTH]
            diff = cum[lo : lo + tokens, h : h + 1] - cum_row[h : h + 1, lo : lo + tokens]
            mix = jnp.exp(jnp.where(mask, diff, -1e30)) * logits[k] * dt_row[h : h + 1, lo : lo + tokens]
            top = mix.astype(BF16)
            yh = jnp.dot(top, xh, preferred_element_type=F32)
            yh = yh + jnp.dot((mix - top.astype(F32)).astype(BF16), xh, preferred_element_type=F32)
            yh = yh + skip_ref[:, at : at + CHANNEL_WIDTH] * xh.astype(F32)
            if k == 1:
                yh = yh + carried[:, at : at + CHANNEL_WIDTH]
            out_ref[lo : lo + tokens, at : at + CHANNEL_WIDTH] = yh


def local_y(xs, bs, cs, scal, skip, heads):
    length, width = xs.shape
    return pl.pallas_call(
        lambda *refs: local_y_kernel(*refs, heads=heads, tokens=length // 2),
        out_shape=jax.ShapeDtypeStruct((length, width), F32),
        compiler_params=params(),
        cost_estimate=cost(4e8, 4e6),
        name="local_y",
    )(xs, bs, cs, scal, skip)


def join_kernel(send_ref, s_ref, got_ref, out_ref):
    state = out_ref.shape[0]
    out_ref[...] = (s_ref[:state, :] + s_ref[state : state + 1, :] * got_ref[:state, :].astype(F32)).astype(BF16)


def join(send, s, got):
    return pl.pallas_call(
        join_kernel,
        out_shape=jax.ShapeDtypeStruct((STATE, s.shape[1]), BF16),
        compiler_params=params(),
        cost_estimate=cost(1e6, 1.5e6),
        name="join",
    )(send, s, got)


def finish_kernel(y_ref, local_ref, cs_ref, scal_ref, one_ref, two_ref, gate_ref, got_ref, gain_ref, out_ref, *, heads):
    length, width = local_ref.shape
    state, tokens = two_ref.shape[0], length // 2
    y = y_ref[0]
    decay = jnp.sum(one_ref[state:, :].astype(F32), axis=0, keepdims=True)
    start = one_ref[:state, :].astype(F32) + decay * two_ref[...].astype(F32)
    top = start.astype(BF16)
    low = (start - top.astype(F32)).astype(BF16)
    grow = jnp.exp(scal_ref[:, :heads])
    for k in range(2):
        at = pl.ds(k * tokens, tokens)
        carried = jnp.dot(cs_ref[at, :], top, preferred_element_type=F32)
        carried = carried + jnp.dot(cs_ref[at, :], low, preferred_element_type=F32)
        value = local_ref[at, :] + carried * spread(grow[k * tokens : (k + 1) * tokens, :], CHANNEL_WIDTH)
        gate = jnp.where(y == k, gate_ref[...], got_ref[...]).astype(F32)
        value = value * (gate / (1.0 + jnp.exp(-gate)))
        mean = jnp.sum(value * value, axis=1, keepdims=True) / width
        out_ref[at, :] = (value * lax.rsqrt(mean + EPS) * gain_ref[...]).astype(BF16)


def finish(y, local, cs, scal, one, two, gate, got, gain, heads):
    length, width = local.shape
    whole = lambda a: pl.BlockSpec(a.shape, lambda i, y: (0,) * a.ndim)
    return pl.pallas_call(
        lambda *refs: finish_kernel(*refs, heads=heads),
        grid_spec=pltpu.PrefetchScalarGridSpec(
            num_scalar_prefetch=1,
            grid=(1,),
            in_specs=[
                whole(local),
                whole(cs),
                whole(scal),
                whole(one),
                whole(two),
                pl.BlockSpec((length // 2, width), lambda i, y: (0, y[0])),
                whole(got),
                whole(gain),
            ],
            out_specs=pl.BlockSpec((length, width), lambda i, y: (0, 0)),
        ),
        out_shape=jax.ShapeDtypeStruct((length, width), BF16),
        compiler_params=params(1),
        cost_estimate=cost(1e8, 4e6),
        name="finish",
    )(y, local, cs, scal, one, two, gate, got, gain)


def project_kernel(yc_ref, own_ref, *refs):
    *got_refs, first_ref, second_ref, keep_ref, send_ref, both_ref = refs
    tokens, depth = keep_ref.shape[0], own_ref.shape[1]
    core = yc_ref[1]

    @pl.when(pl.program_id(0) == 0)
    def _():
        def fill(lower, upper):
            for k in range(2):
                rows = pl.ds(pl.multiple_of(jnp.where(core == 0, k, 1 - k) * tokens, tokens), tokens)
                both_ref[rows, :depth] = own_ref[k * tokens : (k + 1) * tokens, :]
                both_ref[rows, depth:] = (lower, upper)[k]()

        whole = got_refs[0]
        halves = lambda: fill(lambda: whole[:tokens, :], lambda: whole[tokens:, :])
        if len(got_refs) == 1:
            halves()
        else:
            pl.when(yc_ref[2] == 1)(halves)
            pl.when(yc_ref[2] == 0)(lambda: fill(lambda: got_refs[1][...], lambda: got_refs[2][...]))

    part = jnp.dot(both_ref[:, :depth], first_ref[...], preferred_element_type=F32)
    part = part + jnp.dot(both_ref[:, depth:], second_ref[...], preferred_element_type=F32)
    keep_ref[...] = part[:tokens, :]
    send_ref[...] = part[tokens:, :].astype(BF16)


def project(yc, own, got, w):
    length, depth = own.shape
    tokens, cols = length // 2, w.shape[1]
    tile = min(cols, 256)
    whole = lambda a: pl.BlockSpec(a.shape, lambda i, yc: (0, 0))
    return pl.pallas_call(
        project_kernel,
        grid_spec=pltpu.PrefetchScalarGridSpec(
            num_scalar_prefetch=1,
            grid=(cols // tile,),
            in_specs=[whole(own)]
            + [whole(v) for v in got]
            + [
                pl.BlockSpec((depth, tile), lambda i, yc: (yc[0], i)),
                pl.BlockSpec((depth, tile), lambda i, yc: (1 - yc[0], i)),
            ],
            out_specs=[
                pl.BlockSpec((tokens, tile), lambda i, yc: (0, i)),
                pl.BlockSpec((tokens, tile), lambda i, yc: (0, i)),
            ],
            scratch_shapes=[pltpu.VMEM((length, 2 * depth), BF16)],
        ),
        out_shape=[jax.ShapeDtypeStruct((tokens, cols), F32), jax.ShapeDtypeStruct((tokens, cols), BF16)],
        compiler_params=params(1),
        cost_estimate=cost(4.0 * length * depth * cols, 6e6),
        name="project",
    )(yc, own, *got, w, w)


def place_kernel(at_ref, mine_ref, got_ref, out_ref):
    cols = got_ref.shape[1]
    part = at_ref[0]
    out_ref[:, pl.ds(pl.multiple_of(part * cols, cols), cols)] = mine_ref[...]
    out_ref[:, pl.ds(pl.multiple_of((1 - part) * cols, cols), cols)] = got_ref[...]


def place(at, mine, got):
    tokens, cols = got.shape
    whole = pl.BlockSpec((tokens, cols), lambda i, at: (0, 0))
    return pl.pallas_call(
        place_kernel,
        grid_spec=pltpu.PrefetchScalarGridSpec(
            num_scalar_prefetch=1,
            grid=(1,),
            in_specs=[whole, whole],
            out_specs=pl.BlockSpec((tokens, 2 * cols), lambda i, at: (0, 0)),
        ),
        out_shape=jax.ShapeDtypeStruct((tokens, 2 * cols), BF16),
        compiler_params=params(1),
        cost_estimate=cost(1e6, 2e6),
        name="place",
    )(at, mine, got)


def pair_shards(nz, x_in, gate, b_proj, c_proj, dt_raw, dt_bias, a_log, skip_d, norm_gain, w_out):
    tokens = x_in.shape[0]
    heads = dt_raw.shape[1] // 2
    width = heads * CHANNEL_WIDTH
    seq, grp = lax.axis_index("seq"), lax.axis_index("grp")
    z, y = seq // 2, seq % 2
    yv = y.astype(jnp.int32).reshape(1)
    dt_raw = dt_raw.T
    both = ("seq", "grp")
    core = grp % 2
    spots = [(a, b, c, d) for a in range(nz) for b in range(2) for c in range(nz // 2) for d in range(2)]
    flat = lambda a, b, c, d: ((a * 2 + b) * (nz // 2) + c) * 2 + d
    tie = lax.optimization_barrier

    def half(v, axis, which):
        n = v.shape[axis] // 2
        return lax.dynamic_slice_in_dim(v, which * n, n, axis)

    flip = [(s, s ^ 1) for s in range(2 * nz)]
    sibling = [(g, g ^ 1) for g in range(nz)]
    def along(v, step, senders):
        pairs = [(a * 2 + b, (a + step) * 2 + b) for a in senders for b in range(2)]
        return lax.ppermute(v, "seq", pairs)

    got = lax.ppermute(pack(1 - yv, x_in, b_proj, c_proj, dt_raw, heads, 60 * 2**20), "seq", flip)
    own = pack(yv, x_in, b_proj, c_proj, dt_raw, heads, VMEM_LIMIT)
    gate_half = half(gate, 1, 1 - y)
    bias, alog = half(dt_bias, 0, y)[None, :], half(a_log, 0, y)[None, :]
    skip = jnp.repeat(half(skip_d, 0, y), CHANNEL_WIDTH)[None, :]
    gain = half(norm_gain, 0, y)[None, :]
    got_gate = lax.ppermute(gate_half, "seq", flip)
    got, own, bias, alog, skip, gain = tie((got, own, bias, alog, skip, gain))

    xs, bs, cs, scal, send, s = local_state(yv, own, got, bias, alog, heads)
    one = along(send, 1, range(nz - 1))
    base = local_y(xs, bs, cs, scal, skip, heads)
    one, base = tie((one, base))

    two = along(join(send, s, one), 2, range(nz - 2))
    block = finish(yv, base, cs, scal, one, two, gate, got_gate, gain, heads)

    hop = lambda value, *moves: lax.ppermute(value, "seq", [(i * 2 + b, j * 2 + b) for i, j in moves for b in range(2)])
    inner = (z == 1) | (z == 2)
    yc = jnp.stack([y, core, inner]).astype(jnp.int32)
    across = lambda value: lax.ppermute(value, "seq", flip)
    cross = lambda value: lax.ppermute(value, "grp", sibling)

    def reduce_core(full, rounded):
        return (full + cross(rounded).astype(F32)).astype(BF16)

    def deliver(slot, near, distant):
        near_x, total = grp // 2 == z // 2, 0.0
        for turn in range(2):
            pairs = []
            for a, b, c, d in spots:
                at = slot if c ^ turn == a // 2 else slot + 2
                pairs.append((flat(a, b, c, d), flat(a ^ at, d, a // 2, b)))
            value = jnp.where(near_x, near, distant) if turn == 0 else jnp.where(near_x, distant, near)
            moved = lax.ppermute(value, both, [(i, j) for i, j in pairs if i != j])
            if any(i == j for i, j in pairs):
                moved = jnp.where(near_x & (y == core), near, moved)
            total = total + moved.astype(F32)
        return total

    slot1 = hop(block, (0, 1), (1, 0), (2, 3), (3, 2))
    middle = hop(block, (1, 2), (2, 1))
    other0 = across(block)
    inward, outward = hop(slot1, (1, 2), (2, 1)), hop(middle, (1, 0), (2, 3))
    other1 = across(slot1)
    a0 = project(yc, block, [other0], w_out)
    inward, outward, a0 = tie((inward, outward, a0))
    last = hop(inward, (1, 0), (2, 3))
    slot2 = jnp.where(inner, inward, outward)
    other2 = across(slot2)
    a1 = project(yc, slot1, [other1], w_out)
    b0 = reduce_core(*a0)
    inner3 = hop(other0, (1, 2), (2, 1))
    last, inner3, a1, b0 = tie((last, inner3, a1, b0))
    slot3 = jnp.where(inner, middle, last)
    lower3 = lax.ppermute(last[:tokens], "seq", [(i * 2 + b, i * 2 + 1 - b) for i in (0, 3) for b in range(2)])
    upper3 = hop(other2[tokens:], (1, 0), (2, 3))
    b1 = reduce_core(*a1)
    a2 = project(yc, slot2, [other2], w_out)
    lower3, upper3, a2, b1 = tie((lower3, upper3, a2, b1))
    b2 = reduce_core(*a2)
    b3 = reduce_core(*project(yc, slot3, [inner3, lower3, upper3], w_out))
    even = deliver(0, b0, b2)
    b3, = tie((b3,))
    odd = deliver(1, b1, b3)
    here = core == z % 2
    mine, theirs = jnp.where(here, even, odd), jnp.where(here, odd, even)
    return place(core.astype(jnp.int32).reshape(1), mine.astype(BF16), cross(theirs.astype(BF16)))


def prefix(array, axis, combine, identity):
    length, mine = (lax.axis_size(axis), lax.axis_index(axis))
    everything = jax.tree.map(lambda part: lax.all_gather(part, axis), array)
    start = jax.tree.map(
        lambda part, zero: jnp.broadcast_to(jnp.asarray(zero, part.dtype), part.shape),
        array,
        identity,
    )

    def turn(k, before):
        reached = k < mine
        new = combine(before, jax.tree.map(lambda part: part[k], everything))
        return jax.tree.map(lambda a, b: jnp.where(reached, a, b), new, before)

    return lax.fori_loop(0, length, turn, start)


def ssd_blocks(xf, dt, la, bm, cm, braw, craw, init):
    length, heads, width = xf.shape
    groups = bm.shape[1]
    ratio = heads // groups
    block = math.gcd(length, 256)
    count = length // block

    def step(state, blk):
        xb, dtb, lab, bb, cb, bnar, cnar = blk
        cum = jnp.cumsum(lab, axis=0)
        attention_logits = jnp.einsum("tgn,sgn->gts", cnar, bnar, preferred_element_type=F32)
        attention_logits = jnp.repeat(attention_logits, ratio, axis=0)
        diff = cum.T[:, :, None] - cum.T[:, None, :]
        rows = lax.broadcasted_iota(jnp.int32, (block, block), 0)
        cols = lax.broadcasted_iota(jnp.int32, (block, block), 1)
        mask = (rows >= cols)[None, :, :]
        decay = jnp.exp(jnp.where(mask, diff, -1e30))
        mixing = decay * attention_logits * dtb.T[:, None, :]
        outs = jnp.einsum("hts,shp->thp", mixing, xb, precision=HIGH)
        cheads = jnp.repeat(cb, ratio, axis=1)
        bheads = jnp.repeat(bb, ratio, axis=1)
        outs = outs + jnp.exp(cum)[:, :, None] * jnp.einsum("thn,hpn->thp", cheads, state, precision=HIGH)
        weights = jnp.exp(cum[-1][None, :] - cum) * dtb
        fresh = jnp.einsum("sh,shp,shn->hpn", weights, xb, bheads, precision=HIGH)
        state = jnp.exp(cum[-1])[:, None, None] * state + fresh
        return (state, outs)

    cut = lambda v: v.reshape((count, block) + v.shape[1:])
    final, outs = lax.scan(step, init, jax.tree.map(cut, (xf, dt, la, bm, cm, braw, craw)))
    return (outs.reshape(length, heads, width), final, jnp.sum(la, axis=0))


def gated_norm_output(y, multiplier_channels, norm_gain, groups):
    length = y.shape[0]
    gated = y.reshape(length, -1) * jax.nn.silu(multiplier_channels.astype(F32))
    split = gated.reshape(length, groups, -1)
    split = split * lax.rsqrt(jnp.mean(split * split, axis=-1, keepdims=True) + EPS)
    return (split.reshape(length, -1) * norm_gain).astype(BF16)


def combine_states(earlier_state, later):
    return (earlier_state[0] * later[0], later[0][:, None, None] * earlier_state[1] + later[1])


def general_shards(x_in, gate, b_proj, c_proj, dt_raw, dt_bias, a_log, skip_d, norm_gain, w_out):
    length = x_in.shape[0]
    heads = dt_raw.shape[1]
    groups = b_proj.shape[1] // STATE
    xf = x_in.astype(F32).reshape(length, heads, CHANNEL_WIDTH)
    dt = jax.nn.softplus(dt_raw + dt_bias)
    la = -jnp.exp(a_log) * dt
    braw = b_proj.reshape(length, groups, STATE)
    craw = c_proj.reshape(length, groups, STATE)
    bm = braw.astype(F32)
    cm = craw.astype(F32)
    empty = jnp.zeros((heads, CHANNEL_WIDTH, STATE), F32)
    y, local_end, total = ssd_blocks(xf, dt, la, bm, cm, braw, craw, empty)
    identity = (jnp.ones((heads,), F32), empty)
    carried = prefix((jnp.exp(total), local_end), "seq", combine_states, identity)
    cum = jnp.cumsum(la, axis=0)
    cheads = jnp.repeat(cm, heads // groups, axis=1)
    y = y + jnp.exp(cum)[:, :, None] * jnp.einsum("thn,hpn->thp", cheads, carried[1], precision=HIGH)
    y = y + skip_d[None, :, None] * xf
    normed = gated_norm_output(y, gate, norm_gain, groups)
    partial_out = jnp.dot(
        normed, lax.all_gather(w_out, "seq", axis=1, tiled=True), preferred_element_type=F32
    )
    return lax.psum_scatter(partial_out, "grp", scatter_dimension=1, tiled=True).astype(BF16)


def solution(mesh):
    seq, grp = mesh.shape["seq"], mesh.shape["grp"]

    def shards(*args):
        groups = args[2].shape[1] // STATE
        if grp == 4 and seq == 2 * grp and groups == 2:
            return pair_shards(grp, *args)
        return general_shards(*args)

    return jax.shard_map(
        shards,
        mesh=mesh,
        in_specs=(
            P("seq", "grp"),
            P("seq", "grp"),
            P("seq", "grp"),
            P("seq", "grp"),
            P("seq", "grp"),
            P("grp"),
            P("grp"),
            P("grp"),
            P("grp"),
            P("grp", "seq"),
        ),
        out_specs=P("seq", "grp"),
        check_vma=False,
    )
```

```python
import math

import jax
import jax.numpy as jnp
from jax import lax
from jax.experimental import pallas as pl
from jax.experimental.pallas import tpu as pltpu
from jax.sharding import PartitionSpec as P

CHANNEL_WIDTH = 128
STATE = 128
EPS = 1e-05

HIGH = lax.Precision.HIGHEST
F32 = jnp.float32
BF16 = jnp.bfloat16
NT = (((1,), (1,)), ((), ()))
TN = (((0,), (0,)), ((), ()))
VMEM_LIMIT = 24 * 2**20


def params(grid_dims=0, limit=VMEM_LIMIT):
    return pltpu.CompilerParams(
        vmem_limit_bytes=limit,
        dimension_semantics=("arbitrary",) * grid_dims if grid_dims else None,
    )


def cost(flops, moved):
    return pl.CostEstimate(flops=1, bytes_accessed=1, transcendentals=0)


def iota(shape, axis):
    return lax.broadcasted_iota(jnp.int32, shape, axis)


def spread(values, width):
    heads = values.shape[1]
    return jnp.concatenate(
        [jnp.broadcast_to(values[:, h : h + 1], (values.shape[0], width)) for h in range(heads)], axis=1
    )


def split3(value):
    hi = value.astype(BF16)
    rest = value - hi.astype(F32)
    mid = rest.astype(BF16)
    return hi, mid, (rest - mid.astype(F32)).astype(BF16)


def pack_kernel(group_ref, x_ref, b_ref, c_ref, dt_ref, out_ref, *, heads):
    width, state = x_ref.shape[1], b_ref.shape[1]
    out_ref[:, :width] = x_ref[...]
    out_ref[:, width : width + state] = b_ref[...]
    out_ref[:, width + state : width + 2 * state] = c_ref[...]
    group = group_ref[0]
    rows, cols = iota((2 * heads, 128), 0), iota((2 * heads, 128), 1)
    total = jnp.zeros((x_ref.shape[0], 128), F32)
    for part, value in enumerate(split3(dt_ref[...])):
        where = (cols == rows - group * heads + part * heads) & (rows // heads == group)
        total = total + lax.dot_general(value, where.astype(BF16), TN, preferred_element_type=F32)
    out_ref[:, width + 2 * state :] = total.astype(BF16)


def pack(group, x, b, c, dt, heads, limit):
    tokens, width, state = x.shape[0], heads * CHANNEL_WIDTH, STATE
    out = jax.ShapeDtypeStruct((tokens, width + 2 * state + 128), BF16)
    return pl.pallas_call(
        lambda *refs: pack_kernel(*refs, heads=heads),
        grid_spec=pltpu.PrefetchScalarGridSpec(
            num_scalar_prefetch=1,
            grid=(1,),
            in_specs=[
                pl.BlockSpec((tokens, width), lambda i, g: (0, g[0])),
                pl.BlockSpec((tokens, state), lambda i, g: (0, g[0])),
                pl.BlockSpec((tokens, state), lambda i, g: (0, g[0])),
                pl.BlockSpec(dt.shape, lambda i, g: (0, 0)),
            ],
            out_specs=pl.BlockSpec(out.shape, lambda i, g: (0, 0)),
        ),
        out_shape=out,
        compiler_params=params(1, limit),
        cost_estimate=cost(1e6, 1e6),
        name="pack",
    )(group, x, b, c, dt)


def local_state_kernel(
    y_ref, own_ref, pk_ref, bias_ref, alog_ref, xs_ref, bs_ref, cs_ref, scal_ref, send_ref, s_ref, *, heads,
):
    tokens = own_ref.shape[0]
    width, state = xs_ref.shape[1], bs_ref.shape[1]
    y = y_ref[0]
    rows, cols = iota((128, heads), 0), iota((128, heads), 1)
    take = ((rows % heads == cols) & (rows < 3 * heads)).astype(BF16)
    steps = []
    for ref, place in ((own_ref, y), (pk_ref, 1 - y)):
        at = pl.ds(pl.multiple_of(place * tokens, tokens), tokens)
        xs_ref[at, :] = ref[:, :width]
        bs_ref[at, :] = ref[:, width : width + state]
        cs_ref[at, :] = ref[:, width + state : width + 2 * state]
        steps.append(jnp.dot(ref[:, width + 2 * state :], take, preferred_element_type=F32))
    own, other = steps
    raw = jnp.concatenate([jnp.where(y == 0, own, other), jnp.where(y == 0, other, own)], axis=0)
    raw = raw + bias_ref[...]
    dt = jnp.maximum(raw, 0.0) + jnp.log1p(jnp.exp(-jnp.abs(raw)))
    la = -jnp.exp(alog_ref[...]) * dt
    length = 2 * tokens
    lower = (iota((length, length), 0) >= iota((length, length), 1)).astype(F32)
    cum = jnp.dot(lower, la, precision=HIGH)
    last = cum[length - 1 : length, :]
    scal_ref[:, :heads] = cum
    scal_ref[:, heads : 2 * heads] = dt
    weights = jnp.exp(last - cum) * dt
    scaled = (xs_ref[...].astype(F32) * spread(weights, CHANNEL_WIDTH)).astype(BF16)
    s = lax.dot_general(bs_ref[...], scaled, TN, preferred_element_type=F32)
    s_ref[:state, :] = s
    send_ref[:state, :] = s.astype(BF16)
    decay = spread(jnp.exp(last), CHANNEL_WIDTH)
    s_ref[state:, :] = jnp.broadcast_to(decay, (8, width))
    hi, mid, lo = split3(decay)
    which = iota((16, width), 0)
    parts = jnp.where(which == 0, hi.astype(F32), jnp.where(which == 1, mid.astype(F32), lo.astype(F32)))
    send_ref[state:, :] = jnp.where(which < 3, parts, 0.0).astype(BF16)


def local_state(y, own, pk, bias, alog, heads):
    tokens, width, state = own.shape[0], heads * CHANNEL_WIDTH, STATE
    whole = lambda a: pl.BlockSpec(a.shape, lambda i, y: (0,) * a.ndim)
    outs = [
        jax.ShapeDtypeStruct((2 * tokens, width), BF16),
        jax.ShapeDtypeStruct((2 * tokens, state), BF16),
        jax.ShapeDtypeStruct((2 * tokens, state), BF16),
        jax.ShapeDtypeStruct((2 * tokens, 2 * heads), F32),
        jax.ShapeDtypeStruct((state + 16, width), BF16),
        jax.ShapeDtypeStruct((state + 8, width), F32),
    ]
    return pl.pallas_call(
        lambda *refs: local_state_kernel(*refs, heads=heads),
        grid_spec=pltpu.PrefetchScalarGridSpec(
            num_scalar_prefetch=1,
            grid=(1,),
            in_specs=[whole(own), whole(pk), whole(bias), whole(alog)],
            out_specs=[whole(o) for o in outs],
        ),
        out_shape=outs,
        compiler_params=params(1),
        cost_estimate=cost(2e8, 3e6),
        name="local_state",
    )(y, own, pk, bias, alog)


def local_y_kernel(xs_ref, bs_ref, cs_ref, scal_ref, skip_ref, out_ref, *, heads, tokens):
    cum, dt = scal_ref[:, :heads], scal_ref[:, heads : 2 * heads]
    length = 2 * tokens
    eye = (iota((length, length), 0) == iota((length, length), 1)).astype(F32)
    flat = lax.dot_general(scal_ref[...], eye, TN, precision=HIGH)
    cum_row, dt_row = flat[:heads, :], flat[heads : 2 * heads, :]
    mask = iota((tokens, tokens), 0) >= iota((tokens, tokens), 1)
    logits = []
    for k in range(2):
        at = pl.ds(k * tokens, tokens)
        logits.append(lax.dot_general(cs_ref[at, :], bs_ref[at, :], NT, preferred_element_type=F32))
    middle = cum[tokens - 1 : tokens, :]
    weights = jnp.exp(middle - cum[:tokens, :]) * dt[:tokens, :]
    scaled = (xs_ref[:tokens, :].astype(F32) * spread(weights, CHANNEL_WIDTH)).astype(BF16)
    s = lax.dot_general(bs_ref[:tokens, :], scaled, TN, preferred_element_type=F32).astype(BF16)
    carried = jnp.dot(cs_ref[tokens:, :], s, preferred_element_type=F32)
    carried = carried * spread(jnp.exp(cum[tokens:, :] - middle), CHANNEL_WIDTH)
    for k in range(2):
        lo = k * tokens
        for h in range(heads):
            at = h * CHANNEL_WIDTH
            xh = xs_ref[lo : lo + tokens, at : at + CHANNEL_WIDTH]
            diff = cum[lo : lo + tokens, h : h + 1] - cum_row[h : h + 1, lo : lo + tokens]
            mix = jnp.exp(jnp.where(mask, diff, -1e30)) * logits[k] * dt_row[h : h + 1, lo : lo + tokens]
            top = mix.astype(BF16)
            yh = jnp.dot(top, xh, preferred_element_type=F32)
            yh = yh + jnp.dot((mix - top.astype(F32)).astype(BF16), xh, preferred_element_type=F32)
            yh = yh + skip_ref[:, at : at + CHANNEL_WIDTH] * xh.astype(F32)
            if k == 1:
                yh = yh + carried[:, at : at + CHANNEL_WIDTH]
            out_ref[lo : lo + tokens, at : at + CHANNEL_WIDTH] = yh


def local_y(xs, bs, cs, scal, skip, heads):
    length, width = xs.shape
    return pl.pallas_call(
        lambda *refs: local_y_kernel(*refs, heads=heads, tokens=length // 2),
        out_shape=jax.ShapeDtypeStruct((length, width), F32),
        compiler_params=params(),
        cost_estimate=cost(4e8, 4e6),
        name="local_y",
    )(xs, bs, cs, scal, skip)


def join_kernel(send_ref, s_ref, got_ref, out_ref):
    state = out_ref.shape[0]
    out_ref[...] = (s_ref[:state, :] + s_ref[state : state + 1, :] * got_ref[:state, :].astype(F32)).astype(BF16)


def join(send, s, got):
    return pl.pallas_call(
        join_kernel,
        out_shape=jax.ShapeDtypeStruct((STATE, s.shape[1]), BF16),
        compiler_params=params(),
        cost_estimate=cost(1e6, 1.5e6),
        name="join",
    )(send, s, got)


def finish_kernel(y_ref, local_ref, cs_ref, scal_ref, one_ref, two_ref, gate_ref, got_ref, gain_ref, out_ref, *, heads):
    length, width = local_ref.shape
    state, tokens = two_ref.shape[0], length // 2
    y = y_ref[0]
    decay = jnp.sum(one_ref[state:, :].astype(F32), axis=0, keepdims=True)
    start = one_ref[:state, :].astype(F32) + decay * two_ref[...].astype(F32)
    top = start.astype(BF16)
    low = (start - top.astype(F32)).astype(BF16)
    grow = jnp.exp(scal_ref[:, :heads])
    for k in range(2):
        at = pl.ds(k * tokens, tokens)
        carried = jnp.dot(cs_ref[at, :], top, preferred_element_type=F32)
        carried = carried + jnp.dot(cs_ref[at, :], low, preferred_element_type=F32)
        value = local_ref[at, :] + carried * spread(grow[k * tokens : (k + 1) * tokens, :], CHANNEL_WIDTH)
        gate = jnp.where(y == k, gate_ref[...], got_ref[...]).astype(F32)
        value = value * (gate / (1.0 + jnp.exp(-gate)))
        mean = jnp.sum(value * value, axis=1, keepdims=True) / width
        out_ref[at, :] = (value * lax.rsqrt(mean + EPS) * gain_ref[...]).astype(BF16)


def finish(y, local, cs, scal, one, two, gate, got, gain, heads):
    length, width = local.shape
    whole = lambda a: pl.BlockSpec(a.shape, lambda i, y: (0,) * a.ndim)
    return pl.pallas_call(
        lambda *refs: finish_kernel(*refs, heads=heads),
        grid_spec=pltpu.PrefetchScalarGridSpec(
            num_scalar_prefetch=1,
            grid=(1,),
            in_specs=[
                whole(local),
                whole(cs),
                whole(scal),
                whole(one),
                whole(two),
                pl.BlockSpec((length // 2, width), lambda i, y: (0, y[0])),
                whole(got),
                whole(gain),
            ],
            out_specs=pl.BlockSpec((length, width), lambda i, y: (0, 0)),
        ),
        out_shape=jax.ShapeDtypeStruct((length, width), BF16),
        compiler_params=params(1),
        cost_estimate=cost(1e8, 4e6),
        name="finish",
    )(y, local, cs, scal, one, two, gate, got, gain)


def project_kernel(yc_ref, own_ref, *refs):
    *got_refs, first_ref, second_ref, keep_ref, send_ref, both_ref = refs
    tokens, depth = keep_ref.shape[0], own_ref.shape[1]
    core = yc_ref[1]

    @pl.when(pl.program_id(0) == 0)
    def _():
        def fill(lower, upper):
            for k in range(2):
                rows = pl.ds(pl.multiple_of(jnp.where(core == 0, k, 1 - k) * tokens, tokens), tokens)
                both_ref[rows, :depth] = own_ref[k * tokens : (k + 1) * tokens, :]
                both_ref[rows, depth:] = (lower, upper)[k]()

        whole = got_refs[0]
        halves = lambda: fill(lambda: whole[:tokens, :], lambda: whole[tokens:, :])
        if len(got_refs) == 1:
            halves()
        else:
            pl.when(yc_ref[2] == 1)(halves)
            pl.when(yc_ref[2] == 0)(lambda: fill(lambda: got_refs[1][...], lambda: got_refs[2][...]))

    part = jnp.dot(both_ref[:, :depth], first_ref[...], preferred_element_type=F32)
    part = part + jnp.dot(both_ref[:, depth:], second_ref[...], preferred_element_type=F32)
    keep_ref[...] = part[:tokens, :]
    send_ref[...] = part[tokens:, :].astype(BF16)


def project(yc, own, got, w):
    length, depth = own.shape
    tokens, cols = length // 2, w.shape[1]
    tile = min(cols, 256)
    whole = lambda a: pl.BlockSpec(a.shape, lambda i, yc: (0, 0))
    return pl.pallas_call(
        project_kernel,
        grid_spec=pltpu.PrefetchScalarGridSpec(
            num_scalar_prefetch=1,
            grid=(cols // tile,),
            in_specs=[whole(own)]
            + [whole(v) for v in got]
            + [
                pl.BlockSpec((depth, tile), lambda i, yc: (yc[0], i)),
                pl.BlockSpec((depth, tile), lambda i, yc: (1 - yc[0], i)),
            ],
            out_specs=[
                pl.BlockSpec((tokens, tile), lambda i, yc: (0, i)),
                pl.BlockSpec((tokens, tile), lambda i, yc: (0, i)),
            ],
            scratch_shapes=[pltpu.VMEM((length, 2 * depth), BF16)],
        ),
        out_shape=[jax.ShapeDtypeStruct((tokens, cols), F32), jax.ShapeDtypeStruct((tokens, cols), BF16)],
        compiler_params=params(1),
        cost_estimate=cost(4.0 * length * depth * cols, 6e6),
        name="project",
    )(yc, own, *got, w, w)


def place_kernel(at_ref, mine_ref, got_ref, out_ref):
    cols = got_ref.shape[1]
    part = at_ref[0]
    out_ref[:, pl.ds(pl.multiple_of(part * cols, cols), cols)] = mine_ref[...]
    out_ref[:, pl.ds(pl.multiple_of((1 - part) * cols, cols), cols)] = got_ref[...]


def place(at, mine, got):
    tokens, cols = got.shape
    whole = pl.BlockSpec((tokens, cols), lambda i, at: (0, 0))
    return pl.pallas_call(
        place_kernel,
        grid_spec=pltpu.PrefetchScalarGridSpec(
            num_scalar_prefetch=1,
            grid=(1,),
            in_specs=[whole, whole],
            out_specs=pl.BlockSpec((tokens, 2 * cols), lambda i, at: (0, 0)),
        ),
        out_shape=jax.ShapeDtypeStruct((tokens, 2 * cols), BF16),
        compiler_params=params(1),
        cost_estimate=cost(1e6, 2e6),
        name="place",
    )(at, mine, got)


def pair_shards(nz, x_in, gate, b_proj, c_proj, dt_raw, dt_bias, a_log, skip_d, norm_gain, w_out):
    tokens = x_in.shape[0]
    heads = dt_raw.shape[1] // 2
    width = heads * CHANNEL_WIDTH
    seq, grp = lax.axis_index("seq"), lax.axis_index("grp")
    z, y = seq // 2, seq % 2
    yv = y.astype(jnp.int32).reshape(1)
    dt_raw = dt_raw.T
    both = ("seq", "grp")
    core = grp % 2
    spots = [(a, b, c, d) for a in range(nz) for b in range(2) for c in range(nz // 2) for d in range(2)]
    flat = lambda a, b, c, d: ((a * 2 + b) * (nz // 2) + c) * 2 + d
    tie = lax.optimization_barrier

    def half(v, axis, which):
        n = v.shape[axis] // 2
        return lax.dynamic_slice_in_dim(v, which * n, n, axis)

    flip = [(s, s ^ 1) for s in range(2 * nz)]
    sibling = [(g, g ^ 1) for g in range(nz)]
    def along(v, step, senders):
        pairs = [(a * 2 + b, (a + step) * 2 + b) for a in senders for b in range(2)]
        return lax.ppermute(v, "seq", pairs)

    got = lax.ppermute(pack(1 - yv, x_in, b_proj, c_proj, dt_raw, heads, 60 * 2**20), "seq", flip)
    own = pack(yv, x_in, b_proj, c_proj, dt_raw, heads, VMEM_LIMIT)
    gate_half = half(gate, 1, 1 - y)
    bias, alog = half(dt_bias, 0, y)[None, :], half(a_log, 0, y)[None, :]
    skip = jnp.repeat(half(skip_d, 0, y), CHANNEL_WIDTH)[None, :]
    gain = half(norm_gain, 0, y)[None, :]
    got_gate = lax.ppermute(gate_half, "seq", flip)
    got, own, bias, alog, skip, gain = tie((got, own, bias, alog, skip, gain))

    xs, bs, cs, scal, send, s = local_state(yv, own, got, bias, alog, heads)
    one = along(send, 1, range(nz - 1))
    base = local_y(xs, bs, cs, scal, skip, heads)
    one, base = tie((one, base))

    two = along(join(send, s, one), 2, range(nz - 2))
    block = finish(yv, base, cs, scal, one, two, gate, got_gate, gain, heads)

    hop = lambda value, *moves: lax.ppermute(value, "seq", [(i * 2 + b, j * 2 + b) for i, j in moves for b in range(2)])
    inner = (z == 1) | (z == 2)
    yc = jnp.stack([y, core, inner]).astype(jnp.int32)
    across = lambda value: lax.ppermute(value, "seq", flip)
    cross = lambda value: lax.ppermute(value, "grp", sibling)

    def reduce_core(full, rounded):
        return (full + cross(rounded).astype(F32)).astype(BF16)

    def deliver(slot, near, distant):
        near_x, total = grp // 2 == z // 2, 0.0
        for turn in range(2):
            pairs = []
            for a, b, c, d in spots:
                at = slot if c ^ turn == a // 2 else slot + 2
                pairs.append((flat(a, b, c, d), flat(a ^ at, d, a // 2, b)))
            value = jnp.where(near_x, near, distant) if turn == 0 else jnp.where(near_x, distant, near)
            moved = lax.ppermute(value, both, [(i, j) for i, j in pairs if i != j])
            if any(i == j for i, j in pairs):
                moved = jnp.where(near_x & (y == core), near, moved)
            total = total + moved.astype(F32)
        return total

    slot1 = hop(block, (0, 1), (1, 0), (2, 3), (3, 2))
    middle = hop(block, (1, 2), (2, 1))
    other0 = across(block)
    inward, outward = hop(slot1, (1, 2), (2, 1)), hop(middle, (1, 0), (2, 3))
    other1 = across(slot1)
    a0 = project(yc, block, [other0], w_out)
    inward, a0 = tie((inward, a0))
    last = hop(inward, (1, 0), (2, 3))
    slot2 = jnp.where(inner, inward, outward)
    other2 = across(slot2)
    a1 = project(yc, slot1, [other1], w_out)
    b0 = reduce_core(*a0)
    inner3 = hop(other0, (1, 2), (2, 1))
    last, inner3, a1, b0 = tie((last, inner3, a1, b0))
    slot3 = jnp.where(inner, middle, last)
    lower3 = lax.ppermute(last[:tokens], "seq", [(i * 2 + b, i * 2 + 1 - b) for i in (0, 3) for b in range(2)])
    upper3 = hop(other2[tokens:], (1, 0), (2, 3))
    a2 = project(yc, slot2, [other2], w_out)
    rounded = jnp.concatenate([a1[1], a2[1]])
    lower3, upper3, rounded = tie((lower3, upper3, rounded))
    sums = cross(rounded).reshape(2, tokens, -1)
    b1, b2 = ((part[0] + v.astype(F32)).astype(BF16) for part, v in zip((a1, a2), sums))
    b3 = reduce_core(*project(yc, slot3, [inner3, lower3, upper3], w_out))
    b0, b1, b2, b3 = tie((b0, b1, b2, b3))
    odd = deliver(1, b1, b3)
    even = deliver(0, b0, b2)
    here = core == z % 2
    mine, theirs = jnp.where(here, even, odd), jnp.where(here, odd, even)
    return place(core.astype(jnp.int32).reshape(1), mine.astype(BF16), cross(theirs.astype(BF16)))


def prefix(array, axis, combine, identity):
    length, mine = (lax.axis_size(axis), lax.axis_index(axis))
    everything = jax.tree.map(lambda part: lax.all_gather(part, axis), array)
    start = jax.tree.map(
        lambda part, zero: jnp.broadcast_to(jnp.asarray(zero, part.dtype), part.shape),
        array,
        identity,
    )

    def turn(k, before):
        reached = k < mine
        new = combine(before, jax.tree.map(lambda part: part[k], everything))
        return jax.tree.map(lambda a, b: jnp.where(reached, a, b), new, before)

    return lax.fori_loop(0, length, turn, start)


def ssd_blocks(xf, dt, la, bm, cm, braw, craw, init):
    length, heads, width = xf.shape
    groups = bm.shape[1]
    ratio = heads // groups
    block = math.gcd(length, 256)
    count = length // block

    def step(state, blk):
        xb, dtb, lab, bb, cb, bnar, cnar = blk
        cum = jnp.cumsum(lab, axis=0)
        attention_logits = jnp.einsum("tgn,sgn->gts", cnar, bnar, preferred_element_type=F32)
        attention_logits = jnp.repeat(attention_logits, ratio, axis=0)
        diff = cum.T[:, :, None] - cum.T[:, None, :]
        rows = lax.broadcasted_iota(jnp.int32, (block, block), 0)
        cols = lax.broadcasted_iota(jnp.int32, (block, block), 1)
        mask = (rows >= cols)[None, :, :]
        decay = jnp.exp(jnp.where(mask, diff, -1e30))
        mixing = decay * attention_logits * dtb.T[:, None, :]
        outs = jnp.einsum("hts,shp->thp", mixing, xb, precision=HIGH)
        cheads = jnp.repeat(cb, ratio, axis=1)
        bheads = jnp.repeat(bb, ratio, axis=1)
        outs = outs + jnp.exp(cum)[:, :, None] * jnp.einsum("thn,hpn->thp", cheads, state, precision=HIGH)
        weights = jnp.exp(cum[-1][None, :] - cum) * dtb
        fresh = jnp.einsum("sh,shp,shn->hpn", weights, xb, bheads, precision=HIGH)
        state = jnp.exp(cum[-1])[:, None, None] * state + fresh
        return (state, outs)

    cut = lambda v: v.reshape((count, block) + v.shape[1:])
    final, outs = lax.scan(step, init, jax.tree.map(cut, (xf, dt, la, bm, cm, braw, craw)))
    return (outs.reshape(length, heads, width), final, jnp.sum(la, axis=0))


def gated_norm_output(y, multiplier_channels, norm_gain, groups):
    length = y.shape[0]
    gated = y.reshape(length, -1) * jax.nn.silu(multiplier_channels.astype(F32))
    split = gated.reshape(length, groups, -1)
    split = split * lax.rsqrt(jnp.mean(split * split, axis=-1, keepdims=True) + EPS)
    return (split.reshape(length, -1) * norm_gain).astype(BF16)


def combine_states(earlier_state, later):
    return (earlier_state[0] * later[0], later[0][:, None, None] * earlier_state[1] + later[1])


def general_shards(x_in, gate, b_proj, c_proj, dt_raw, dt_bias, a_log, skip_d, norm_gain, w_out):
    length = x_in.shape[0]
    heads = dt_raw.shape[1]
    groups = b_proj.shape[1] // STATE
    xf = x_in.astype(F32).reshape(length, heads, CHANNEL_WIDTH)
    dt = jax.nn.softplus(dt_raw + dt_bias)
    la = -jnp.exp(a_log) * dt
    braw = b_proj.reshape(length, groups, STATE)
    craw = c_proj.reshape(length, groups, STATE)
    bm = braw.astype(F32)
    cm = craw.astype(F32)
    empty = jnp.zeros((heads, CHANNEL_WIDTH, STATE), F32)
    y, local_end, total = ssd_blocks(xf, dt, la, bm, cm, braw, craw, empty)
    identity = (jnp.ones((heads,), F32), empty)
    carried = prefix((jnp.exp(total), local_end), "seq", combine_states, identity)
    cum = jnp.cumsum(la, axis=0)
    cheads = jnp.repeat(cm, heads // groups, axis=1)
    y = y + jnp.exp(cum)[:, :, None] * jnp.einsum("thn,hpn->thp", cheads, carried[1], precision=HIGH)
    y = y + skip_d[None, :, None] * xf
    normed = gated_norm_output(y, gate, norm_gain, groups)
    partial_out = jnp.dot(
        normed, lax.all_gather(w_out, "seq", axis=1, tiled=True), preferred_element_type=F32
    )
    return lax.psum_scatter(partial_out, "grp", scatter_dimension=1, tiled=True).astype(BF16)


def solution(mesh):
    seq, grp = mesh.shape["seq"], mesh.shape["grp"]

    def shards(*args):
        groups = args[2].shape[1] // STATE
        if grp == 4 and seq == 2 * grp and groups == 2:
            return pair_shards(grp, *args)
        return general_shards(*args)

    return jax.shard_map(
        shards,
        mesh=mesh,
        in_specs=(
            P("seq", "grp"),
            P("seq", "grp"),
            P("seq", "grp"),
            P("seq", "grp"),
            P("seq", "grp"),
            P("grp"),
            P("grp"),
            P("grp"),
            P("grp"),
            P("grp", "seq"),
        ),
        out_specs=P("seq", "grp"),
        check_vma=False,
    )
```

```python
import math

import jax
import jax.numpy as jnp
from jax import lax
from jax.experimental import pallas as pl
from jax.experimental.pallas import tpu as pltpu
from jax.sharding import PartitionSpec as P

CHANNEL_WIDTH = 128
STATE = 128
EPS = 1e-05

HIGH = lax.Precision.HIGHEST
F32 = jnp.float32
BF16 = jnp.bfloat16
NT = (((1,), (1,)), ((), ()))
TN = (((0,), (0,)), ((), ()))
VMEM_LIMIT = 24 * 2**20


def params(grid_dims=0, limit=VMEM_LIMIT):
    return pltpu.CompilerParams(
        vmem_limit_bytes=limit,
        dimension_semantics=("arbitrary",) * grid_dims if grid_dims else None,
    )


def cost(flops, moved):
    return pl.CostEstimate(flops=int(flops), bytes_accessed=int(moved), transcendentals=0)


def iota(shape, axis):
    return lax.broadcasted_iota(jnp.int32, shape, axis)


def spread(values, width):
    heads = values.shape[1]
    return jnp.concatenate(
        [jnp.broadcast_to(values[:, h : h + 1], (values.shape[0], width)) for h in range(heads)], axis=1
    )


def split3(value):
    hi = value.astype(BF16)
    rest = value - hi.astype(F32)
    mid = rest.astype(BF16)
    return hi, mid, (rest - mid.astype(F32)).astype(BF16)


def pack_kernel(group_ref, x_ref, b_ref, c_ref, dt_ref, out_ref, *, heads):
    width, state = x_ref.shape[1], b_ref.shape[1]
    out_ref[:, :width] = x_ref[...]
    out_ref[:, width : width + state] = b_ref[...]
    out_ref[:, width + state : width + 2 * state] = c_ref[...]
    group = group_ref[0]
    rows, cols = iota((2 * heads, 128), 0), iota((2 * heads, 128), 1)
    total = jnp.zeros((x_ref.shape[0], 128), F32)
    for part, value in enumerate(split3(dt_ref[...])):
        where = (cols == rows - group * heads + part * heads) & (rows // heads == group)
        total = total + lax.dot_general(value, where.astype(BF16), TN, preferred_element_type=F32)
    out_ref[:, width + 2 * state :] = total.astype(BF16)


def pack(group, x, b, c, dt, heads, limit):
    tokens, width, state = x.shape[0], heads * CHANNEL_WIDTH, STATE
    out = jax.ShapeDtypeStruct((tokens, width + 2 * state + 128), BF16)
    return pl.pallas_call(
        lambda *refs: pack_kernel(*refs, heads=heads),
        grid_spec=pltpu.PrefetchScalarGridSpec(
            num_scalar_prefetch=1,
            grid=(1,),
            in_specs=[
                pl.BlockSpec((tokens, width), lambda i, g: (0, g[0])),
                pl.BlockSpec((tokens, state), lambda i, g: (0, g[0])),
                pl.BlockSpec((tokens, state), lambda i, g: (0, g[0])),
                pl.BlockSpec(dt.shape, lambda i, g: (0, 0)),
            ],
            out_specs=pl.BlockSpec(out.shape, lambda i, g: (0, 0)),
        ),
        out_shape=out,
        compiler_params=params(1, limit),
        cost_estimate=cost(1e6, 1e6),
        name="pack",
    )(group, x, b, c, dt)


def local_state_kernel(
    y_ref, own_ref, pk_ref, bias_ref, alog_ref, xs_ref, bs_ref, cs_ref, scal_ref, send_ref, s_ref, *, heads,
):
    tokens = own_ref.shape[0]
    width, state = xs_ref.shape[1], bs_ref.shape[1]
    y = y_ref[0]
    rows, cols = iota((128, heads), 0), iota((128, heads), 1)
    take = ((rows % heads == cols) & (rows < 3 * heads)).astype(BF16)
    steps = []
    for ref, place in ((own_ref, y), (pk_ref, 1 - y)):
        at = pl.ds(pl.multiple_of(place * tokens, tokens), tokens)
        xs_ref[at, :] = ref[:, :width]
        bs_ref[at, :] = ref[:, width : width + state]
        cs_ref[at, :] = ref[:, width + state : width + 2 * state]
        steps.append(jnp.dot(ref[:, width + 2 * state :], take, preferred_element_type=F32))
    own, other = steps
    raw = jnp.concatenate([jnp.where(y == 0, own, other), jnp.where(y == 0, other, own)], axis=0)
    raw = raw + bias_ref[...]
    dt = jnp.maximum(raw, 0.0) + jnp.log1p(jnp.exp(-jnp.abs(raw)))
    la = -jnp.exp(alog_ref[...]) * dt
    length = 2 * tokens
    lower = (iota((length, length), 0) >= iota((length, length), 1)).astype(F32)
    cum = jnp.dot(lower, la, precision=HIGH)
    last = cum[length - 1 : length, :]
    scal_ref[:, :heads] = cum
    scal_ref[:, heads : 2 * heads] = dt
    weights = jnp.exp(last - cum) * dt
    scaled = (xs_ref[...].astype(F32) * spread(weights, CHANNEL_WIDTH)).astype(BF16)
    s = lax.dot_general(bs_ref[...], scaled, TN, preferred_element_type=F32)
    s_ref[:state, :] = s
    send_ref[:state, :] = s.astype(BF16)
    decay = spread(jnp.exp(last), CHANNEL_WIDTH)
    s_ref[state:, :] = jnp.broadcast_to(decay, (8, width))
    hi, mid, lo = split3(decay)
    which = iota((16, width), 0)
    parts = jnp.where(which == 0, hi.astype(F32), jnp.where(which == 1, mid.astype(F32), lo.astype(F32)))
    send_ref[state:, :] = jnp.where(which < 3, parts, 0.0).astype(BF16)


def local_state(y, own, pk, bias, alog, heads):
    tokens, width, state = own.shape[0], heads * CHANNEL_WIDTH, STATE
    whole = lambda a: pl.BlockSpec(a.shape, lambda i, y: (0,) * a.ndim)
    outs = [
        jax.ShapeDtypeStruct((2 * tokens, width), BF16),
        jax.ShapeDtypeStruct((2 * tokens, state), BF16),
        jax.ShapeDtypeStruct((2 * tokens, state), BF16),
        jax.ShapeDtypeStruct((2 * tokens, 2 * heads), F32),
        jax.ShapeDtypeStruct((state + 16, width), BF16),
        jax.ShapeDtypeStruct((state + 8, width), F32),
    ]
    return pl.pallas_call(
        lambda *refs: local_state_kernel(*refs, heads=heads),
        grid_spec=pltpu.PrefetchScalarGridSpec(
            num_scalar_prefetch=1,
            grid=(1,),
            in_specs=[whole(own), whole(pk), whole(bias), whole(alog)],
            out_specs=[whole(o) for o in outs],
        ),
        out_shape=outs,
        compiler_params=params(1),
        cost_estimate=cost(2e8, 3e6),
        name="local_state",
    )(y, own, pk, bias, alog)


def local_y_kernel(xs_ref, bs_ref, cs_ref, scal_ref, skip_ref, out_ref, *, heads, tokens):
    cum, dt = scal_ref[:, :heads], scal_ref[:, heads : 2 * heads]
    length = 2 * tokens
    eye = (iota((length, length), 0) == iota((length, length), 1)).astype(F32)
    flat = lax.dot_general(scal_ref[...], eye, TN, precision=HIGH)
    cum_row, dt_row = flat[:heads, :], flat[heads : 2 * heads, :]
    mask = iota((tokens, tokens), 0) >= iota((tokens, tokens), 1)
    logits = []
    for k in range(2):
        at = pl.ds(k * tokens, tokens)
        logits.append(lax.dot_general(cs_ref[at, :], bs_ref[at, :], NT, preferred_element_type=F32))
    middle = cum[tokens - 1 : tokens, :]
    weights = jnp.exp(middle - cum[:tokens, :]) * dt[:tokens, :]
    scaled = (xs_ref[:tokens, :].astype(F32) * spread(weights, CHANNEL_WIDTH)).astype(BF16)
    s = lax.dot_general(bs_ref[:tokens, :], scaled, TN, preferred_element_type=F32).astype(BF16)
    carried = jnp.dot(cs_ref[tokens:, :], s, preferred_element_type=F32)
    carried = carried * spread(jnp.exp(cum[tokens:, :] - middle), CHANNEL_WIDTH)
    for k in range(2):
        lo = k * tokens
        for h in range(heads):
            at = h * CHANNEL_WIDTH
            xh = xs_ref[lo : lo + tokens, at : at + CHANNEL_WIDTH]
            diff = cum[lo : lo + tokens, h : h + 1] - cum_row[h : h + 1, lo : lo + tokens]
            mix = jnp.exp(jnp.where(mask, diff, -1e30)) * logits[k] * dt_row[h : h + 1, lo : lo + tokens]
            top = mix.astype(BF16)
            yh = jnp.dot(top, xh, preferred_element_type=F32)
            yh = yh + jnp.dot((mix - top.astype(F32)).astype(BF16), xh, preferred_element_type=F32)
            yh = yh + skip_ref[:, at : at + CHANNEL_WIDTH] * xh.astype(F32)
            if k == 1:
                yh = yh + carried[:, at : at + CHANNEL_WIDTH]
            out_ref[lo : lo + tokens, at : at + CHANNEL_WIDTH] = yh


def local_y(xs, bs, cs, scal, skip, heads):
    length, width = xs.shape
    return pl.pallas_call(
        lambda *refs: local_y_kernel(*refs, heads=heads, tokens=length // 2),
        out_shape=jax.ShapeDtypeStruct((length, width), F32),
        compiler_params=params(),
        cost_estimate=cost(4e8, 4e6),
        name="local_y",
    )(xs, bs, cs, scal, skip)


def join_kernel(send_ref, s_ref, got_ref, out_ref):
    state = out_ref.shape[0]
    out_ref[...] = (s_ref[:state, :] + s_ref[state : state + 1, :] * got_ref[:state, :].astype(F32)).astype(BF16)


def join(send, s, got):
    return pl.pallas_call(
        join_kernel,
        out_shape=jax.ShapeDtypeStruct((STATE, s.shape[1]), BF16),
        compiler_params=params(),
        cost_estimate=cost(1e6, 1.5e6),
        name="join",
    )(send, s, got)


def finish_kernel(y_ref, local_ref, cs_ref, scal_ref, one_ref, two_ref, gate_ref, got_ref, gain_ref, out_ref, *, heads):
    length, width = local_ref.shape
    state, tokens = two_ref.shape[0], length // 2
    y = y_ref[0]
    decay = jnp.sum(one_ref[state:, :].astype(F32), axis=0, keepdims=True)
    start = one_ref[:state, :].astype(F32) + decay * two_ref[...].astype(F32)
    top = start.astype(BF16)
    low = (start - top.astype(F32)).astype(BF16)
    grow = jnp.exp(scal_ref[:, :heads])
    for k in range(2):
        at = pl.ds(k * tokens, tokens)
        carried = jnp.dot(cs_ref[at, :], top, preferred_element_type=F32)
        carried = carried + jnp.dot(cs_ref[at, :], low, preferred_element_type=F32)
        value = local_ref[at, :] + carried * spread(grow[k * tokens : (k + 1) * tokens, :], CHANNEL_WIDTH)
        gate = jnp.where(y == k, gate_ref[...], got_ref[...]).astype(F32)
        value = value * (gate / (1.0 + jnp.exp(-gate)))
        mean = jnp.sum(value * value, axis=1, keepdims=True) / width
        out_ref[at, :] = (value * lax.rsqrt(mean + EPS) * gain_ref[...]).astype(BF16)


def finish(y, local, cs, scal, one, two, gate, got, gain, heads):
    length, width = local.shape
    whole = lambda a: pl.BlockSpec(a.shape, lambda i, y: (0,) * a.ndim)
    return pl.pallas_call(
        lambda *refs: finish_kernel(*refs, heads=heads),
        grid_spec=pltpu.PrefetchScalarGridSpec(
            num_scalar_prefetch=1,
            grid=(1,),
            in_specs=[
                whole(local),
                whole(cs),
                whole(scal),
                whole(one),
                whole(two),
                pl.BlockSpec((length // 2, width), lambda i, y: (0, y[0])),
                whole(got),
                whole(gain),
            ],
            out_specs=pl.BlockSpec((length, width), lambda i, y: (0, 0)),
        ),
        out_shape=jax.ShapeDtypeStruct((length, width), BF16),
        compiler_params=params(1),
        cost_estimate=cost(1e8, 4e6),
        name="finish",
    )(y, local, cs, scal, one, two, gate, got, gain)


def project_kernel(yc_ref, own_ref, *refs):
    *got_refs, first_ref, second_ref, keep_ref, send_ref, both_ref = refs
    tokens, depth = keep_ref.shape[0], own_ref.shape[1]
    core = yc_ref[1]

    @pl.when(pl.program_id(0) == 0)
    def _():
        def fill(lower, upper):
            for k in range(2):
                rows = pl.ds(pl.multiple_of(jnp.where(core == 0, k, 1 - k) * tokens, tokens), tokens)
                both_ref[rows, :depth] = own_ref[k * tokens : (k + 1) * tokens, :]
                both_ref[rows, depth:] = (lower, upper)[k]()

        whole = got_refs[0]
        halves = lambda: fill(lambda: whole[:tokens, :], lambda: whole[tokens:, :])
        if len(got_refs) == 1:
            halves()
        else:
            pl.when(yc_ref[2] == 1)(halves)
            pl.when(yc_ref[2] == 0)(lambda: fill(lambda: got_refs[1][...], lambda: got_refs[2][...]))

    part = jnp.dot(both_ref[:, :depth], first_ref[...], preferred_element_type=F32)
    part = part + jnp.dot(both_ref[:, depth:], second_ref[...], preferred_element_type=F32)
    keep_ref[...] = part[:tokens, :]
    send_ref[...] = part[tokens:, :].astype(BF16)


def project(yc, own, got, w):
    length, depth = own.shape
    tokens, cols = length // 2, w.shape[1]
    tile = min(cols, 256)
    whole = lambda a: pl.BlockSpec(a.shape, lambda i, yc: (0, 0))
    return pl.pallas_call(
        project_kernel,
        grid_spec=pltpu.PrefetchScalarGridSpec(
            num_scalar_prefetch=1,
            grid=(cols // tile,),
            in_specs=[whole(own)]
            + [whole(v) for v in got]
            + [
                pl.BlockSpec((depth, tile), lambda i, yc: (yc[0], i)),
                pl.BlockSpec((depth, tile), lambda i, yc: (1 - yc[0], i)),
            ],
            out_specs=[
                pl.BlockSpec((tokens, tile), lambda i, yc: (0, i)),
                pl.BlockSpec((tokens, tile), lambda i, yc: (0, i)),
            ],
            scratch_shapes=[pltpu.VMEM((length, 2 * depth), BF16)],
        ),
        out_shape=[jax.ShapeDtypeStruct((tokens, cols), F32), jax.ShapeDtypeStruct((tokens, cols), BF16)],
        compiler_params=params(1),
        cost_estimate=cost(4.0 * length * depth * cols, 6e6),
        name="project",
    )(yc, own, *got, w, w)


def place_kernel(at_ref, mine_ref, got_ref, out_ref):
    cols = got_ref.shape[1]
    part = at_ref[0]
    out_ref[:, pl.ds(pl.multiple_of(part * cols, cols), cols)] = mine_ref[...]
    out_ref[:, pl.ds(pl.multiple_of((1 - part) * cols, cols), cols)] = got_ref[...]


def place(at, mine, got):
    tokens, cols = got.shape
    whole = pl.BlockSpec((tokens, cols), lambda i, at: (0, 0))
    return pl.pallas_call(
        place_kernel,
        grid_spec=pltpu.PrefetchScalarGridSpec(
            num_scalar_prefetch=1,
            grid=(1,),
            in_specs=[whole, whole],
            out_specs=pl.BlockSpec((tokens, 2 * cols), lambda i, at: (0, 0)),
        ),
        out_shape=jax.ShapeDtypeStruct((tokens, 2 * cols), BF16),
        compiler_params=params(1),
        cost_estimate=cost(1e6, 2e6),
        name="place",
    )(at, mine, got)


def pair_shards(nz, x_in, gate, b_proj, c_proj, dt_raw, dt_bias, a_log, skip_d, norm_gain, w_out):
    tokens = x_in.shape[0]
    heads = dt_raw.shape[1] // 2
    width = heads * CHANNEL_WIDTH
    seq, grp = lax.axis_index("seq"), lax.axis_index("grp")
    z, y = seq // 2, seq % 2
    yv = y.astype(jnp.int32).reshape(1)
    dt_raw = dt_raw.T
    both = ("seq", "grp")
    core = grp % 2
    spots = [(a, b, c, d) for a in range(nz) for b in range(2) for c in range(nz // 2) for d in range(2)]
    flat = lambda a, b, c, d: ((a * 2 + b) * (nz // 2) + c) * 2 + d
    tie = lax.optimization_barrier

    def half(v, axis, which):
        n = v.shape[axis] // 2
        return lax.dynamic_slice_in_dim(v, which * n, n, axis)

    flip = [(s, s ^ 1) for s in range(2 * nz)]
    sibling = [(g, g ^ 1) for g in range(nz)]
    def along(v, step, senders):
        pairs = [(a * 2 + b, (a + step) * 2 + b) for a in senders for b in range(2)]
        return lax.ppermute(v, "seq", pairs)

    got = lax.ppermute(pack(1 - yv, x_in, b_proj, c_proj, dt_raw, heads, 60 * 2**20), "seq", flip)
    own = pack(yv, x_in, b_proj, c_proj, dt_raw, heads, VMEM_LIMIT)
    gate_half = half(gate, 1, 1 - y)
    bias, alog = half(dt_bias, 0, y)[None, :], half(a_log, 0, y)[None, :]
    skip = jnp.repeat(half(skip_d, 0, y), CHANNEL_WIDTH)[None, :]
    gain = half(norm_gain, 0, y)[None, :]
    got_gate = lax.ppermute(gate_half, "seq", flip)
    got, own, bias, alog, skip, gain = tie((got, own, bias, alog, skip, gain))

    xs, bs, cs, scal, send, s = local_state(yv, own, got, bias, alog, heads)
    one = along(send, 1, range(nz - 1))
    base = local_y(xs, bs, cs, scal, skip, heads)
    one, base = tie((one, base))

    two = along(join(send, s, one), 2, range(nz - 2))
    block = finish(yv, base, cs, scal, one, two, gate, got_gate, gain, heads)

    hop = lambda value, *moves: lax.ppermute(value, "seq", [(i * 2 + b, j * 2 + b) for i, j in moves for b in range(2)])
    inner = (z == 1) | (z == 2)
    yc = jnp.stack([y, core, inner]).astype(jnp.int32)
    across = lambda value: lax.ppermute(value, "seq", flip)
    cross = lambda value: lax.ppermute(value, "grp", sibling)

    def reduce_core(full, rounded):
        return (full + cross(rounded).astype(F32)).astype(BF16)

    def deliver(slot, near, distant):
        near_x, total = grp // 2 == z // 2, 0.0
        for turn in range(2):
            pairs = []
            for a, b, c, d in spots:
                at = slot if c ^ turn == a // 2 else slot + 2
                pairs.append((flat(a, b, c, d), flat(a ^ at, d, a // 2, b)))
            value = jnp.where(near_x, near, distant) if turn == 0 else jnp.where(near_x, distant, near)
            moved = lax.ppermute(value, both, [(i, j) for i, j in pairs if i != j])
            if any(i == j for i, j in pairs):
                moved = jnp.where(near_x & (y == core), near, moved)
            total = total + moved.astype(F32)
        return total

    slot1 = hop(block, (0, 1), (1, 0), (2, 3), (3, 2))
    middle = hop(block, (1, 2), (2, 1))
    other0 = across(block)
    inward, outward = hop(slot1, (1, 2), (2, 1)), hop(middle, (1, 0), (2, 3))
    other1 = across(slot1)
    a0 = project(yc, block, [other0], w_out)
    inward, a0 = tie((inward, a0))
    last = hop(inward, (1, 0), (2, 3))
    slot2 = jnp.where(inner, inward, outward)
    other2 = across(slot2)
    a1 = project(yc, slot1, [other1], w_out)
    b0 = reduce_core(*a0)
    inner3 = hop(other0, (1, 2), (2, 1))
    last, inner3, a1, b0 = tie((last, inner3, a1, b0))
    slot3 = jnp.where(inner, middle, last)
    lower3 = lax.ppermute(last[:tokens], "seq", [(i * 2 + b, i * 2 + 1 - b) for i in (0, 3) for b in range(2)])
    upper3 = hop(other2[tokens:], (1, 0), (2, 3))
    a2 = project(yc, slot2, [other2], w_out)
    rounded = jnp.concatenate([a1[1], a2[1]])
    lower3, upper3, rounded = tie((lower3, upper3, rounded))
    sums = cross(rounded).reshape(2, tokens, -1)
    b1, b2 = ((part[0] + v.astype(F32)).astype(BF16) for part, v in zip((a1, a2), sums))
    b3 = reduce_core(*project(yc, slot3, [inner3, lower3, upper3], w_out))
    b0, b1, b2, b3 = tie((b0, b1, b2, b3))
    odd = deliver(1, b1, b3)
    even = deliver(0, b0, b2)
    here = core == z % 2
    mine, theirs = jnp.where(here, even, odd), jnp.where(here, odd, even)
    return place(core.astype(jnp.int32).reshape(1), mine.astype(BF16), cross(theirs.astype(BF16)))


def prefix(array, axis, combine, identity):
    length, mine = (lax.axis_size(axis), lax.axis_index(axis))
    everything = jax.tree.map(lambda part: lax.all_gather(part, axis), array)
    start = jax.tree.map(
        lambda part, zero: jnp.broadcast_to(jnp.asarray(zero, part.dtype), part.shape),
        array,
        identity,
    )

    def turn(k, before):
        reached = k < mine
        new = combine(before, jax.tree.map(lambda part: part[k], everything))
        return jax.tree.map(lambda a, b: jnp.where(reached, a, b), new, before)

    return lax.fori_loop(0, length, turn, start)


def ssd_blocks(xf, dt, la, bm, cm, braw, craw, init):
    length, heads, width = xf.shape
    groups = bm.shape[1]
    ratio = heads // groups
    block = math.gcd(length, 256)
    count = length // block

    def step(state, blk):
        xb, dtb, lab, bb, cb, bnar, cnar = blk
        cum = jnp.cumsum(lab, axis=0)
        attention_logits = jnp.einsum("tgn,sgn->gts", cnar, bnar, preferred_element_type=F32)
        attention_logits = jnp.repeat(attention_logits, ratio, axis=0)
        diff = cum.T[:, :, None] - cum.T[:, None, :]
        rows = lax.broadcasted_iota(jnp.int32, (block, block), 0)
        cols = lax.broadcasted_iota(jnp.int32, (block, block), 1)
        mask = (rows >= cols)[None, :, :]
        decay = jnp.exp(jnp.where(mask, diff, -1e30))
        mixing = decay * attention_logits * dtb.T[:, None, :]
        outs = jnp.einsum("hts,shp->thp", mixing, xb, precision=HIGH)
        cheads = jnp.repeat(cb, ratio, axis=1)
        bheads = jnp.repeat(bb, ratio, axis=1)
        outs = outs + jnp.exp(cum)[:, :, None] * jnp.einsum("thn,hpn->thp", cheads, state, precision=HIGH)
        weights = jnp.exp(cum[-1][None, :] - cum) * dtb
        fresh = jnp.einsum("sh,shp,shn->hpn", weights, xb, bheads, precision=HIGH)
        state = jnp.exp(cum[-1])[:, None, None] * state + fresh
        return (state, outs)

    cut = lambda v: v.reshape((count, block) + v.shape[1:])
    final, outs = lax.scan(step, init, jax.tree.map(cut, (xf, dt, la, bm, cm, braw, craw)))
    return (outs.reshape(length, heads, width), final, jnp.sum(la, axis=0))


def gated_norm_output(y, multiplier_channels, norm_gain, groups):
    length = y.shape[0]
    gated = y.reshape(length, -1) * jax.nn.silu(multiplier_channels.astype(F32))
    split = gated.reshape(length, groups, -1)
    split = split * lax.rsqrt(jnp.mean(split * split, axis=-1, keepdims=True) + EPS)
    return (split.reshape(length, -1) * norm_gain).astype(BF16)


def combine_states(earlier_state, later):
    return (earlier_state[0] * later[0], later[0][:, None, None] * earlier_state[1] + later[1])


def general_shards(x_in, gate, b_proj, c_proj, dt_raw, dt_bias, a_log, skip_d, norm_gain, w_out):
    length = x_in.shape[0]
    heads = dt_raw.shape[1]
    groups = b_proj.shape[1] // STATE
    xf = x_in.astype(F32).reshape(length, heads, CHANNEL_WIDTH)
    dt = jax.nn.softplus(dt_raw + dt_bias)
    la = -jnp.exp(a_log) * dt
    braw = b_proj.reshape(length, groups, STATE)
    craw = c_proj.reshape(length, groups, STATE)
    bm = braw.astype(F32)
    cm = craw.astype(F32)
    empty = jnp.zeros((heads, CHANNEL_WIDTH, STATE), F32)
    y, local_end, total = ssd_blocks(xf, dt, la, bm, cm, braw, craw, empty)
    identity = (jnp.ones((heads,), F32), empty)
    carried = prefix((jnp.exp(total), local_end), "seq", combine_states, identity)
    cum = jnp.cumsum(la, axis=0)
    cheads = jnp.repeat(cm, heads // groups, axis=1)
    y = y + jnp.exp(cum)[:, :, None] * jnp.einsum("thn,hpn->thp", cheads, carried[1], precision=HIGH)
    y = y + skip_d[None, :, None] * xf
    normed = gated_norm_output(y, gate, norm_gain, groups)
    partial_out = jnp.dot(
        normed, lax.all_gather(w_out, "seq", axis=1, tiled=True), preferred_element_type=F32
    )
    return lax.psum_scatter(partial_out, "grp", scatter_dimension=1, tiled=True).astype(BF16)


def solution(mesh):
    seq, grp = mesh.shape["seq"], mesh.shape["grp"]

    def shards(*args):
        groups = args[2].shape[1] // STATE
        if grp == 4 and seq == 2 * grp and groups == 2:
            return pair_shards(grp, *args)
        return general_shards(*args)

    return jax.shard_map(
        shards,
        mesh=mesh,
        in_specs=(
            P("seq", "grp"),
            P("seq", "grp"),
            P("seq", "grp"),
            P("seq", "grp"),
            P("seq", "grp"),
            P("grp"),
            P("grp"),
            P("grp"),
            P("grp"),
            P("grp", "seq"),
        ),
        out_specs=P("seq", "grp"),
        check_vma=False,
    )
```

```python
import math

import jax
import jax.numpy as jnp
from jax import lax
from jax.experimental import pallas as pl
from jax.experimental.pallas import tpu as pltpu
from jax.sharding import PartitionSpec as P

CHANNEL_WIDTH = 128
STATE = 128
EPS = 1e-05

HIGH = lax.Precision.HIGHEST
F32 = jnp.float32
BF16 = jnp.bfloat16
NT = (((1,), (1,)), ((), ()))
TN = (((0,), (0,)), ((), ()))
VMEM_LIMIT = 24 * 2**20


def params(grid_dims=0, limit=VMEM_LIMIT):
    return pltpu.CompilerParams(
        vmem_limit_bytes=limit,
        dimension_semantics=("arbitrary",) * grid_dims if grid_dims else None,
    )


def cost(flops, moved):
    return pl.CostEstimate(flops=int(flops), bytes_accessed=int(moved), transcendentals=0)


def iota(shape, axis):
    return lax.broadcasted_iota(jnp.int32, shape, axis)


def spread(values, width):
    heads = values.shape[1]
    return jnp.concatenate(
        [jnp.broadcast_to(values[:, h : h + 1], (values.shape[0], width)) for h in range(heads)], axis=1
    )


def split3(value):
    hi = value.astype(BF16)
    rest = value - hi.astype(F32)
    mid = rest.astype(BF16)
    return hi, mid, (rest - mid.astype(F32)).astype(BF16)


def pack_kernel(group_ref, x_ref, b_ref, c_ref, dt_ref, out_ref, *, heads):
    width, state = x_ref.shape[1], b_ref.shape[1]
    out_ref[:, :width] = x_ref[...]
    out_ref[:, width : width + state] = b_ref[...]
    out_ref[:, width + state : width + 2 * state] = c_ref[...]
    group = group_ref[0]
    rows, cols = iota((2 * heads, 128), 0), iota((2 * heads, 128), 1)
    total = jnp.zeros((x_ref.shape[0], 128), F32)
    for part, value in enumerate(split3(dt_ref[...])):
        where = (cols == rows - group * heads + part * heads) & (rows // heads == group)
        total = total + lax.dot_general(value, where.astype(BF16), TN, preferred_element_type=F32)
    out_ref[:, width + 2 * state :] = total.astype(BF16)


def pack(group, x, b, c, dt, heads, limit):
    tokens, width, state = x.shape[0], heads * CHANNEL_WIDTH, STATE
    out = jax.ShapeDtypeStruct((tokens, width + 2 * state + 128), BF16)
    return pl.pallas_call(
        lambda *refs: pack_kernel(*refs, heads=heads),
        grid_spec=pltpu.PrefetchScalarGridSpec(
            num_scalar_prefetch=1,
            grid=(1,),
            in_specs=[
                pl.BlockSpec((tokens, width), lambda i, g: (0, g[0])),
                pl.BlockSpec((tokens, state), lambda i, g: (0, g[0])),
                pl.BlockSpec((tokens, state), lambda i, g: (0, g[0])),
                pl.BlockSpec(dt.shape, lambda i, g: (0, 0)),
            ],
            out_specs=pl.BlockSpec(out.shape, lambda i, g: (0, 0)),
        ),
        out_shape=out,
        compiler_params=params(1, limit),
        cost_estimate=cost(1e6, 1e6),
        name="pack",
    )(group, x, b, c, dt)


def local_state_kernel(
    y_ref, own_ref, pk_ref, bias_ref, alog_ref, xs_ref, bs_ref, cs_ref, scal_ref, send_ref, s_ref, *, heads,
):
    tokens = own_ref.shape[0]
    width, state = xs_ref.shape[1], bs_ref.shape[1]
    y = y_ref[0]
    rows, cols = iota((128, heads), 0), iota((128, heads), 1)
    take = ((rows % heads == cols) & (rows < 3 * heads)).astype(BF16)
    steps = []
    for ref, place in ((own_ref, y), (pk_ref, 1 - y)):
        at = pl.ds(pl.multiple_of(place * tokens, tokens), tokens)
        xs_ref[at, :] = ref[:, :width]
        bs_ref[at, :] = ref[:, width : width + state]
        cs_ref[at, :] = ref[:, width + state : width + 2 * state]
        steps.append(jnp.dot(ref[:, width + 2 * state :], take, preferred_element_type=F32))
    own, other = steps
    raw = jnp.concatenate([jnp.where(y == 0, own, other), jnp.where(y == 0, other, own)], axis=0)
    raw = raw + bias_ref[...]
    dt = jnp.maximum(raw, 0.0) + jnp.log1p(jnp.exp(-jnp.abs(raw)))
    la = -jnp.exp(alog_ref[...]) * dt
    length = 2 * tokens
    lower = (iota((length, length), 0) >= iota((length, length), 1)).astype(F32)
    cum = jnp.dot(lower, la, precision=HIGH)
    last = cum[length - 1 : length, :]
    scal_ref[:, :heads] = cum
    scal_ref[:, heads : 2 * heads] = dt
    weights = jnp.exp(last - cum) * dt
    scaled = (xs_ref[...].astype(F32) * spread(weights, CHANNEL_WIDTH)).astype(BF16)
    s = lax.dot_general(bs_ref[...], scaled, TN, preferred_element_type=F32)
    s_ref[:state, :] = s
    send_ref[:state, :] = s.astype(BF16)
    decay = spread(jnp.exp(last), CHANNEL_WIDTH)
    s_ref[state:, :] = jnp.broadcast_to(decay, (8, width))
    hi, mid, lo = split3(decay)
    which = iota((16, width), 0)
    parts = jnp.where(which == 0, hi.astype(F32), jnp.where(which == 1, mid.astype(F32), lo.astype(F32)))
    send_ref[state:, :] = jnp.where(which < 3, parts, 0.0).astype(BF16)


def local_state(y, own, pk, bias, alog, heads):
    tokens, width, state = own.shape[0], heads * CHANNEL_WIDTH, STATE
    whole = lambda a: pl.BlockSpec(a.shape, lambda i, y: (0,) * a.ndim)
    outs = [
        jax.ShapeDtypeStruct((2 * tokens, width), BF16),
        jax.ShapeDtypeStruct((2 * tokens, state), BF16),
        jax.ShapeDtypeStruct((2 * tokens, state), BF16),
        jax.ShapeDtypeStruct((2 * tokens, 2 * heads), F32),
        jax.ShapeDtypeStruct((state + 16, width), BF16),
        jax.ShapeDtypeStruct((state + 8, width), F32),
    ]
    return pl.pallas_call(
        lambda *refs: local_state_kernel(*refs, heads=heads),
        grid_spec=pltpu.PrefetchScalarGridSpec(
            num_scalar_prefetch=1,
            grid=(1,),
            in_specs=[whole(own), whole(pk), whole(bias), whole(alog)],
            out_specs=[whole(o) for o in outs],
        ),
        out_shape=outs,
        compiler_params=params(1),
        cost_estimate=cost(2e8, 3e6),
        name="local_state",
    )(y, own, pk, bias, alog)


def local_y_kernel(xs_ref, bs_ref, cs_ref, scal_ref, skip_ref, out_ref, *, heads, tokens):
    cum, dt = scal_ref[:, :heads], scal_ref[:, heads : 2 * heads]
    length = 2 * tokens
    eye = (iota((length, length), 0) == iota((length, length), 1)).astype(F32)
    flat = lax.dot_general(scal_ref[...], eye, TN, precision=HIGH)
    cum_row, dt_row = flat[:heads, :], flat[heads : 2 * heads, :]
    mask = iota((tokens, tokens), 0) >= iota((tokens, tokens), 1)
    logits = []
    for k in range(2):
        at = pl.ds(k * tokens, tokens)
        logits.append(lax.dot_general(cs_ref[at, :], bs_ref[at, :], NT, preferred_element_type=F32))
    middle = cum[tokens - 1 : tokens, :]
    weights = jnp.exp(middle - cum[:tokens, :]) * dt[:tokens, :]
    scaled = (xs_ref[:tokens, :].astype(F32) * spread(weights, CHANNEL_WIDTH)).astype(BF16)
    s = lax.dot_general(bs_ref[:tokens, :], scaled, TN, preferred_element_type=F32).astype(BF16)
    carried = jnp.dot(cs_ref[tokens:, :], s, preferred_element_type=F32)
    carried = carried * spread(jnp.exp(cum[tokens:, :] - middle), CHANNEL_WIDTH)
    for k in range(2):
        lo = k * tokens
        for h in range(heads):
            at = h * CHANNEL_WIDTH
            xh = xs_ref[lo : lo + tokens, at : at + CHANNEL_WIDTH]
            diff = cum[lo : lo + tokens, h : h + 1] - cum_row[h : h + 1, lo : lo + tokens]
            mix = jnp.exp(jnp.where(mask, diff, -1e30)) * logits[k] * dt_row[h : h + 1, lo : lo + tokens]
            top = mix.astype(BF16)
            yh = jnp.dot(top, xh, preferred_element_type=F32)
            yh = yh + jnp.dot((mix - top.astype(F32)).astype(BF16), xh, preferred_element_type=F32)
            yh = yh + skip_ref[:, at : at + CHANNEL_WIDTH] * xh.astype(F32)
            if k == 1:
                yh = yh + carried[:, at : at + CHANNEL_WIDTH]
            out_ref[lo : lo + tokens, at : at + CHANNEL_WIDTH] = yh


def local_y(xs, bs, cs, scal, skip, heads):
    length, width = xs.shape
    return pl.pallas_call(
        lambda *refs: local_y_kernel(*refs, heads=heads, tokens=length // 2),
        out_shape=jax.ShapeDtypeStruct((length, width), F32),
        compiler_params=params(),
        cost_estimate=cost(4e8, 4e6),
        name="local_y",
    )(xs, bs, cs, scal, skip)


def join_kernel(send_ref, s_ref, got_ref, out_ref):
    state = out_ref.shape[0]
    out_ref[...] = (s_ref[:state, :] + s_ref[state : state + 1, :] * got_ref[:state, :].astype(F32)).astype(BF16)


def join(send, s, got):
    return pl.pallas_call(
        join_kernel,
        out_shape=jax.ShapeDtypeStruct((STATE, s.shape[1]), BF16),
        compiler_params=params(),
        cost_estimate=cost(1e6, 1.5e6),
        name="join",
    )(send, s, got)


def finish_kernel(y_ref, local_ref, cs_ref, scal_ref, one_ref, two_ref, gate_ref, got_ref, gain_ref, out_ref, *, heads):
    length, width = local_ref.shape
    state, tokens = two_ref.shape[0], length // 2
    y = y_ref[0]
    decay = jnp.sum(one_ref[state:, :].astype(F32), axis=0, keepdims=True)
    start = one_ref[:state, :].astype(F32) + decay * two_ref[...].astype(F32)
    top = start.astype(BF16)
    low = (start - top.astype(F32)).astype(BF16)
    grow = jnp.exp(scal_ref[:, :heads])
    for k in range(2):
        at = pl.ds(k * tokens, tokens)
        carried = jnp.dot(cs_ref[at, :], top, preferred_element_type=F32)
        carried = carried + jnp.dot(cs_ref[at, :], low, preferred_element_type=F32)
        value = local_ref[at, :] + carried * spread(grow[k * tokens : (k + 1) * tokens, :], CHANNEL_WIDTH)
        gate = jnp.where(y == k, gate_ref[...], got_ref[...]).astype(F32)
        value = value * (gate / (1.0 + jnp.exp(-gate)))
        mean = jnp.sum(value * value, axis=1, keepdims=True) / width
        out_ref[at, :] = (value * lax.rsqrt(mean + EPS) * gain_ref[...]).astype(BF16)


def finish(y, local, cs, scal, one, two, gate, got, gain, heads):
    length, width = local.shape
    whole = lambda a: pl.BlockSpec(a.shape, lambda i, y: (0,) * a.ndim)
    return pl.pallas_call(
        lambda *refs: finish_kernel(*refs, heads=heads),
        grid_spec=pltpu.PrefetchScalarGridSpec(
            num_scalar_prefetch=1,
            grid=(1,),
            in_specs=[
                whole(local),
                whole(cs),
                whole(scal),
                whole(one),
                whole(two),
                pl.BlockSpec((length // 2, width), lambda i, y: (0, y[0])),
                whole(got),
                whole(gain),
            ],
            out_specs=pl.BlockSpec((length, width), lambda i, y: (0, 0)),
        ),
        out_shape=jax.ShapeDtypeStruct((length, width), BF16),
        compiler_params=params(1),
        cost_estimate=cost(1e8, 4e6),
        name="finish",
    )(y, local, cs, scal, one, two, gate, got, gain)


def project_kernel(yc_ref, own_ref, *refs):
    *got_refs, first_ref, second_ref, keep_ref, send_ref, both_ref = refs
    tokens, depth = keep_ref.shape[0], own_ref.shape[1]
    core = yc_ref[1]

    @pl.when(pl.program_id(0) == 0)
    def _():
        def fill(lower, upper):
            for k in range(2):
                rows = pl.ds(pl.multiple_of(jnp.where(core == 0, k, 1 - k) * tokens, tokens), tokens)
                both_ref[rows, :depth] = own_ref[k * tokens : (k + 1) * tokens, :]
                both_ref[rows, depth:] = (lower, upper)[k]()

        whole = got_refs[0]
        halves = lambda: fill(lambda: whole[:tokens, :], lambda: whole[tokens:, :])
        if len(got_refs) == 1:
            halves()
        else:
            pl.when(yc_ref[2] == 1)(halves)
            pl.when(yc_ref[2] == 0)(lambda: fill(lambda: got_refs[1][...], lambda: got_refs[2][...]))

    part = jnp.dot(both_ref[:, :depth], first_ref[...], preferred_element_type=F32)
    part = part + jnp.dot(both_ref[:, depth:], second_ref[...], preferred_element_type=F32)
    keep_ref[...] = part[:tokens, :]
    send_ref[...] = part[tokens:, :].astype(BF16)


def project(yc, own, got, w):
    length, depth = own.shape
    tokens, cols = length // 2, w.shape[1]
    tile = min(cols, 256)
    whole = lambda a: pl.BlockSpec(a.shape, lambda i, yc: (0, 0))
    return pl.pallas_call(
        project_kernel,
        grid_spec=pltpu.PrefetchScalarGridSpec(
            num_scalar_prefetch=1,
            grid=(cols // tile,),
            in_specs=[whole(own)]
            + [whole(v) for v in got]
            + [
                pl.BlockSpec((depth, tile), lambda i, yc: (yc[0], i)),
                pl.BlockSpec((depth, tile), lambda i, yc: (1 - yc[0], i)),
            ],
            out_specs=[
                pl.BlockSpec((tokens, tile), lambda i, yc: (0, i)),
                pl.BlockSpec((tokens, tile), lambda i, yc: (0, i)),
            ],
            scratch_shapes=[pltpu.VMEM((length, 2 * depth), BF16)],
        ),
        out_shape=[jax.ShapeDtypeStruct((tokens, cols), F32), jax.ShapeDtypeStruct((tokens, cols), BF16)],
        compiler_params=params(1),
        cost_estimate=cost(4.0 * length * depth * cols, 6e6),
        name="project",
    )(yc, own, *got, w, w)


def place_kernel(at_ref, mine_ref, got_ref, out_ref):
    cols = got_ref.shape[1]
    part = at_ref[0]
    out_ref[:, pl.ds(pl.multiple_of(part * cols, cols), cols)] = mine_ref[...]
    out_ref[:, pl.ds(pl.multiple_of((1 - part) * cols, cols), cols)] = got_ref[...]


def place(at, mine, got):
    tokens, cols = got.shape
    whole = pl.BlockSpec((tokens, cols), lambda i, at: (0, 0))
    return pl.pallas_call(
        place_kernel,
        grid_spec=pltpu.PrefetchScalarGridSpec(
            num_scalar_prefetch=1,
            grid=(1,),
            in_specs=[whole, whole],
            out_specs=pl.BlockSpec((tokens, 2 * cols), lambda i, at: (0, 0)),
        ),
        out_shape=jax.ShapeDtypeStruct((tokens, 2 * cols), BF16),
        compiler_params=params(1),
        cost_estimate=cost(1e6, 2e6),
        name="place",
    )(at, mine, got)


def pair_shards(nz, x_in, gate, b_proj, c_proj, dt_raw, dt_bias, a_log, skip_d, norm_gain, w_out):
    tokens = x_in.shape[0]
    heads = dt_raw.shape[1] // 2
    width = heads * CHANNEL_WIDTH
    seq, grp = lax.axis_index("seq"), lax.axis_index("grp")
    z, y = seq // 2, seq % 2
    yv = y.astype(jnp.int32).reshape(1)
    dt_raw = dt_raw.T
    both = ("seq", "grp")
    core = grp % 2
    spots = [(a, b, c, d) for a in range(nz) for b in range(2) for c in range(nz // 2) for d in range(2)]
    flat = lambda a, b, c, d: ((a * 2 + b) * (nz // 2) + c) * 2 + d
    tie = lax.optimization_barrier

    def half(v, axis, which):
        n = v.shape[axis] // 2
        return lax.dynamic_slice_in_dim(v, which * n, n, axis)

    flip = [(s, s ^ 1) for s in range(2 * nz)]
    sibling = [(g, g ^ 1) for g in range(nz)]
    def along(v, step, senders):
        pairs = [(a * 2 + b, (a + step) * 2 + b) for a in senders for b in range(2)]
        return lax.ppermute(v, "seq", pairs)

    got = lax.ppermute(pack(1 - yv, x_in, b_proj, c_proj, dt_raw, heads, 60 * 2**20), "seq", flip)
    own = pack(yv, x_in, b_proj, c_proj, dt_raw, heads, VMEM_LIMIT)
    gate_half = half(gate, 1, 1 - y)
    bias, alog = half(dt_bias, 0, y)[None, :], half(a_log, 0, y)[None, :]
    skip = jnp.repeat(half(skip_d, 0, y), CHANNEL_WIDTH)[None, :]
    gain = half(norm_gain, 0, y)[None, :]
    got_gate = lax.ppermute(gate_half, "seq", flip)
    got, own, bias, alog, skip, gain = tie((got, own, bias, alog, skip, gain))

    xs, bs, cs, scal, send, s = local_state(yv, own, got, bias, alog, heads)
    one = along(send, 1, range(nz - 1))
    base = local_y(xs, bs, cs, scal, skip, heads)
    one, base = tie((one, base))

    two = along(join(send, s, one), 2, range(nz - 2))
    block = finish(yv, base, cs, scal, one, two, gate, got_gate, gain, heads)

    hop = lambda value, *moves: lax.ppermute(value, "seq", [(i * 2 + b, j * 2 + b) for i, j in moves for b in range(2)])
    inner = (z == 1) | (z == 2)
    yc = jnp.stack([y, core, inner]).astype(jnp.int32)
    across = lambda value: lax.ppermute(value, "seq", flip)
    cross = lambda value: lax.ppermute(value, "grp", sibling)

    def reduce_core(full, rounded):
        return (full + cross(rounded).astype(F32)).astype(BF16)

    def deliver(slot, far, near, distant):
        near_x, total = grp // 2 == z // 2, 0.0
        for turn in range(2):
            pairs = []
            for a, b, c, d in spots:
                at = slot if c ^ turn == a // 2 else far
                pairs.append((flat(a, b, c, d), flat(a ^ at, d, a // 2, b)))
            value = jnp.where(near_x, near, distant) if turn == 0 else jnp.where(near_x, distant, near)
            moved = lax.ppermute(value, both, [(i, j) for i, j in pairs if i != j])
            if any(i == j for i, j in pairs):
                moved = jnp.where(near_x & (y == core), near, moved)
            total = total + moved.astype(F32)
        return total

    slot1 = hop(block, (0, 1), (1, 0), (2, 3), (3, 2))
    middle = hop(block, (1, 2), (2, 1))
    other0 = across(block)
    inward, outward = hop(slot1, (1, 2), (2, 1)), hop(middle, (1, 0), (2, 3))
    other1 = across(slot1)
    a0 = project(yc, block, [other0], w_out)
    inward, a0 = tie((inward, a0))
    last = hop(inward, (1, 0), (2, 3))
    slot2 = jnp.where(inner, inward, outward)
    other2 = across(slot2)
    a1 = project(yc, slot1, [other1], w_out)
    b0 = reduce_core(*a0)
    inner3 = hop(other0, (1, 2), (2, 1))
    last, inner3, a1, b0 = tie((last, inner3, a1, b0))
    slot3 = jnp.where(inner, middle, last)
    lower3 = lax.ppermute(last[:tokens], "seq", [(i * 2 + b, i * 2 + 1 - b) for i in (0, 3) for b in range(2)])
    upper3 = hop(other2[tokens:], (1, 0), (2, 3))
    a2 = project(yc, slot2, [other2], w_out)
    rounded = jnp.concatenate([a1[1], a2[1]])
    lower3, upper3, rounded = tie((lower3, upper3, rounded))
    sums = cross(rounded).reshape(2, tokens, -1)
    b1, b2 = ((part[0] + v.astype(F32)).astype(BF16) for part, v in zip((a1, a2), sums))
    b3 = reduce_core(*project(yc, slot3, [inner3, lower3, upper3], w_out))
    b0, b1, b2, b3 = tie((b0, b1, b2, b3))
    last_sums = deliver(0, 3, b0, b3)
    early_sums = deliver(1, 2, b1, b2)
    here = (core == z % 2) == (grp // 2 == z // 2)
    mine, theirs = jnp.where(here, last_sums, early_sums), jnp.where(here, early_sums, last_sums)
    return place(core.astype(jnp.int32).reshape(1), mine.astype(BF16), cross(theirs.astype(BF16)))


def prefix(array, axis, combine, identity):
    length, mine = (lax.axis_size(axis), lax.axis_index(axis))
    everything = jax.tree.map(lambda part: lax.all_gather(part, axis), array)
    start = jax.tree.map(
        lambda part, zero: jnp.broadcast_to(jnp.asarray(zero, part.dtype), part.shape),
        array,
        identity,
    )

    def turn(k, before):
        reached = k < mine
        new = combine(before, jax.tree.map(lambda part: part[k], everything))
        return jax.tree.map(lambda a, b: jnp.where(reached, a, b), new, before)

    return lax.fori_loop(0, length, turn, start)


def ssd_blocks(xf, dt, la, bm, cm, braw, craw, init):
    length, heads, width = xf.shape
    groups = bm.shape[1]
    ratio = heads // groups
    block = math.gcd(length, 256)
    count = length // block

    def step(state, blk):
        xb, dtb, lab, bb, cb, bnar, cnar = blk
        cum = jnp.cumsum(lab, axis=0)
        attention_logits = jnp.einsum("tgn,sgn->gts", cnar, bnar, preferred_element_type=F32)
        attention_logits = jnp.repeat(attention_logits, ratio, axis=0)
        diff = cum.T[:, :, None] - cum.T[:, None, :]
        rows = lax.broadcasted_iota(jnp.int32, (block, block), 0)
        cols = lax.broadcasted_iota(jnp.int32, (block, block), 1)
        mask = (rows >= cols)[None, :, :]
        decay = jnp.exp(jnp.where(mask, diff, -1e30))
        mixing = decay * attention_logits * dtb.T[:, None, :]
        outs = jnp.einsum("hts,shp->thp", mixing, xb, precision=HIGH)
        cheads = jnp.repeat(cb, ratio, axis=1)
        bheads = jnp.repeat(bb, ratio, axis=1)
        outs = outs + jnp.exp(cum)[:, :, None] * jnp.einsum("thn,hpn->thp", cheads, state, precision=HIGH)
        weights = jnp.exp(cum[-1][None, :] - cum) * dtb
        fresh = jnp.einsum("sh,shp,shn->hpn", weights, xb, bheads, precision=HIGH)
        state = jnp.exp(cum[-1])[:, None, None] * state + fresh
        return (state, outs)

    cut = lambda v: v.reshape((count, block) + v.shape[1:])
    final, outs = lax.scan(step, init, jax.tree.map(cut, (xf, dt, la, bm, cm, braw, craw)))
    return (outs.reshape(length, heads, width), final, jnp.sum(la, axis=0))


def gated_norm_output(y, multiplier_channels, norm_gain, groups):
    length = y.shape[0]
    gated = y.reshape(length, -1) * jax.nn.silu(multiplier_channels.astype(F32))
    split = gated.reshape(length, groups, -1)
    split = split * lax.rsqrt(jnp.mean(split * split, axis=-1, keepdims=True) + EPS)
    return (split.reshape(length, -1) * norm_gain).astype(BF16)


def combine_states(earlier_state, later):
    return (earlier_state[0] * later[0], later[0][:, None, None] * earlier_state[1] + later[1])


def general_shards(x_in, gate, b_proj, c_proj, dt_raw, dt_bias, a_log, skip_d, norm_gain, w_out):
    length = x_in.shape[0]
    heads = dt_raw.shape[1]
    groups = b_proj.shape[1] // STATE
    xf = x_in.astype(F32).reshape(length, heads, CHANNEL_WIDTH)
    dt = jax.nn.softplus(dt_raw + dt_bias)
    la = -jnp.exp(a_log) * dt
    braw = b_proj.reshape(length, groups, STATE)
    craw = c_proj.reshape(length, groups, STATE)
    bm = braw.astype(F32)
    cm = craw.astype(F32)
    empty = jnp.zeros((heads, CHANNEL_WIDTH, STATE), F32)
    y, local_end, total = ssd_blocks(xf, dt, la, bm, cm, braw, craw, empty)
    identity = (jnp.ones((heads,), F32), empty)
    carried = prefix((jnp.exp(total), local_end), "seq", combine_states, identity)
    cum = jnp.cumsum(la, axis=0)
    cheads = jnp.repeat(cm, heads // groups, axis=1)
    y = y + jnp.exp(cum)[:, :, None] * jnp.einsum("thn,hpn->thp", cheads, carried[1], precision=HIGH)
    y = y + skip_d[None, :, None] * xf
    normed = gated_norm_output(y, gate, norm_gain, groups)
    partial_out = jnp.dot(
        normed, lax.all_gather(w_out, "seq", axis=1, tiled=True), preferred_element_type=F32
    )
    return lax.psum_scatter(partial_out, "grp", scatter_dimension=1, tiled=True).astype(BF16)


def solution(mesh):
    seq, grp = mesh.shape["seq"], mesh.shape["grp"]

    def shards(*args):
        groups = args[2].shape[1] // STATE
        if grp == 4 and seq == 2 * grp and groups == 2:
            return pair_shards(grp, *args)
        return general_shards(*args)

    return jax.shard_map(
        shards,
        mesh=mesh,
        in_specs=(
            P("seq", "grp"),
            P("seq", "grp"),
            P("seq", "grp"),
            P("seq", "grp"),
            P("seq", "grp"),
            P("grp"),
            P("grp"),
            P("grp"),
            P("grp"),
            P("grp", "seq"),
        ),
        out_specs=P("seq", "grp"),
        check_vma=False,
    )
```

```python
import math

import jax
import jax.numpy as jnp
from jax import lax
from jax.experimental import pallas as pl
from jax.experimental.pallas import tpu as pltpu
from jax.sharding import PartitionSpec as P

CHANNEL_WIDTH = 128
STATE = 128
EPS = 1e-05

HIGH = lax.Precision.HIGHEST
F32 = jnp.float32
BF16 = jnp.bfloat16
NT = (((1,), (1,)), ((), ()))
TN = (((0,), (0,)), ((), ()))
VMEM_LIMIT = 24 * 2**20


def params(grid_dims=0, limit=VMEM_LIMIT):
    return pltpu.CompilerParams(
        vmem_limit_bytes=limit,
        dimension_semantics=("arbitrary",) * grid_dims if grid_dims else None,
    )


def cost(flops, moved):
    return pl.CostEstimate(flops=int(flops), bytes_accessed=int(moved), transcendentals=0)


def iota(shape, axis):
    return lax.broadcasted_iota(jnp.int32, shape, axis)


def spread(values, width):
    heads = values.shape[1]
    return jnp.concatenate(
        [jnp.broadcast_to(values[:, h : h + 1], (values.shape[0], width)) for h in range(heads)], axis=1
    )


def split3(value):
    hi = value.astype(BF16)
    rest = value - hi.astype(F32)
    mid = rest.astype(BF16)
    return hi, mid, (rest - mid.astype(F32)).astype(BF16)


def pack_kernel(group_ref, x_ref, b_ref, c_ref, dt_ref, out_ref, *, heads):
    width, state = x_ref.shape[1], b_ref.shape[1]
    out_ref[:, :width] = x_ref[...]
    out_ref[:, width : width + state] = b_ref[...]
    out_ref[:, width + state : width + 2 * state] = c_ref[...]
    group = group_ref[0]
    rows, cols = iota((2 * heads, 128), 0), iota((2 * heads, 128), 1)
    total = jnp.zeros((x_ref.shape[0], 128), F32)
    for part, value in enumerate(split3(dt_ref[...])):
        where = (cols == rows - group * heads + part * heads) & (rows // heads == group)
        total = total + lax.dot_general(value, where.astype(BF16), TN, preferred_element_type=F32)
    out_ref[:, width + 2 * state :] = total.astype(BF16)


def pack(group, x, b, c, dt, heads, limit):
    tokens, width, state = x.shape[0], heads * CHANNEL_WIDTH, STATE
    out = jax.ShapeDtypeStruct((tokens, width + 2 * state + 128), BF16)
    return pl.pallas_call(
        lambda *refs: pack_kernel(*refs, heads=heads),
        grid_spec=pltpu.PrefetchScalarGridSpec(
            num_scalar_prefetch=1,
            grid=(1,),
            in_specs=[
                pl.BlockSpec((tokens, width), lambda i, g: (0, g[0])),
                pl.BlockSpec((tokens, state), lambda i, g: (0, g[0])),
                pl.BlockSpec((tokens, state), lambda i, g: (0, g[0])),
                pl.BlockSpec(dt.shape, lambda i, g: (0, 0)),
            ],
            out_specs=pl.BlockSpec(out.shape, lambda i, g: (0, 0)),
        ),
        out_shape=out,
        compiler_params=params(1, limit),
        cost_estimate=cost(1e6, 1e6),
        name="pack",
    )(group, x, b, c, dt)


def local_state_kernel(
    y_ref, own_ref, pk_ref, bias_ref, alog_ref, xs_ref, bs_ref, cs_ref, scal_ref, send_ref, s_ref, *, heads,
):
    tokens = own_ref.shape[0]
    width, state = xs_ref.shape[1], bs_ref.shape[1]
    y = y_ref[0]
    rows, cols = iota((128, heads), 0), iota((128, heads), 1)
    take = ((rows % heads == cols) & (rows < 3 * heads)).astype(BF16)
    steps = []
    for ref, place in ((own_ref, y), (pk_ref, 1 - y)):
        at = pl.ds(pl.multiple_of(place * tokens, tokens), tokens)
        xs_ref[at, :] = ref[:, :width]
        bs_ref[at, :] = ref[:, width : width + state]
        cs_ref[at, :] = ref[:, width + state : width + 2 * state]
        steps.append(jnp.dot(ref[:, width + 2 * state :], take, preferred_element_type=F32))
    own, other = steps
    raw = jnp.concatenate([jnp.where(y == 0, own, other), jnp.where(y == 0, other, own)], axis=0)
    raw = raw + bias_ref[...]
    dt = jnp.maximum(raw, 0.0) + jnp.log1p(jnp.exp(-jnp.abs(raw)))
    la = -jnp.exp(alog_ref[...]) * dt
    length = 2 * tokens
    lower = (iota((length, length), 0) >= iota((length, length), 1)).astype(F32)
    cum = jnp.dot(lower, la, precision=HIGH)
    last = cum[length - 1 : length, :]
    scal_ref[:, :heads] = cum
    scal_ref[:, heads : 2 * heads] = dt
    weights = jnp.exp(last - cum) * dt
    scaled = (xs_ref[...].astype(F32) * spread(weights, CHANNEL_WIDTH)).astype(BF16)
    s = lax.dot_general(bs_ref[...], scaled, TN, preferred_element_type=F32)
    s_ref[:state, :] = s
    send_ref[:state, :] = s.astype(BF16)
    decay = spread(jnp.exp(last), CHANNEL_WIDTH)
    s_ref[state:, :] = jnp.broadcast_to(decay, (8, width))
    hi, mid, lo = split3(decay)
    which = iota((16, width), 0)
    parts = jnp.where(which == 0, hi.astype(F32), jnp.where(which == 1, mid.astype(F32), lo.astype(F32)))
    send_ref[state:, :] = jnp.where(which < 3, parts, 0.0).astype(BF16)


def local_state(y, own, pk, bias, alog, heads):
    tokens, width, state = own.shape[0], heads * CHANNEL_WIDTH, STATE
    whole = lambda a: pl.BlockSpec(a.shape, lambda i, y: (0,) * a.ndim)
    outs = [
        jax.ShapeDtypeStruct((2 * tokens, width), BF16),
        jax.ShapeDtypeStruct((2 * tokens, state), BF16),
        jax.ShapeDtypeStruct((2 * tokens, state), BF16),
        jax.ShapeDtypeStruct((2 * tokens, 2 * heads), F32),
        jax.ShapeDtypeStruct((state + 16, width), BF16),
        jax.ShapeDtypeStruct((state + 8, width), F32),
    ]
    return pl.pallas_call(
        lambda *refs: local_state_kernel(*refs, heads=heads),
        grid_spec=pltpu.PrefetchScalarGridSpec(
            num_scalar_prefetch=1,
            grid=(1,),
            in_specs=[whole(own), whole(pk), whole(bias), whole(alog)],
            out_specs=[whole(o) for o in outs],
        ),
        out_shape=outs,
        compiler_params=params(1),
        cost_estimate=cost(2e8, 3e6),
        name="local_state",
    )(y, own, pk, bias, alog)


def local_y_kernel(xs_ref, bs_ref, cs_ref, scal_ref, skip_ref, out_ref, *, heads, tokens):
    cum, dt = scal_ref[:, :heads], scal_ref[:, heads : 2 * heads]
    length = 2 * tokens
    eye = (iota((length, length), 0) == iota((length, length), 1)).astype(F32)
    flat = lax.dot_general(scal_ref[...], eye, TN, precision=HIGH)
    cum_row, dt_row = flat[:heads, :], flat[heads : 2 * heads, :]
    mask = iota((tokens, tokens), 0) >= iota((tokens, tokens), 1)
    logits = []
    for k in range(2):
        at = pl.ds(k * tokens, tokens)
        logits.append(lax.dot_general(cs_ref[at, :], bs_ref[at, :], NT, preferred_element_type=F32))
    middle = cum[tokens - 1 : tokens, :]
    weights = jnp.exp(middle - cum[:tokens, :]) * dt[:tokens, :]
    scaled = (xs_ref[:tokens, :].astype(F32) * spread(weights, CHANNEL_WIDTH)).astype(BF16)
    s = lax.dot_general(bs_ref[:tokens, :], scaled, TN, preferred_element_type=F32).astype(BF16)
    carried = jnp.dot(cs_ref[tokens:, :], s, preferred_element_type=F32)
    carried = carried * spread(jnp.exp(cum[tokens:, :] - middle), CHANNEL_WIDTH)
    for k in range(2):
        lo = k * tokens
        for h in range(heads):
            at = h * CHANNEL_WIDTH
            xh = xs_ref[lo : lo + tokens, at : at + CHANNEL_WIDTH]
            diff = cum[lo : lo + tokens, h : h + 1] - cum_row[h : h + 1, lo : lo + tokens]
            mix = jnp.exp(jnp.where(mask, diff, -1e30)) * logits[k] * dt_row[h : h + 1, lo : lo + tokens]
            top = mix.astype(BF16)
            yh = jnp.dot(top, xh, preferred_element_type=F32)
            yh = yh + jnp.dot((mix - top.astype(F32)).astype(BF16), xh, preferred_element_type=F32)
            yh = yh + skip_ref[:, at : at + CHANNEL_WIDTH] * xh.astype(F32)
            if k == 1:
                yh = yh + carried[:, at : at + CHANNEL_WIDTH]
            out_ref[lo : lo + tokens, at : at + CHANNEL_WIDTH] = yh


def local_y(xs, bs, cs, scal, skip, heads):
    length, width = xs.shape
    return pl.pallas_call(
        lambda *refs: local_y_kernel(*refs, heads=heads, tokens=length // 2),
        out_shape=jax.ShapeDtypeStruct((length, width), F32),
        compiler_params=params(),
        cost_estimate=cost(4e8, 4e6),
        name="local_y",
    )(xs, bs, cs, scal, skip)


def join_kernel(send_ref, s_ref, got_ref, out_ref):
    state = out_ref.shape[0]
    out_ref[...] = (s_ref[:state, :] + s_ref[state : state + 1, :] * got_ref[:state, :].astype(F32)).astype(BF16)


def join(send, s, got):
    return pl.pallas_call(
        join_kernel,
        out_shape=jax.ShapeDtypeStruct((STATE, s.shape[1]), BF16),
        compiler_params=params(),
        cost_estimate=cost(1e6, 1.5e6),
        name="join",
    )(send, s, got)


def finish_kernel(y_ref, local_ref, cs_ref, scal_ref, one_ref, two_ref, gate_ref, got_ref, gain_ref, out_ref, *, heads):
    length, width = local_ref.shape
    state, tokens = two_ref.shape[0], length // 2
    y = y_ref[0]
    decay = jnp.sum(one_ref[state:, :].astype(F32), axis=0, keepdims=True)
    start = one_ref[:state, :].astype(F32) + decay * two_ref[...].astype(F32)
    top = start.astype(BF16)
    low = (start - top.astype(F32)).astype(BF16)
    grow = jnp.exp(scal_ref[:, :heads])
    for k in range(2):
        at = pl.ds(k * tokens, tokens)
        carried = jnp.dot(cs_ref[at, :], top, preferred_element_type=F32)
        carried = carried + jnp.dot(cs_ref[at, :], low, preferred_element_type=F32)
        value = local_ref[at, :] + carried * spread(grow[k * tokens : (k + 1) * tokens, :], CHANNEL_WIDTH)
        gate = jnp.where(y == k, gate_ref[...], got_ref[...]).astype(F32)
        value = value * (gate / (1.0 + jnp.exp(-gate)))
        mean = jnp.sum(value * value, axis=1, keepdims=True) / width
        out_ref[at, :] = (value * lax.rsqrt(mean + EPS) * gain_ref[...]).astype(BF16)


def finish(y, local, cs, scal, one, two, gate, got, gain, heads):
    length, width = local.shape
    whole = lambda a: pl.BlockSpec(a.shape, lambda i, y: (0,) * a.ndim)
    return pl.pallas_call(
        lambda *refs: finish_kernel(*refs, heads=heads),
        grid_spec=pltpu.PrefetchScalarGridSpec(
            num_scalar_prefetch=1,
            grid=(1,),
            in_specs=[
                whole(local),
                whole(cs),
                whole(scal),
                whole(one),
                whole(two),
                pl.BlockSpec((length // 2, width), lambda i, y: (0, y[0])),
                whole(got),
                whole(gain),
            ],
            out_specs=pl.BlockSpec((length, width), lambda i, y: (0, 0)),
        ),
        out_shape=jax.ShapeDtypeStruct((length, width), BF16),
        compiler_params=params(1),
        cost_estimate=cost(1e8, 4e6),
        name="finish",
    )(y, local, cs, scal, one, two, gate, got, gain)


def project_kernel(yc_ref, own_ref, *refs):
    *got_refs, first_ref, second_ref, keep_ref, send_ref, both_ref = refs
    tokens, depth = keep_ref.shape[0], own_ref.shape[1]
    core = yc_ref[1]

    @pl.when(pl.program_id(0) == 0)
    def _():
        def fill(lower, upper):
            for k in range(2):
                rows = pl.ds(pl.multiple_of(jnp.where(core == 0, k, 1 - k) * tokens, tokens), tokens)
                both_ref[rows, :depth] = own_ref[k * tokens : (k + 1) * tokens, :]
                both_ref[rows, depth:] = (lower, upper)[k]()

        whole = got_refs[0]
        extra = got_refs[2].shape[0] - tokens if len(got_refs) > 1 else 0
        pieces = lambda: jnp.concatenate([got_refs[1][...], got_refs[2][:extra, :]])
        halves = lambda: fill(lambda: whole[:tokens, :], lambda: whole[tokens:, :])
        if len(got_refs) == 1:
            halves()
        else:
            pl.when(yc_ref[2] == 1)(halves)
            pl.when(yc_ref[2] == 0)(lambda: fill(pieces, lambda: got_refs[2][extra:, :]))

    part = jnp.dot(both_ref[:, :depth], first_ref[...], preferred_element_type=F32)
    part = part + jnp.dot(both_ref[:, depth:], second_ref[...], preferred_element_type=F32)
    keep_ref[...] = part[:tokens, :]
    send_ref[...] = part[tokens:, :].astype(BF16)


def project(yc, own, got, w):
    length, depth = own.shape
    tokens, cols = length // 2, w.shape[1]
    tile = min(cols, 256)
    whole = lambda a: pl.BlockSpec(a.shape, lambda i, yc: (0, 0))
    return pl.pallas_call(
        project_kernel,
        grid_spec=pltpu.PrefetchScalarGridSpec(
            num_scalar_prefetch=1,
            grid=(cols // tile,),
            in_specs=[whole(own)]
            + [whole(v) for v in got]
            + [
                pl.BlockSpec((depth, tile), lambda i, yc: (yc[0], i)),
                pl.BlockSpec((depth, tile), lambda i, yc: (1 - yc[0], i)),
            ],
            out_specs=[
                pl.BlockSpec((tokens, tile), lambda i, yc: (0, i)),
                pl.BlockSpec((tokens, tile), lambda i, yc: (0, i)),
            ],
            scratch_shapes=[pltpu.VMEM((length, 2 * depth), BF16)],
        ),
        out_shape=[jax.ShapeDtypeStruct((tokens, cols), F32), jax.ShapeDtypeStruct((tokens, cols), BF16)],
        compiler_params=params(1),
        cost_estimate=cost(4.0 * length * depth * cols, 6e6),
        name="project",
    )(yc, own, *got, w, w)


def place_kernel(at_ref, mine_ref, got_ref, out_ref):
    cols = got_ref.shape[1]
    part = at_ref[0]
    out_ref[:, pl.ds(pl.multiple_of(part * cols, cols), cols)] = mine_ref[...]
    out_ref[:, pl.ds(pl.multiple_of((1 - part) * cols, cols), cols)] = got_ref[...]


def place(at, mine, got):
    tokens, cols = got.shape
    whole = pl.BlockSpec((tokens, cols), lambda i, at: (0, 0))
    return pl.pallas_call(
        place_kernel,
        grid_spec=pltpu.PrefetchScalarGridSpec(
            num_scalar_prefetch=1,
            grid=(1,),
            in_specs=[whole, whole],
            out_specs=pl.BlockSpec((tokens, 2 * cols), lambda i, at: (0, 0)),
        ),
        out_shape=jax.ShapeDtypeStruct((tokens, 2 * cols), BF16),
        compiler_params=params(1),
        cost_estimate=cost(1e6, 2e6),
        name="place",
    )(at, mine, got)


def pair_shards(nz, x_in, gate, b_proj, c_proj, dt_raw, dt_bias, a_log, skip_d, norm_gain, w_out):
    tokens = x_in.shape[0]
    heads = dt_raw.shape[1] // 2
    width = heads * CHANNEL_WIDTH
    seq, grp = lax.axis_index("seq"), lax.axis_index("grp")
    z, y = seq // 2, seq % 2
    yv = y.astype(jnp.int32).reshape(1)
    dt_raw = dt_raw.T
    both = ("seq", "grp")
    core = grp % 2
    spots = [(a, b, c, d) for a in range(nz) for b in range(2) for c in range(nz // 2) for d in range(2)]
    flat = lambda a, b, c, d: ((a * 2 + b) * (nz // 2) + c) * 2 + d
    tie = lax.optimization_barrier

    def half(v, axis, which):
        n = v.shape[axis] // 2
        return lax.dynamic_slice_in_dim(v, which * n, n, axis)

    flip = [(s, s ^ 1) for s in range(2 * nz)]
    sibling = [(g, g ^ 1) for g in range(nz)]
    def along(v, step, senders):
        pairs = [(a * 2 + b, (a + step) * 2 + b) for a in senders for b in range(2)]
        return lax.ppermute(v, "seq", pairs)

    got = lax.ppermute(pack(1 - yv, x_in, b_proj, c_proj, dt_raw, heads, 60 * 2**20), "seq", flip)
    own = pack(yv, x_in, b_proj, c_proj, dt_raw, heads, VMEM_LIMIT)
    gate_half = half(gate, 1, 1 - y)
    bias, alog = half(dt_bias, 0, y)[None, :], half(a_log, 0, y)[None, :]
    skip = jnp.repeat(half(skip_d, 0, y), CHANNEL_WIDTH)[None, :]
    gain = half(norm_gain, 0, y)[None, :]
    got_gate = lax.ppermute(gate_half, "seq", flip)
    got, own, bias, alog, skip, gain = tie((got, own, bias, alog, skip, gain))

    xs, bs, cs, scal, send, s = local_state(yv, own, got, bias, alog, heads)
    one = along(send, 1, range(nz - 1))
    base = local_y(xs, bs, cs, scal, skip, heads)
    one, base = tie((one, base))

    two = along(join(send, s, one), 2, range(nz - 2))
    block = finish(yv, base, cs, scal, one, two, gate, got_gate, gain, heads)

    hop = lambda value, *moves: lax.ppermute(value, "seq", [(i * 2 + b, j * 2 + b) for i, j in moves for b in range(2)])
    inner = (z == 1) | (z == 2)
    yc = jnp.stack([y, core, inner]).astype(jnp.int32)
    across = lambda value: lax.ppermute(value, "seq", flip)
    cross = lambda value: lax.ppermute(value, "grp", sibling)

    def reduce_core(full, rounded):
        return (full + cross(rounded).astype(F32)).astype(BF16)

    def deliver(slot, far, near, distant):
        near_x, total = grp // 2 == z // 2, 0.0
        for turn in range(2):
            pairs = []
            for a, b, c, d in spots:
                at = slot if c ^ turn == a // 2 else far
                pairs.append((flat(a, b, c, d), flat(a ^ at, d, a // 2, b)))
            value = jnp.where(near_x, near, distant) if turn == 0 else jnp.where(near_x, distant, near)
            moved = lax.ppermute(value, both, [(i, j) for i, j in pairs if i != j])
            if any(i == j for i, j in pairs):
                moved = jnp.where(near_x & (y == core), near, moved)
            total = total + moved.astype(F32)
        return total

    slot1 = hop(block, (0, 1), (1, 0), (2, 3), (3, 2))
    middle = hop(block, (1, 2), (2, 1))
    other0 = across(block)
    inward, outward = hop(slot1, (1, 2), (2, 1)), hop(middle, (1, 0), (2, 3))
    other1 = across(slot1)
    a0 = project(yc, block, [other0], w_out)
    inward, a0 = tie((inward, a0))
    last = hop(inward, (1, 0), (2, 3))
    slot2 = jnp.where(inner, inward, outward)
    other2 = across(slot2)
    a1 = project(yc, slot1, [other1], w_out)
    b0 = reduce_core(*a0)
    inner3 = hop(other0, (1, 2), (2, 1))
    last, inner3, a1, b0 = tie((last, inner3, a1, b0))
    slot3 = jnp.where(inner, middle, last)
    cut = tokens - 16
    lower3 = lax.ppermute(last[:cut], "seq", [(i * 2 + b, i * 2 + 1 - b) for i in (0, 3) for b in range(2)])
    upper3 = hop(other2[cut:], (1, 0), (2, 3))
    a2 = project(yc, slot2, [other2], w_out)
    rounded = jnp.concatenate([a1[1], a2[1]])
    lower3, upper3, rounded = tie((lower3, upper3, rounded))
    sums = cross(rounded).reshape(2, tokens, -1)
    b1, b2 = ((part[0] + v.astype(F32)).astype(BF16) for part, v in zip((a1, a2), sums))
    b3 = reduce_core(*project(yc, slot3, [inner3, lower3, upper3], w_out))
    b0, b1, b2, b3 = tie((b0, b1, b2, b3))
    last_sums = deliver(0, 3, b0, b3)
    early_sums = deliver(1, 2, b1, b2)
    here = (core == z % 2) == (grp // 2 == z // 2)
    mine, theirs = jnp.where(here, last_sums, early_sums), jnp.where(here, early_sums, last_sums)
    return place(core.astype(jnp.int32).reshape(1), mine.astype(BF16), cross(theirs.astype(BF16)))


def prefix(array, axis, combine, identity):
    length, mine = (lax.axis_size(axis), lax.axis_index(axis))
    everything = jax.tree.map(lambda part: lax.all_gather(part, axis), array)
    start = jax.tree.map(
        lambda part, zero: jnp.broadcast_to(jnp.asarray(zero, part.dtype), part.shape),
        array,
        identity,
    )

    def turn(k, before):
        reached = k < mine
        new = combine(before, jax.tree.map(lambda part: part[k], everything))
        return jax.tree.map(lambda a, b: jnp.where(reached, a, b), new, before)

    return lax.fori_loop(0, length, turn, start)


def ssd_blocks(xf, dt, la, bm, cm, braw, craw, init):
    length, heads, width = xf.shape
    groups = bm.shape[1]
    ratio = heads // groups
    block = math.gcd(length, 256)
    count = length // block

    def step(state, blk):
        xb, dtb, lab, bb, cb, bnar, cnar = blk
        cum = jnp.cumsum(lab, axis=0)
        attention_logits = jnp.einsum("tgn,sgn->gts", cnar, bnar, preferred_element_type=F32)
        attention_logits = jnp.repeat(attention_logits, ratio, axis=0)
        diff = cum.T[:, :, None] - cum.T[:, None, :]
        rows = lax.broadcasted_iota(jnp.int32, (block, block), 0)
        cols = lax.broadcasted_iota(jnp.int32, (block, block), 1)
        mask = (rows >= cols)[None, :, :]
        decay = jnp.exp(jnp.where(mask, diff, -1e30))
        mixing = decay * attention_logits * dtb.T[:, None, :]
        outs = jnp.einsum("hts,shp->thp", mixing, xb, precision=HIGH)
        cheads = jnp.repeat(cb, ratio, axis=1)
        bheads = jnp.repeat(bb, ratio, axis=1)
        outs = outs + jnp.exp(cum)[:, :, None] * jnp.einsum("thn,hpn->thp", cheads, state, precision=HIGH)
        weights = jnp.exp(cum[-1][None, :] - cum) * dtb
        fresh = jnp.einsum("sh,shp,shn->hpn", weights, xb, bheads, precision=HIGH)
        state = jnp.exp(cum[-1])[:, None, None] * state + fresh
        return (state, outs)

    cut = lambda v: v.reshape((count, block) + v.shape[1:])
    final, outs = lax.scan(step, init, jax.tree.map(cut, (xf, dt, la, bm, cm, braw, craw)))
    return (outs.reshape(length, heads, width), final, jnp.sum(la, axis=0))


def gated_norm_output(y, multiplier_channels, norm_gain, groups):
    length = y.shape[0]
    gated = y.reshape(length, -1) * jax.nn.silu(multiplier_channels.astype(F32))
    split = gated.reshape(length, groups, -1)
    split = split * lax.rsqrt(jnp.mean(split * split, axis=-1, keepdims=True) + EPS)
    return (split.reshape(length, -1) * norm_gain).astype(BF16)


def combine_states(earlier_state, later):
    return (earlier_state[0] * later[0], later[0][:, None, None] * earlier_state[1] + later[1])


def general_shards(x_in, gate, b_proj, c_proj, dt_raw, dt_bias, a_log, skip_d, norm_gain, w_out):
    length = x_in.shape[0]
    heads = dt_raw.shape[1]
    groups = b_proj.shape[1] // STATE
    xf = x_in.astype(F32).reshape(length, heads, CHANNEL_WIDTH)
    dt = jax.nn.softplus(dt_raw + dt_bias)
    la = -jnp.exp(a_log) * dt
    braw = b_proj.reshape(length, groups, STATE)
    craw = c_proj.reshape(length, groups, STATE)
    bm = braw.astype(F32)
    cm = craw.astype(F32)
    empty = jnp.zeros((heads, CHANNEL_WIDTH, STATE), F32)
    y, local_end, total = ssd_blocks(xf, dt, la, bm, cm, braw, craw, empty)
    identity = (jnp.ones((heads,), F32), empty)
    carried = prefix((jnp.exp(total), local_end), "seq", combine_states, identity)
    cum = jnp.cumsum(la, axis=0)
    cheads = jnp.repeat(cm, heads // groups, axis=1)
    y = y + jnp.exp(cum)[:, :, None] * jnp.einsum("thn,hpn->thp", cheads, carried[1], precision=HIGH)
    y = y + skip_d[None, :, None] * xf
    normed = gated_norm_output(y, gate, norm_gain, groups)
    partial_out = jnp.dot(
        normed, lax.all_gather(w_out, "seq", axis=1, tiled=True), preferred_element_type=F32
    )
    return lax.psum_scatter(partial_out, "grp", scatter_dimension=1, tiled=True).astype(BF16)


def solution(mesh):
    seq, grp = mesh.shape["seq"], mesh.shape["grp"]

    def shards(*args):
        groups = args[2].shape[1] // STATE
        if grp == 4 and seq == 2 * grp and groups == 2:
            return pair_shards(grp, *args)
        return general_shards(*args)

    return jax.shard_map(
        shards,
        mesh=mesh,
        in_specs=(
            P("seq", "grp"),
            P("seq", "grp"),
            P("seq", "grp"),
            P("seq", "grp"),
            P("seq", "grp"),
            P("grp"),
            P("grp"),
            P("grp"),
            P("grp"),
            P("grp", "seq"),
        ),
        out_specs=P("seq", "grp"),
        check_vma=False,
    )
```
